32 devices in a mesh: seq: 8 (over z, x), dp: 4 (over y, core).
Axes of the slice: x: 2, y: 2, z: 4, core: 2. Of those that a mesh axis runs over, the one named last changes fastest.
Arguments:
- layer_input: bfloat16 [16384, 576], P(('seq', 'dp')), may hold values from -6 to 6
- w_qkv: bfloat16 [552960], P(('seq', 'dp')), may hold values from -0.25 to 0.25
- w_out: bfloat16 [331776], P(('seq', 'dp')), may hold values from -4 to 4
- w_gu: bfloat16 [1769472], P(('seq', 'dp')), may hold values from -0.25 to 0.25
- w_down: bfloat16 [884736], P(('seq', 'dp')), may hold values from -0.15625 to 0.15625
- norm_gains: float32 [2, 576], replicated, may hold values from 0.1 to 1.9
- lengths: int32 [4, 6], P('dp'), may hold values from 1 to 2048, 4096 in all within a row
- cotangent: bfloat16 [16384, 576], P(('seq', 'dp')), may hold values from -6 to 6
Outputs:
- layer_output: bfloat16 [16384, 576], P(('seq', 'dp'))
- input_grad: float32 [16384, 576], P(('seq', 'dp'))
- g_qkv: float32 [552960], P(('seq', 'dp'))
- g_out: float32 [331776], P(('seq', 'dp'))
- g_gu: float32 [1769472], P(('seq', 'dp'))
- g_down: float32 [884736], P(('seq', 'dp'))
- gains_grad: float32 [2, 576], replicated
The draws below stay inside these ranges and needn't reach their ends.
Inputs may be any that keep to these rules, and one draw needn't show every extreme that they name: Each row lists the lengths of the 6 sequences of one dp group in order; a row sums to 4096, and its largest entry is exactly 2048.
All inputs are finite; a program needn't handle non-finite values.
Results may differ from the reference program's by a relative error of at most 0.012.
Values may be sent and summed in bfloat16 or wider, within the bound.
A program may use at most 128 MiB of HBM per device.

```python
import math
import jax
import jax.numpy as jnp
import numpy as np
from jax import lax

D = 576
QUERY_HEADS = 9
KEY_VALUE_HEADS = 3
HEAD_SIZE = 64
FF = 1536
TOK_DEV = 512
NDOCS = 6
GROUP = 4096
MAXLEN = 2048
QKV = 960
TOKENS = 16384
N_SEQ = 8
N_DP = 4


def block_scale(rng, dims, shards, least, top_value):
    def one(position, shards_of):
        steps = jax.random.uniform(jax.random.fold_in(jax.random.fold_in(rng, 6), position), (shards_of,), jnp.float32, least / len(shards), top_value / len(shards))
        return jnp.repeat(jnp.exp(steps), dims[position] // shards_of).reshape((-1,) + (1,) * (len(dims) - position - 1))

    factor_of = one(*shards[0])
    for cut in shards[1:]:
        factor_of = factor_of * one(*cut)
    return factor_of


def profile(number_of, total, limit, skew):
    weights = [(1 << 20) // math.isqrt(grade ** skew) + 1 for grade in range(2, number_of + 1)]
    spare, holding = total - limit - (number_of - 1), [1] * (number_of - 1)
    while spare > 0:
        free = [i for i in range(number_of - 1) if holding[i] < limit]
        mass, left = sum([weights[i] for i in free]), spare
        for i in free:
            addition = min(limit - holding[i], max(1, left * weights[i] // mass), spare)
            holding[i] = holding[i] + addition
            spare = spare - addition
    return np.array([limit] + holding)


def ragged(own_key, amount, total, reach, lean):
    if amount == 2:
        one = jax.random.randint(own_key, (), max(1, total - reach), min(reach, total - 1) + 1)
        return jnp.stack([one, total - one])
    tallies = jnp.asarray(profile(amount, total, reach, lean), jnp.int32)
    pairs = (amount - 1) // 2
    donor, sink = tallies[1:1 + 2 * pairs:2], tallies[2:2 + 2 * pairs:2]
    slack = jnp.minimum(donor - 1, reach - sink)
    passed = jax.random.randint(jax.random.fold_in(own_key, 1), (pairs,), 0, 1 << 20) % (slack + 1)
    tallies = tallies.at[1:1 + 2 * pairs:2].set(donor - passed).at[2:2 + 2 * pairs:2].set(sink + passed)
    return tallies[jax.random.permutation(jax.random.fold_in(own_key, 2), amount)]


def normal_values(own_key, shape, scale, reach, shards=(), held_as=jnp.bfloat16):
    values = scale * jax.random.normal(own_key, shape, jnp.float32)
    if shards:
        values = values * block_scale(own_key, shape, shards, -0.22, 0.18)
    return jnp.clip(values, -reach, reach).astype(held_as)


def setup_inputs(seed: int = 0) -> dict:
    splits = jax.random.split(jax.random.key(seed), 9)
    layer_input = normal_values(splits[0], (TOKENS, D), 1.0, 6.0, ((0, 32),))
    w_qkv = normal_values(splits[1], (D * QKV,), D ** -0.5, 0.25, ((0, 32),))
    w_out = normal_values(splits[2], (QUERY_HEADS * HEAD_SIZE * D,), 2 ** -0.5, 4.0, ((0, 32),))
    w_gu = normal_values(splits[3], (2 * D * FF,), D ** -0.5, 0.25, ((0, 32),))
    w_down = normal_values(splits[4], (FF * D,), FF ** -0.5, 0.15625, ((0, 32),))
    norm_gains = jnp.clip(1.0 + 0.18 * jax.random.normal(splits[5], (2, D), jnp.float32), 0.1, 1.9)
    lengths = jax.vmap(lambda own: ragged(own, NDOCS, GROUP, MAXLEN, 2))(jax.random.split(splits[6], N_DP)).reshape((N_DP, NDOCS)).astype(jnp.int32)
    cotangent = normal_values(splits[7], (TOKENS, D), 1.0, 6.0, ((0, 32),))
    return {"layer_input": layer_input, "w_qkv": w_qkv, "w_out": w_out, "w_gu": w_gu, "w_down": w_down, "norm_gains": norm_gains, "lengths": lengths, "cotangent": cotangent}


@jax.custom_vjp
def lower_precision(v):
    return lax.optimization_barrier(v.astype(jnp.bfloat16)).astype(jnp.float32)

@jax.custom_vjp
def lower_precision_back(v):
    return v

def low_keep(v):
    return (lower_precision(v), None)

def low_pass(kept, grad):
    return (grad,)

def back_keep(v):
    return (v, None)

def back_low(kept, grad):
    return (lower_precision(grad),)
lower_precision.defvjp(low_keep, low_pass)
lower_precision_back.defvjp(back_keep, back_low)
EPS = 1e-05
THETA = 100000.0
MASKED = -1e+30
HIGH = lax.Precision.HIGHEST

def rms_norm(value_rows, gain):
    return value_rows * lax.rsqrt(lax.optimization_barrier(jnp.mean(value_rows * value_rows, axis=-1, keepdims=True)) + EPS) * gain

def apply_rotary(value_rows, token_position):
    half = value_rows.shape[-1] // 2
    freq = jnp.exp(jnp.arange(half, dtype=jnp.float32) * (-2.0 * math.log(THETA) / value_rows.shape[-1]))
    angle = token_position.astype(jnp.float32)[:, None] * freq[None, :]
    cosine = jnp.cos(angle)[:, None, :]
    sine = jnp.sin(angle)[:, None, :]
    first = value_rows[..., :half]
    second = value_rows[..., half:]
    return jnp.concatenate([first * cosine - second * sine, second * cosine + first * sine], axis=-1)

def layout(lengths_row, index):
    ends = jnp.cumsum(lengths_row, dtype=jnp.int32)
    done = ends[None, :] <= index[:, None]
    segment_index = lax.optimization_barrier(jnp.sum(done.astype(jnp.int32), axis=1, dtype=jnp.int32))
    token_position = index - lax.optimization_barrier(jnp.sum(jnp.where(done, lengths_row[None, :], 0), axis=1, dtype=jnp.int32))
    return (segment_index, token_position)

def group_attention(query_rows, key_rows, value_rows, segment_index):
    count_total = query_rows.shape[0]
    row_count = min(512, count_total)
    scale = 1.0 / math.sqrt(HEAD_SIZE)
    index = jnp.arange(count_total, dtype=jnp.int32)
    grouped_heads = query_rows.reshape(count_total // row_count, row_count, KEY_VALUE_HEADS, QUERY_HEADS // KEY_VALUE_HEADS, HEAD_SIZE)

    def one_block(args):
        block_query, block_segment, block_index = args
        scores = lower_precision_back(jnp.einsum('tkgd,skd->kgts', block_query, key_rows, precision=HIGH) * scale)
        allowed = (block_segment[:, None] == segment_index[None, :]) & (block_index[:, None] >= index[None, :])
        scores = jnp.where(allowed[None, None], scores, MASKED)
        weights = lower_precision(jax.nn.softmax(scores, axis=-1))
        return jnp.einsum('kgts,skd->tkgd', weights, value_rows, precision=HIGH)
    result = lax.map(jax.checkpoint(one_block), (grouped_heads, segment_index.reshape(-1, row_count), index.reshape(-1, row_count)))
    return result.reshape(count_total, QUERY_HEADS * HEAD_SIZE)

def forward(inputs, mixing_in, mixing_out, expand_matrix, shrink_matrix, gains, segment_index, token_position):
    token_count = inputs.shape[0]
    query_width = QUERY_HEADS * HEAD_SIZE
    key_width = KEY_VALUE_HEADS * HEAD_SIZE
    normed = lower_precision(rms_norm(inputs, gains[0]))
    projected_output = jnp.dot(normed, mixing_in, precision=HIGH)
    query_rows = lower_precision(apply_rotary(lower_precision_back(projected_output[:, :query_width]).reshape(token_count, QUERY_HEADS, HEAD_SIZE), token_position))
    key_rows = lower_precision(apply_rotary(lower_precision_back(projected_output[:, query_width:query_width + key_width]).reshape(token_count, KEY_VALUE_HEADS, HEAD_SIZE), token_position))
    value_rows = lower_precision(lower_precision_back(projected_output[:, query_width + key_width:])).reshape(token_count, KEY_VALUE_HEADS, HEAD_SIZE)

    def query_per_group(args):
        return group_attention(args[0], args[1], args[2], args[3])
    attended_rows = lax.map(query_per_group, (query_rows.reshape(N_DP, -1, QUERY_HEADS, HEAD_SIZE), key_rows.reshape(N_DP, -1, KEY_VALUE_HEADS, HEAD_SIZE), value_rows.reshape(N_DP, -1, KEY_VALUE_HEADS, HEAD_SIZE), segment_index))
    attended_rows = lower_precision(lower_precision_back(attended_rows.reshape(token_count, query_width)))
    mid = inputs + lower_precision_back(jnp.dot(attended_rows, mixing_out, precision=HIGH))
    normed_two = lower_precision(rms_norm(mid, gains[1]))
    gate_up = lower_precision_back(jnp.dot(normed_two, expand_matrix, precision=HIGH))
    hidden = lower_precision(jax.nn.silu(gate_up[:, :FF]) * gate_up[:, FF:])
    return mid + jnp.dot(hidden, shrink_matrix, precision=HIGH)

def reference(layer_input, w_qkv, w_out, w_gu, w_down, norm_gains, lengths, cotangent):
    group = N_SEQ * TOK_DEV

    def to_groups(array):
        return array.reshape(N_SEQ, N_DP, TOK_DEV, D).transpose(1, 0, 2, 3).reshape(N_DP * group, D)

    def from_groups(array):
        return array.reshape(N_DP, N_SEQ, TOK_DEV, D).transpose(1, 0, 2, 3).reshape(N_DP * group, D)
    index = jnp.arange(group, dtype=jnp.int32)
    segment_index, token_position = jax.vmap(lambda row: layout(row, index))(lengths)
    flat_position = token_position.reshape(-1)
    inputs = to_groups(layer_input.astype(jnp.float32))
    grad_out = to_groups(cotangent.astype(jnp.float32))
    mixing_in = w_qkv.astype(jnp.float32).reshape(D, -1)
    mixing_out = w_out.astype(jnp.float32).reshape(QUERY_HEADS * HEAD_SIZE, D)
    expand_matrix = w_gu.astype(jnp.float32).reshape(D, 2 * FF)
    shrink_matrix = w_down.astype(jnp.float32).reshape(FF, D)

    def run(inputs, mixing_in, mixing_out, expand_matrix, shrink_matrix, gains):
        return forward(inputs, mixing_in, mixing_out, expand_matrix, shrink_matrix, gains, segment_index, flat_position)
    result, pullback = jax.vjp(run, inputs, mixing_in, mixing_out, expand_matrix, shrink_matrix, norm_gains.astype(jnp.float32))
    grads = pullback(grad_out)
    return (from_groups(result).astype(jnp.bfloat16), from_groups(grads[0]), grads[1].reshape(-1), grads[2].reshape(-1), grads[3].reshape(-1), grads[4].reshape(-1), grads[5])
```

```python
import functools
import math

import jax
import jax.numpy as jnp
from jax import lax
from jax.experimental import pallas as pl
from jax.experimental.pallas import tpu as pltpu
from jax.sharding import PartitionSpec as P

D = 576
QUERY_HEADS = 9
KEY_VALUE_HEADS = 3
HEAD_SIZE = 64
FF = 1536
HG = QUERY_HEADS // KEY_VALUE_HEADS

EPS = 1e-05
THETA = 100000.0
MASKED = -1e30
MESH = pl.DeviceIdType.MESH
BLK = 256
VMEM_LIMIT = 56 * 1024 * 1024
ORDERS = ((0, 2, 1), (1, 0, 2), (1, 0, 2))


def rms_norm(value_rows, gain):
    return (
        value_rows
        * lax.rsqrt(jnp.mean(value_rows * value_rows, axis=-1, keepdims=True) + EPS)
        * gain
    )


def layout(lengths_row, index):
    count = lengths_row.shape[0]
    earlier = jnp.arange(count)[:, None] >= jnp.arange(count)[None, :]
    ends = jnp.sum(jnp.where(earlier, lengths_row[None, :], 0), axis=1, dtype=jnp.int32)
    done = ends[None, :] <= index[:, None]
    return jnp.sum(jnp.where(done, lengths_row[None, :], 0), axis=1, dtype=jnp.int32)


def silu_product(gate_up):
    width = gate_up.shape[1] // 2
    return jax.nn.silu(gate_up[:, :width]) * gate_up[:, width:]


def grid_sizes(seq_count, dp_count):
    return (seq_count // 2, 2, dp_count // 2, 2)


def coords():
    seq, dp = lax.axis_index("seq"), lax.axis_index("dp")
    return [seq // 2, seq % 2, dp // 2, dp % 2]


def device_at(coord):
    return (coord[0] * 2 + coord[1], coord[2] * 2 + coord[3])


def moved(me, sizes, axis, step):
    other = list(me)
    other[axis] = lax.rem(me[axis] + step + sizes[axis], sizes[axis])
    return other


def greet(me, sizes):
    barrier = pltpu.get_barrier_semaphore()
    count = 0
    for axis in range(4):
        for step in range(1, sizes[axis]):
            pl.semaphore_signal(
                barrier,
                inc=1,
                device_id=device_at(moved(me, sizes, axis, step)),
                device_id_type=MESH,
            )
            count += 1
    pl.semaphore_wait(barrier, count)


def gather_steps(me, sizes, shards, outs, send, recv, core_send, core_recv, local):
    parts = len(shards)
    started = []
    for part in range(parts):
        own = pltpu.make_async_copy(
            shards[part], outs[part].at[me[0], me[1], me[2], me[3]], local.at[part]
        )
        own.start()
        started.append(own)
    for own in started:
        own.wait()

    def region(part, held, where):
        return outs[part].at[
            tuple(slice(None) if a in held else where[a] for a in range(3)) + (where[3],)
        ]

    def copy(part, phase, axis, held, step, arriving=False):
        where = moved(me, sizes, axis, -step) if arriving else me
        block = region(part, held, where)
        return pltpu.make_async_remote_copy(
            src_ref=block,
            dst_ref=block,
            send_sem=send.at[part, phase, step],
            recv_sem=recv.at[part, phase, step],
            device_id=device_at(moved(me, sizes, axis, step)),
            device_id_type=MESH,
        )

    def to_core(part, slot, held, where, arriving=False):
        there = moved(where, sizes, 3, 1) if arriving else where
        block = region(part, held, there)
        return pltpu.make_async_remote_copy(
            src_ref=block,
            dst_ref=block,
            send_sem=core_send.at[part, slot],
            recv_sem=core_recv.at[part, slot],
            device_id=device_at(moved(me, sizes, 3, 1)),
            device_id_type=MESH,
        )

    for part in range(parts):
        axis = ORDERS[part][0]
        for step in range(1, sizes[axis]):
            copy(part, 0, axis, (), step).start()
    yield
    pending = []
    for phase in range(3):
        for part in range(parts):
            axis = ORDERS[part][phase]
            held = ORDERS[part][:phase]
            for step in range(1, sizes[axis]):
                copy(part, phase, axis, held, step, arriving=True).wait_recv()
                if phase == 2:
                    origin = moved(me, sizes, axis, -step)
                    to_core(part, step, held, origin).start()
                    pending.append((part, step, held, origin))
            if phase < 2:
                following = ORDERS[part][phase + 1]
                for step in range(1, sizes[following]):
                    copy(part, phase + 1, following, ORDERS[part][: phase + 1], step).start()
            if phase == 1:
                to_core(part, 0, ORDERS[part][:2], me).start()
                pending.append((part, 0, ORDERS[part][:2], me))
            yield
    for part in range(parts):
        for phase in range(3):
            axis = ORDERS[part][phase]
            for step in range(1, sizes[axis]):
                copy(part, phase, axis, ORDERS[part][:phase], step).wait_send()
    for part, slot, held, origin in pending:
        to_core(part, slot, held, origin).wait_send()
        to_core(part, slot, held, origin, arriving=True).wait_recv()


def gather_semaphores(parts, most):
    return [
        pltpu.SemaphoreType.DMA((parts, 3, most)),
        pltpu.SemaphoreType.DMA((parts, 3, most)),
        pltpu.SemaphoreType.DMA((parts, most)),
        pltpu.SemaphoreType.DMA((parts, most)),
        pltpu.SemaphoreType.DMA((parts,)),
    ]


def gather_kernel(sizes, parts, *refs):
    me = coords()
    greet(me, sizes)
    for _ in gather_steps(
        me, sizes, refs[:parts], refs[parts : 2 * parts], *refs[2 * parts :]
    ):
        pass


def all_gather(shards, sizes, ident):
    parts = len(shards)
    most = max(sizes)
    return pl.pallas_call(
        functools.partial(gather_kernel, sizes, parts),
        out_shape=[jax.ShapeDtypeStruct(sizes + s.shape, s.dtype) for s in shards],
        in_specs=[pl.BlockSpec(memory_space=pltpu.VMEM)] * parts,
        out_specs=[pl.BlockSpec(memory_space=pltpu.VMEM)] * parts,
        scratch_shapes=gather_semaphores(parts, most),
        compiler_params=pltpu.CompilerParams(
            collective_id=ident, has_side_effects=True, vmem_limit_bytes=VMEM_LIMIT
        ),
        cost_estimate=pl.CostEstimate(flops=0, bytes_accessed=60_000_000, transcendentals=0),
    )(*shards)


def scatter_order(part):
    return (3,) + tuple(reversed(ORDERS[part]))


def scatter_kernel(sizes, parts, with_gains, *refs):
    me = coords()
    greet(me, sizes)
    for _ in scatter_steps(me, sizes, parts, with_gains, *refs):
        pass


def scatter_steps(me, sizes, parts, with_gains, *refs):
    n_in = parts + with_gains
    grads, outs = refs[:n_in], refs[n_in : 2 * n_in]
    rest = list(refs[2 * n_in :])
    arrived = [[rest.pop(0) for _ in range(4)] for _ in range(parts)]
    totals = [[rest.pop(0) for _ in range(3)] for _ in range(parts)]
    if with_gains:
        gain_arrived, gain_total = rest.pop(0), rest.pop(0)
        gain_send, gain_recv = rest.pop(0), rest.pop(0)
    send, recv = rest

    def held_ref(part, phase):
        return grads[part] if phase == 0 else totals[part][phase - 1]

    def view(part, phase, index):
        order = scatter_order(part)
        left = sorted(set(range(4)) - set(order[:phase]))
        return tuple(index if a == order[phase] else slice(None) for a in left)

    def copy(part, phase, step):
        axis = scatter_order(part)[phase]
        target = moved(me, sizes, axis, step)
        return pltpu.make_async_remote_copy(
            src_ref=held_ref(part, phase).at[view(part, phase, target[axis])],
            dst_ref=arrived[part][phase].at[step - 1],
            send_sem=send.at[part, phase, step],
            recv_sem=recv.at[part, phase, step],
            device_id=device_at(target),
            device_id_type=MESH,
        )

    def add(part, phase):
        axis = scatter_order(part)[phase]
        mine = held_ref(part, phase).at[view(part, phase, me[axis])]
        lead = mine.shape[:-2]
        others = arrived[part][phase]

        def total_at(place):
            value = mine[place].astype(jnp.float32)
            for step in range(1, sizes[axis]):
                value = value + others[(step - 1,) + place].astype(jnp.float32)
            return value

        if phase == 3:
            outs[part][...] = total_at((slice(None), slice(None)))
            return
        target = totals[part][phase]

        def body(flat, carry):
            place = []
            for size in reversed(lead):
                place.insert(0, lax.rem(flat, size))
                flat = flat // size
            place = tuple(place) + (slice(None), slice(None))
            target[place] = total_at(place).astype(target.dtype)
            return carry

        lax.fori_loop(0, math.prod(lead), body, 0)

    def gain_copy(phase, step):
        return pltpu.make_async_remote_copy(
            src_ref=gain_total.at[phase],
            dst_ref=gain_arrived.at[phase, step - 1],
            send_sem=gain_send.at[phase, step],
            recv_sem=gain_recv.at[phase, step],
            device_id=device_at(moved(me, sizes, phase, step)),
            device_id_type=MESH,
        )

    def start(phase, part):
        for step in range(1, sizes[scatter_order(part)[phase]]):
            copy(part, phase, step).start()

    def gain_start(phase):
        for step in range(1, sizes[phase]):
            gain_copy(phase, step).start()

    for part in range(parts):
        start(0, part)
    if with_gains:
        gain_total[0] = grads[parts][...]
        gain_start(0)
    yield
    for phase in range(4):
        for part in reversed(range(parts)):
            for step in range(1, sizes[scatter_order(part)[phase]]):
                copy(part, phase, step).wait_recv()
            add(part, phase)
            if phase < 3:
                start(phase + 1, part)
            yield
        if with_gains:
            value = gain_total[phase]
            for step in range(1, sizes[phase]):
                gain_copy(phase, step).wait_recv()
            slots = [value] + [gain_arrived[phase, s - 1] for s in range(1, sizes[phase])]
            value = sum(slots[1:], slots[0])
            if phase < 3:
                gain_total[phase + 1] = value
                gain_start(phase + 1)
            else:
                outs[parts][...] = value
    for phase in range(4):
        for part in range(parts):
            for step in range(1, sizes[scatter_order(part)[phase]]):
                copy(part, phase, step).wait_send()
        if with_gains:
            for step in range(1, sizes[phase]):
                gain_copy(phase, step).wait_send()


def scatter_buffers(grads, sizes):
    parts = len(grads)
    scratch = []
    for part in range(parts):
        left = [0, 1, 2, 3]
        for axis in scatter_order(part):
            left.remove(axis)
            shape = (sizes[axis] - 1,) + tuple(sizes[a] for a in left) + grads[part].shape[4:]
            scratch.append(pltpu.VMEM(shape, jnp.bfloat16))
    for part in range(parts):
        left = [0, 1, 2, 3]
        for axis in scatter_order(part)[:3]:
            left.remove(axis)
            shape = tuple(sizes[a] for a in left) + grads[part].shape[4:]
            scratch.append(pltpu.VMEM(shape, jnp.bfloat16))
    return scratch


def reduce_scatter(grads, gains, sizes, ident):
    parts = len(grads)
    most = max(sizes)
    scratch = scatter_buffers(grads, sizes)
    outs = [jax.ShapeDtypeStruct(g.shape[4:], jnp.float32) for g in grads]
    args = list(grads)
    if gains is not None:
        args.append(gains)
        outs.append(jax.ShapeDtypeStruct(gains.shape, jnp.float32))
        scratch += [
            pltpu.VMEM((4, most - 1) + gains.shape, jnp.float32),
            pltpu.VMEM((4,) + gains.shape, jnp.float32),
            pltpu.SemaphoreType.DMA((4, most)),
            pltpu.SemaphoreType.DMA((4, most)),
        ]
    scratch += [pltpu.SemaphoreType.DMA((parts, 4, most))] * 2
    return pl.pallas_call(
        functools.partial(scatter_kernel, sizes, parts, int(gains is not None)),
        out_shape=outs,
        in_specs=[pl.BlockSpec(memory_space=pltpu.VMEM)] * len(args),
        out_specs=[pl.BlockSpec(memory_space=pltpu.VMEM)] * len(outs),
        scratch_shapes=scratch,
        compiler_params=pltpu.CompilerParams(
            collective_id=ident, has_side_effects=True, vmem_limit_bytes=VMEM_LIMIT
        ),
        cost_estimate=pl.CostEstimate(flops=0, bytes_accessed=60_000_000, transcendentals=0),
    )(*args)


def padded_rows(count):
    return -(-count // 2048) * 16


def pack(flat, lead):
    size = flat.shape[-1]
    rows = padded_rows(size)
    none = [(0, 0)] * len(lead)
    if size % 128 == 0:
        flat = flat.reshape(lead + (size // 128, 128))
        return jnp.pad(flat, none + [(0, rows - size // 128), (0, 0)])
    return jnp.pad(flat, none + [(0, rows * 128 - size)]).reshape(lead + (rows, 128))


def unpack(packed, lead, size):
    if size % 128 == 0:
        return packed[..., : size // 128, :].reshape(lead + (size,))
    return packed.reshape(lead + (-1,))[..., :size]


def dot_rows(left, right):
    return lax.dot_general(left, right, (((1,), (1,)), ((), ())), preferred_element_type=jnp.float32)


def dot_columns(left, right):
    return lax.dot_general(left, right, (((0,), (0,)), ((), ())), preferred_element_type=jnp.float32)


def head_columns(head):
    first = head * HEAD_SIZE
    second = first + KEY_VALUE_HEADS * HEAD_SIZE
    return slice(first, first + HEAD_SIZE), slice(second, second + HEAD_SIZE)


def head_columns(head):
    first = head * HEAD_SIZE
    second = first + KEY_VALUE_HEADS * HEAD_SIZE
    return slice(first, first + HEAD_SIZE), slice(second, second + HEAD_SIZE)


def blocks_of(offset, window, tile, tiles):
    return (tile if offset == window else 0), (tile + 1 if offset == 0 else tiles)


def neighbour(me, sizes, axis, step):
    return device_at(moved(me, sizes, axis, step))


class PairFlow:
    def __init__(self, me, sizes, mine, slots, chain_send, cross_send, recv):
        self.me, self.sizes, self.mine, self.slots = me, sizes, mine, slots
        self.chain_send, self.cross_send, self.recv = chain_send, cross_send, recv
        self.reach = sizes[0] // 2

    def chain(self, j):
        return pltpu.make_async_remote_copy(
            src_ref=self.mine if j == 0 else self.slots.at[2 * j],
            dst_ref=self.slots.at[2 * j + 2],
            send_sem=self.chain_send.at[j],
            recv_sem=self.recv.at[2 * j + 2],
            device_id=neighbour(self.me, self.sizes, 0, 1),
            device_id_type=MESH,
        )

    def cross(self, j, side):
        slot = 2 * j + 1 if side == 0 else 2 * j - 1
        return pltpu.make_async_remote_copy(
            src_ref=self.mine if j == 0 else self.slots.at[2 * j],
            dst_ref=self.slots.at[slot],
            send_sem=self.cross_send.at[j],
            recv_sem=self.recv.at[slot],
            device_id=neighbour(self.me, self.sizes, 1, 1),
            device_id_type=MESH,
        )

    def each(self, j, act):
        there = self.me[0] >= j
        if j < self.reach:

            @pl.when(there & (self.me[0] + 1 < self.sizes[0]))
            def _():
                act(self.chain(j))

            @pl.when(there & (self.me[1] == 0))
            def _():
                act(self.cross(j, 0))

        if j > 0:

            @pl.when(there & (self.me[1] == 1))
            def _():
                act(self.cross(j, 1))

    def forward(self, j):
        self.each(j, lambda copy: copy.start())

    def finish(self, j):
        self.each(j, lambda copy: copy.wait_send())

    def arrive(self, offset):
        block = self.slots.at[offset]
        pltpu.make_async_remote_copy(
            src_ref=block,
            dst_ref=block,
            send_sem=self.cross_send.at[0],
            recv_sem=self.recv.at[offset],
            device_id=neighbour(self.me, self.sizes, 1, 1),
            device_id_type=MESH,
        ).wait_recv()


def gather_attend_kernel(sizes, parts, tiles, *refs):
    shards, refs = refs[:parts], refs[parts:]
    (q_ref, mine_ref, index_ref, start_ref), refs = refs[:4], refs[4:]
    outs, refs = refs[:parts], refs[parts:]
    slots, o_ref, lse_ref, total_ref = refs[:4]
    semaphores, (chain_send, cross_send, recv, own_sem) = refs[4:9], refs[9:]
    me = coords()
    place = me[0] * 2 + me[1]
    window = sizes[0]
    greet(me, sizes)
    flow = PairFlow(me, sizes, mine_ref, slots, chain_send, cross_send, recv)
    flow.forward(0)
    own = pltpu.make_async_copy(mine_ref, slots.at[0], own_sem)
    own.start()
    weights = gather_steps(me, sizes, shards, outs, *semaphores)
    next(weights)
    token_rows = tiles * BLK

    def unit(offset, tile, head):
        key_part, value_part = head_columns(head)
        low, high = blocks_of(offset, window, tile, tiles)
        q = q_ref[head, tile]
        index, start = index_ref[tile], start_ref[tile]
        width = q.shape[0]
        held = mine_ref if offset == 0 else slots.at[offset]
        base = (place - offset) * token_rows

        def step(block, carry):
            highest, total, acc = carry
            first = pl.multiple_of(block * BLK, BLK)
            rows = pl.ds(first, BLK)
            s = dot_rows(held[rows, key_part], q)
            row = base + first + lax.broadcasted_iota(jnp.int32, s.shape, 0)
            s = jnp.where((row <= index) & (row >= start), s, MASKED)
            new = jnp.maximum(highest, jnp.max(s, axis=0, keepdims=True))
            p = jnp.exp(s - new)
            fade = jnp.exp(highest - new)
            total = total * fade + jnp.sum(p, axis=0, keepdims=True)
            acc = acc * fade + dot_columns(held[rows, value_part], p.astype(jnp.bfloat16))
            return new, total, acc

        if offset == 0:
            carry = (
                jnp.full((1, width), MASKED, jnp.float32),
                jnp.zeros((1, width), jnp.float32),
                jnp.zeros((HEAD_SIZE, width), jnp.float32),
            )
        else:
            carry = lse_ref[head, tile], total_ref[head, tile], o_ref[head, tile]
        highest, total, acc = lax.fori_loop(low, high, step, carry)
        lse_ref[head, tile], total_ref[head, tile], o_ref[head, tile] = highest, total, acc

    def attend(offset):
        for tile, head in [(t, h) for t in range(tiles) for h in range(KEY_VALUE_HEADS)]:
            unit(offset, tile, head)

    attend(0)
    for j in range(1, flow.reach + 1):

        @pl.when(me[0] >= j)
        def _(j=j):
            flow.arrive(2 * j)

        flow.forward(j)

        @pl.when(me[0] >= j)
        def _(j=j):
            attend(2 * j)

        if j == 1:
            next(weights)
            next(weights)
            next(weights)

        @pl.when(place >= 2 * j - 1)
        def _(j=j):
            flow.arrive(2 * j - 1)
            attend(2 * j - 1)

        if j == 1:
            next(weights)

    for tile, head in [(t, h) for t in range(tiles) for h in range(KEY_VALUE_HEADS)]:
        total = total_ref[head, tile]
        o_ref[head, tile] = o_ref[head, tile] / total
        lse_ref[head, tile] = lse_ref[head, tile] + jnp.log(total)
    for _ in weights:
        pass
    for j in range(flow.reach + 1):
        flow.finish(j)
    own.wait()


def gather_attend(shards, query, pairs_mine, index_rows, start_rows, sizes, ident):
    parts = len(shards)
    kvh, tiles, width, _ = query.shape
    window = sizes[0]
    f32 = jnp.float32
    whole = pl.BlockSpec(memory_space=pltpu.VMEM)
    column = jax.ShapeDtypeStruct((kvh, tiles, HEAD_SIZE, width), f32)
    line = jax.ShapeDtypeStruct((kvh, tiles, 1, width), f32)
    out_shape = [jax.ShapeDtypeStruct(sizes + s.shape, s.dtype) for s in shards]
    out_shape += [
        jax.ShapeDtypeStruct((window + 1,) + pairs_mine.shape, pairs_mine.dtype),
        column,
        line,
    ]
    dma = pltpu.SemaphoreType.DMA
    results = pl.pallas_call(
        functools.partial(gather_attend_kernel, sizes, parts, tiles),
        out_shape=out_shape,
        in_specs=[whole] * (parts + 4),
        out_specs=[whole] * len(out_shape),
        scratch_shapes=[pltpu.VMEM(line.shape, f32)]
        + gather_semaphores(parts, max(sizes))
        + [dma((window // 2 + 1,)), dma((window // 2 + 1,)), dma((window + 1,)), dma],
        compiler_params=pltpu.CompilerParams(
            collective_id=ident, has_side_effects=True, vmem_limit_bytes=VMEM_LIMIT
        ),
        cost_estimate=pl.CostEstimate(
            flops=10_000_000_000, bytes_accessed=60_000_000, transcendentals=0
        ),
    )(*shards, query, pairs_mine, index_rows, start_rows)
    return results[:parts], *results[parts:]


class SumFlow:
    def __init__(self, me, sizes, partial, crossed, chained, chain_send, cross_send, chain_recv, cross_recv):
        self.me, self.sizes, self.partial = me, sizes, partial
        self.crossed, self.chained = crossed, chained
        self.chain_send, self.cross_send = chain_send, cross_send
        self.chain_recv, self.cross_recv = chain_recv, cross_recv
        self.reach = sizes[0] // 2

    def chain(self, j):
        return pltpu.make_async_remote_copy(
            src_ref=self.partial.at[2 * j],
            dst_ref=self.chained.at[j - 1],
            send_sem=self.chain_send.at[j],
            recv_sem=self.chain_recv.at[j - 1],
            device_id=neighbour(self.me, self.sizes, 0, -1),
            device_id_type=MESH,
        )

    def cross(self, offset, side):
        j = (offset + 1) // 2 if side == 0 else offset // 2
        return pltpu.make_async_remote_copy(
            src_ref=self.partial.at[offset],
            dst_ref=self.crossed.at[j],
            send_sem=self.cross_send.at[offset // 2],
            recv_sem=self.cross_recv.at[j],
            device_id=neighbour(self.me, self.sizes, 1, 1),
            device_id_type=MESH,
        )

    def each_cross(self, offset, act):
        for side in range(2):

            @pl.when((self.me[1] == side) & (self.me[0] * 2 + side >= offset))
            def _(side=side):
                act(self.cross(offset, side))

    def has_cross(self, j):
        side = self.me[1]
        if j == 0:
            return side == 0
        if j == self.reach:
            return (side == 1) & (self.me[0] >= j)
        return self.me[0] >= j

    def has_chain(self, j):
        return (self.me[0] >= j) & (self.me[0] + 1 < self.sizes[0])

    def cross_arrive(self, j):
        pltpu.make_async_remote_copy(
            src_ref=self.crossed.at[j],
            dst_ref=self.crossed.at[j],
            send_sem=self.cross_send.at[0],
            recv_sem=self.cross_recv.at[j],
            device_id=neighbour(self.me, self.sizes, 1, 1),
            device_id_type=MESH,
        ).wait_recv()

    def chain_arrive(self, j):
        pltpu.make_async_remote_copy(
            src_ref=self.chained.at[j],
            dst_ref=self.chained.at[j],
            send_sem=self.chain_send.at[0],
            recv_sem=self.chain_recv.at[j],
            device_id=neighbour(self.me, self.sizes, 0, -1),
            device_id_type=MESH,
        ).wait_recv()


def scatter_attend_kernel(sizes, parts, tiles, rounds, *refs):
    grads, refs = refs[:parts], refs[parts:]
    (q_ref, do_ref, slots, index_ref, start_ref, lse_ref, delta_ref), refs = refs[:7], refs[7:]
    outs, refs = refs[:parts], refs[parts:]
    (dq_ref, dkv_ref), refs = refs[:2], refs[2:]
    accs, refs = refs[: 2 * KEY_VALUE_HEADS], refs[2 * KEY_VALUE_HEADS :]
    flow_refs, scatter_refs = refs[:7], refs[7:]
    me = coords()
    place = me[0] * 2 + me[1]
    window = sizes[0]
    greet(me, sizes)
    flow = SumFlow(me, sizes, *flow_refs)
    partial, crossed, chained = flow_refs[:3]
    weights = scatter_steps(me, sizes, parts, 0, *grads, *outs, *scatter_refs)
    next(weights)
    token_rows = tiles * BLK
    dq_ref[...] = jnp.zeros_like(dq_ref)

    def unit(offset, tile, head):
        key_part, value_part = head_columns(head)
        low, high = blocks_of(offset, window, tile, tiles)
        q, do = q_ref[head, tile], do_ref[head, tile]
        index, start = index_ref[tile], start_ref[tile]
        lse, delta = lse_ref[head, tile], delta_ref[head, tile]
        dk_acc, dv_acc = accs[head], accs[KEY_VALUE_HEADS + head]
        base = (place - offset) * token_rows

        def step(block, dq):
            first = pl.multiple_of(block * BLK, BLK)
            rows = pl.ds(first, BLK)
            k = slots[offset, rows, key_part]
            s = dot_rows(k, q)
            dp = dot_rows(slots[offset, rows, value_part], do)
            row = base + first + lax.broadcasted_iota(jnp.int32, s.shape, 0)
            s = jnp.where((row <= index) & (row >= start), s - lse, MASKED)
            p = jnp.exp(s)
            ds = (p * (dp - delta)).astype(jnp.bfloat16)
            dv_acc[rows, :] += jnp.dot(p.astype(jnp.bfloat16), do, preferred_element_type=jnp.float32)
            dk_acc[rows, :] += jnp.dot(ds, q, preferred_element_type=jnp.float32)
            return dq + dot_columns(k, ds)

        dq_ref[head, tile] = lax.fori_loop(low, high, step, dq_ref[head, tile])

    def collect(offset):
        for acc in accs:
            acc[...] = jnp.zeros_like(acc)
        for tile, head in [(t, h) for t in range(tiles) for h in range(KEY_VALUE_HEADS)]:
            unit(offset, tile, head)

    def summed(rows):
        return jnp.concatenate([acc[rows, :] for acc in accs], axis=1)

    def over_rows(body):
        def run(block, carry):
            body(pl.ds(pl.multiple_of(block * BLK, BLK), BLK))
            return carry

        lax.fori_loop(0, tiles, run, 0)

    def keep(offset):
        def body(rows):
            partial[offset, rows, :] = summed(rows).astype(partial.dtype)

        over_rows(body)

    def fold(j, source):
        def body(rows):
            partial[2 * j, rows, :] = (
                partial[2 * j, rows, :].astype(jnp.float32) + source[j, rows, :].astype(jnp.float32)
            ).astype(partial.dtype)

        over_rows(body)

    def fold_own(source):
        def body(rows):
            dkv_ref[rows, :] += source[0, rows, :].astype(jnp.float32)

        over_rows(body)

    def progress(place_in_order):
        for _ in range(rounds[place_in_order]):
            next(weights)

    turn = 0
    for j in reversed(range(1, flow.reach + 1)):
        odd = 2 * j - 1

        @pl.when(place >= odd)
        def _(odd=odd):
            collect(odd)
            keep(odd)

        flow.each_cross(odd, lambda copy: copy.start())
        progress(turn)

        @pl.when(me[0] >= j)
        def _(j=j):
            collect(2 * j)
            keep(2 * j)

        @pl.when(flow.has_cross(j))
        def _(j=j):
            flow.cross_arrive(j)
            fold(j, crossed)

        if j < flow.reach:

            @pl.when(flow.has_chain(j))
            def _(j=j):
                flow.chain_arrive(j)
                fold(j, chained)

        @pl.when(me[0] >= j)
        def _(j=j):
            flow.chain(j).start()

        progress(turn + 1)
        turn += 2
    collect(0)

    def first(rows):
        dkv_ref[rows, :] = summed(rows)

    over_rows(first)
    progress(turn)

    @pl.when(flow.has_cross(0))
    def _():
        flow.cross_arrive(0)
        fold_own(crossed)

    @pl.when(flow.has_chain(0))
    def _():
        flow.chain_arrive(0)
        fold_own(chained)

    for _ in weights:
        pass
    for j in range(1, flow.reach + 1):
        flow.each_cross(2 * j - 1, lambda copy: copy.wait_send())

        @pl.when(me[0] >= j)
        def _(j=j):
            flow.chain(j).wait_send()


def scatter_attend(grads, arrays, sizes, ident):
    parts = len(grads)
    kvh, tiles, width, _ = arrays[0].shape
    window, reach = sizes[0], sizes[0] // 2
    pair_shape = arrays[2].shape[1:]
    f32 = jnp.float32
    whole = pl.BlockSpec(memory_space=pltpu.VMEM)
    out_shape = [jax.ShapeDtypeStruct(g.shape[4:], f32) for g in grads]
    out_shape += [
        jax.ShapeDtypeStruct((kvh, tiles, HEAD_SIZE, width), f32),
        jax.ShapeDtypeStruct(pair_shape, f32),
    ]
    dma = pltpu.SemaphoreType.DMA
    scratch = [pltpu.VMEM((pair_shape[0], HEAD_SIZE), f32)] * (2 * kvh)
    scratch += [
        pltpu.VMEM((window + 1,) + pair_shape, jnp.bfloat16),
        pltpu.VMEM((reach + 1,) + pair_shape, jnp.bfloat16),
        pltpu.VMEM((reach,) + pair_shape, jnp.bfloat16),
        dma((reach + 1,)),
        dma((reach + 1,)),
        dma((reach,)),
        dma((reach + 1,)),
    ]
    scratch += scatter_buffers(grads, sizes) + [dma((parts, 4, max(sizes)))] * 2
    rounds = [parts, 0] + [0] * (window - 4) + [parts, parts, 0]
    results = pl.pallas_call(
        functools.partial(scatter_attend_kernel, sizes, parts, tiles, rounds),
        out_shape=out_shape,
        in_specs=[whole] * (parts + len(arrays)),
        out_specs=[whole] * len(out_shape),
        scratch_shapes=scratch,
        compiler_params=pltpu.CompilerParams(
            collective_id=ident, has_side_effects=True, vmem_limit_bytes=VMEM_LIMIT
        ),
        cost_estimate=pl.CostEstimate(
            flops=25_000_000_000, bytes_accessed=60_000_000, transcendentals=0
        ),
    )(*grads, *arrays)
    return results[:parts], *results[parts:]


def per_device(sizes, layer_input, w_qkv, w_out, w_gu, w_down, norm_gains, lengths, cotangent):
    token_rows = layer_input.shape[0]
    query_width = QUERY_HEADS * HEAD_SIZE
    key_width = KEY_VALUE_HEADS * HEAD_SIZE
    scale = 1.0 / math.sqrt(HEAD_SIZE)
    tiles = token_rows // BLK
    kvh = KEY_VALUE_HEADS

    (qkv_all,) = all_gather([pack(w_qkv, ())], sizes, 0)
    mixing_in = unpack(qkv_all, sizes, w_qkv.shape[0]).reshape(D, -1)

    query_index = lax.axis_index("seq") * token_rows + jnp.arange(token_rows, dtype=jnp.int32)
    start = layout(lengths[0], query_index)
    half = HEAD_SIZE // 2
    freq = jnp.exp(jnp.arange(half, dtype=jnp.float32) * (-2.0 * math.log(THETA) / HEAD_SIZE))
    angle = (query_index - start).astype(jnp.float32)[:, None] * freq[None, :]
    cosine, sine = jnp.cos(angle)[:, None, :], jnp.sin(angle)[:, None, :]

    def rotated(rows, sign):
        first, second = rows[..., :half], rows[..., half:]
        turn = sign * sine
        return jnp.concatenate(
            [first * cosine - second * turn, second * cosine + first * turn], axis=-1
        )

    inputs = layer_input.astype(jnp.float32)
    normed, norm_back = jax.vjp(rms_norm, inputs, norm_gains[0])
    normed_low = normed.astype(jnp.bfloat16)
    projected = jnp.dot(normed_low, mixing_in, preferred_element_type=jnp.float32)
    heads = projected[:, : query_width + key_width].reshape(token_rows, -1, HEAD_SIZE)
    turned = rotated(heads, 1.0).astype(jnp.bfloat16)
    pairs_mine = jnp.concatenate(
        [
            turned[:, QUERY_HEADS:].reshape(token_rows, key_width),
            projected[:, query_width + key_width :].astype(jnp.bfloat16),
        ],
        axis=1,
    )
    def stacked(rows):
        return (
            rows.reshape(tiles, BLK, kvh, HG, HEAD_SIZE)
            .transpose(2, 0, 3, 1, 4)
            .reshape(kvh, tiles, HG * BLK, HEAD_SIZE)
        )

    def unstacked(columns):
        return (
            columns.reshape(kvh, tiles, HEAD_SIZE, HG, BLK)
            .transpose(1, 4, 0, 3, 2)
            .reshape(token_rows, QUERY_HEADS, HEAD_SIZE)
        )

    def row_vector(values):
        return jnp.tile(values.reshape(tiles, 1, BLK), (1, 1, HG))

    query = stacked(turned[:, :QUERY_HEADS] * jnp.bfloat16(scale))
    index_rows, start_rows = row_vector(query_index), row_vector(start)

    width = HG * BLK
    f32 = jnp.float32
    gathered, pairs, attended_t, lse = gather_attend(
        [pack(w, ()) for w in (w_gu, w_down, w_out)],
        query,
        pairs_mine,
        index_rows,
        start_rows,
        sizes,
        1,
    )
    expand_matrix = unpack(gathered[0], sizes, w_gu.shape[0]).reshape(D, 2 * FF)
    shrink_matrix = unpack(gathered[1], sizes, w_down.shape[0]).reshape(FF, D)
    mixing_out = unpack(gathered[2], sizes, w_out.shape[0]).reshape(query_width, D)
    attended_rows = unstacked(attended_t)
    attended_low = attended_rows.reshape(token_rows, query_width).astype(jnp.bfloat16)
    mid = inputs + jnp.dot(attended_low, mixing_out, preferred_element_type=f32)
    normed_two, norm_two_back = jax.vjp(rms_norm, mid, norm_gains[1])
    normed_two_low = normed_two.astype(jnp.bfloat16)
    gate_up = jnp.dot(normed_two_low, expand_matrix, preferred_element_type=f32)
    hidden, hidden_back = jax.vjp(silu_product, gate_up)
    hidden_low = hidden.astype(jnp.bfloat16)
    result = (mid + jnp.dot(hidden_low, shrink_matrix, preferred_element_type=f32)).astype(
        jnp.bfloat16
    )
    grad_down = jnp.einsum("tf,td->fd", hidden_low, cotangent, preferred_element_type=f32)
    d_hidden = jnp.einsum("td,fd->tf", cotangent, shrink_matrix, preferred_element_type=f32)
    d_gate_up = hidden_back(d_hidden)[0].astype(jnp.bfloat16)
    grad_expand = jnp.einsum("td,tf->df", normed_two_low, d_gate_up, preferred_element_type=f32)
    d_normed_two = jnp.einsum("tf,df->td", d_gate_up, expand_matrix, preferred_element_type=f32)
    d_mid_part, grad_gain_two = norm_two_back(d_normed_two)
    d_mid = cotangent.astype(f32) + d_mid_part
    d_branch = d_mid.astype(jnp.bfloat16)
    grad_mixing_out = jnp.einsum("tq,td->qd", attended_low, d_branch, preferred_element_type=f32)
    d_attended = jnp.einsum("td,qd->tq", d_branch, mixing_out, preferred_element_type=f32).astype(
        jnp.bfloat16
    )
    delta = jnp.sum(
        d_attended.reshape(token_rows, QUERY_HEADS, HEAD_SIZE).astype(f32) * attended_rows, axis=-1
    )
    delta_rows = (
        delta.reshape(tiles, BLK, kvh, HG).transpose(2, 0, 3, 1).reshape(kvh, tiles, 1, width)
    )
    def by_owner(grad):
        return grad.astype(jnp.bfloat16).reshape(sizes + (-1,))

    (gu_mine, down_mine, out_mine), d_query_t, d_pairs_mine = scatter_attend(
        [pack(by_owner(g), sizes) for g in (grad_expand, grad_down, grad_mixing_out)],
        [query, stacked(d_attended), pairs, index_rows, start_rows, lse, delta_rows],
        sizes,
        2,
    )
    d_query = unstacked(d_query_t) * scale
    d_turned = jnp.concatenate(
        [d_query, d_pairs_mine[:, :key_width].reshape(token_rows, kvh, HEAD_SIZE)], axis=1
    )
    d_projected = jnp.concatenate(
        [rotated(d_turned, -1.0).reshape(token_rows, -1), d_pairs_mine[:, key_width:]], axis=1
    ).astype(jnp.bfloat16)
    grad_mixing_in = jnp.einsum("td,tq->dq", normed_low, d_projected, preferred_element_type=f32)
    d_normed = jnp.einsum("tq,dq->td", d_projected, mixing_in, preferred_element_type=f32)
    d_input_part, grad_gain_one = norm_back(d_normed)
    gains = jnp.stack([grad_gain_one, grad_gain_two])
    qkv_mine, gains_sum = reduce_scatter(
        [pack(by_owner(grad_mixing_in), sizes)], gains, sizes, 3
    )
    return (
        result,
        d_mid + d_input_part,
        unpack(qkv_mine, (), w_qkv.shape[0]),
        unpack(out_mine, (), w_out.shape[0]),
        unpack(gu_mine, (), w_gu.shape[0]),
        unpack(down_mine, (), w_down.shape[0]),
        gains_sum,
    )


def solution(mesh):
    spread = P(("seq", "dp"))
    rows = P(("seq", "dp"), None)
    return jax.shard_map(
        functools.partial(per_device, grid_sizes(mesh.shape["seq"], mesh.shape["dp"])),
        mesh=mesh,
        in_specs=(rows, spread, spread, spread, spread, P(), P("dp", None), rows),
        out_specs=(rows, rows, spread, spread, spread, spread, P()),
        check_vma=False,
    )
```

```python
import functools
import math

import jax
import jax.numpy as jnp
from jax import lax
from jax.experimental import pallas as pl
from jax.experimental.pallas import tpu as pltpu
from jax.sharding import PartitionSpec as P

D = 576
QUERY_HEADS = 9
KEY_VALUE_HEADS = 3
HEAD_SIZE = 64
FF = 1536
HG = QUERY_HEADS // KEY_VALUE_HEADS

EPS = 1e-05
THETA = 100000.0
MASKED = -1e30
MESH = pl.DeviceIdType.MESH
BLK = 256
VMEM_LIMIT = 56 * 1024 * 1024
ACROSS_LAST, ALONG_Y_LAST = (0, 2, 1), (0, 1, 2)
GATHER_ROUNDS = (0, 2, 2, 2, 2, 1, 1, 0, 1)
SCATTER_ROUNDS = (2, 2, 0, 1, 1, 2, 2, 1, 2)


def rms_norm(value_rows, gain):
    return (
        value_rows
        * lax.rsqrt(jnp.mean(value_rows * value_rows, axis=-1, keepdims=True) + EPS)
        * gain
    )


def layout(lengths_row, index):
    count = lengths_row.shape[0]
    earlier = jnp.arange(count)[:, None] >= jnp.arange(count)[None, :]
    ends = jnp.sum(jnp.where(earlier, lengths_row[None, :], 0), axis=1, dtype=jnp.int32)
    done = ends[None, :] <= index[:, None]
    return jnp.sum(jnp.where(done, lengths_row[None, :], 0), axis=1, dtype=jnp.int32)


def silu_product(gate_up):
    width = gate_up.shape[1] // 2
    return jax.nn.silu(gate_up[:, :width]) * gate_up[:, width:]


def grid_sizes(seq_count, dp_count):
    return (seq_count // 2, 2, dp_count // 2, 2)


def coords():
    seq, dp = lax.axis_index("seq"), lax.axis_index("dp")
    return [seq // 2, seq % 2, dp // 2, dp % 2]


def device_at(coord):
    return (coord[0] * 2 + coord[1], coord[2] * 2 + coord[3])


def moved(me, sizes, axis, step):
    other = list(me)
    other[axis] = lax.rem(me[axis] + step + sizes[axis], sizes[axis])
    return other


def greet(me, sizes):
    barrier = pltpu.get_barrier_semaphore()
    count = 0
    for axis in range(4):
        for step in range(1, sizes[axis]):
            pl.semaphore_signal(
                barrier,
                inc=1,
                device_id=device_at(moved(me, sizes, axis, step)),
                device_id_type=MESH,
            )
            count += 1
    pl.semaphore_wait(barrier, count)


class Piece:
    def __init__(self, array, shape, order):
        self.array, self.order = array, order
        self.rows, self.columns = shape[0][1], shape[1][1]
        self.at = tuple(pl.ds(first, size) for first, size in shape)


def pieces_of(shards, orders, cuts):
    pieces = []
    for array, shard in enumerate(shards):
        rows, columns = shard.shape[-2:]
        cut = rows // 32 * 16 if cuts[array] and rows >= 64 else 0
        spans = [(0, cut), (cut, rows - cut)] if cut else [(0, rows)]
        for number, span in enumerate(spans):
            order = orders[array][number % len(orders[array])]
            pieces.append(Piece(array, (span, (0, columns)), order))
    return pieces


def gather_steps(me, sizes, pieces, shards, outs, send, recv, core_send, core_recv, local):
    parts = len(pieces)
    started = []
    for array in range(len(shards)):
        own = pltpu.make_async_copy(
            shards[array], outs[array].at[me[0], me[1], me[2], me[3]], local.at[array]
        )
        own.start()
        started.append(own)

    def region(part, held, where):
        piece = pieces[part]
        lead = tuple(slice(None) if a in held else where[a] for a in range(3)) + (where[3],)
        return outs[piece.array].at[lead + piece.at]

    def copy(part, phase, step, arriving=False):
        order = pieces[part].order
        where = moved(me, sizes, order[phase], -step) if arriving else me
        block = region(part, order[:phase], where)
        source = block
        if phase == 0 and not arriving:
            source = shards[pieces[part].array].at[pieces[part].at]
        return pltpu.make_async_remote_copy(
            src_ref=source,
            dst_ref=block,
            send_sem=send.at[part, phase, step],
            recv_sem=recv.at[part, phase, step],
            device_id=device_at(moved(me, sizes, order[phase], step)),
            device_id_type=MESH,
        )

    def to_core(part, slot, held, where, arriving=False):
        there = moved(where, sizes, 3, 1) if arriving else where
        block = region(part, held, there)
        return pltpu.make_async_remote_copy(
            src_ref=block,
            dst_ref=block,
            send_sem=core_send.at[part, slot],
            recv_sem=core_recv.at[part, slot],
            device_id=device_at(moved(me, sizes, 3, 1)),
            device_id_type=MESH,
        )

    for part in range(parts):
        for step in range(1, sizes[pieces[part].order[0]]):
            copy(part, 0, step).start()
    for own in started:
        own.wait()
    yield
    pending = []
    turns = [(phase, part) for phase in range(3) for part in range(parts)]
    for phase, part in sorted(turns, key=lambda turn: (2 * turn[0] + turn[1], turn[0])):
        order = pieces[part].order
        held = order[:phase]
        for step in range(1, sizes[order[phase]]):
            copy(part, phase, step, arriving=True).wait_recv()
            if phase == 2:
                origin = moved(me, sizes, order[phase], -step)
                to_core(part, step, held, origin).start()
                pending.append((part, step, held, origin))
        if phase < 2:
            for step in range(1, sizes[order[phase + 1]]):
                copy(part, phase + 1, step).start()
        if phase == 1:
            to_core(part, 0, order[:2], me).start()
            pending.append((part, 0, order[:2], me))
        yield
    for part in range(parts):
        for phase in range(3):
            for step in range(1, sizes[pieces[part].order[phase]]):
                copy(part, phase, step).wait_send()
    for part, slot, held, origin in pending:
        to_core(part, slot, held, origin).wait_send()
        to_core(part, slot, held, origin, arriving=True).wait_recv()


def gather_semaphores(arrays, parts, most):
    return [
        pltpu.SemaphoreType.DMA((parts, 3, most)),
        pltpu.SemaphoreType.DMA((parts, 3, most)),
        pltpu.SemaphoreType.DMA((parts, most)),
        pltpu.SemaphoreType.DMA((parts, most)),
        pltpu.SemaphoreType.DMA((arrays,)),
    ]


def gather_kernel(sizes, pieces, arrays, *refs):
    me = coords()
    greet(me, sizes)
    for _ in gather_steps(
        me, sizes, pieces, refs[:arrays], refs[arrays : 2 * arrays], *refs[2 * arrays :]
    ):
        pass


def all_gather(shards, sizes, ident):
    arrays = len(shards)
    pieces = pieces_of(shards, [(ALONG_Y_LAST, ACROSS_LAST)] * arrays, [True] * arrays)
    return pl.pallas_call(
        functools.partial(gather_kernel, sizes, pieces, arrays),
        out_shape=[jax.ShapeDtypeStruct(sizes + s.shape, s.dtype) for s in shards],
        in_specs=[pl.BlockSpec(memory_space=pltpu.VMEM)] * arrays,
        out_specs=[pl.BlockSpec(memory_space=pltpu.VMEM)] * arrays,
        scratch_shapes=gather_semaphores(arrays, len(pieces), max(sizes)),
        compiler_params=pltpu.CompilerParams(
            collective_id=ident, has_side_effects=True, vmem_limit_bytes=VMEM_LIMIT
        ),
        cost_estimate=pl.CostEstimate(flops=0, bytes_accessed=60_000_000, transcendentals=0),
    )(*shards)


def scatter_order(piece):
    return (3,) + tuple(reversed(piece.order))


def scatter_kernel(sizes, pieces, arrays, with_gains, *refs):
    me = coords()
    greet(me, sizes)
    for _ in scatter_steps(me, sizes, pieces, arrays, with_gains, *refs):
        pass


def scatter_steps(me, sizes, pieces, arrays, with_gains, *refs):
    parts = len(pieces)
    n_in = arrays + with_gains
    grads, outs = refs[:n_in], refs[n_in : 2 * n_in]
    rest = list(refs[2 * n_in :])
    arrived = [[rest.pop(0) for _ in range(4)] for _ in range(parts)]
    totals = [[rest.pop(0) for _ in range(3)] for _ in range(parts)]
    if with_gains:
        gain_arrived, gain_total = rest.pop(0), rest.pop(0)
        gain_send, gain_recv = rest.pop(0), rest.pop(0)
    send, recv = rest

    def held_at(part, phase, index):
        order = scatter_order(pieces[part])
        left = sorted(set(range(4)) - set(order[:phase]))
        lead = tuple(index if a == order[phase] else slice(None) for a in left)
        if phase == 0:
            return grads[pieces[part].array].at[lead + pieces[part].at]
        return totals[part][phase - 1].at[lead]

    def copy(part, phase, step):
        axis = scatter_order(pieces[part])[phase]
        target = moved(me, sizes, axis, step)
        return pltpu.make_async_remote_copy(
            src_ref=held_at(part, phase, target[axis]),
            dst_ref=arrived[part][phase].at[step - 1],
            send_sem=send.at[part, phase, step],
            recv_sem=recv.at[part, phase, step],
            device_id=device_at(target),
            device_id_type=MESH,
        )

    def add(part, phase):
        piece = pieces[part]
        axis = scatter_order(piece)[phase]
        mine = held_at(part, phase, me[axis])
        lead = mine.shape[:-2]
        others = arrived[part][phase]

        def total_at(place):
            if phase < 3 and sizes[axis] == 2:
                return mine[place] + others[(0,) + place]
            value = mine[place].astype(jnp.float32)
            for step in range(1, sizes[axis]):
                value = value + others[(step - 1,) + place].astype(jnp.float32)
            return value

        if phase == 3:
            outs[piece.array][piece.at] = total_at((slice(None), slice(None)))
            return
        target = totals[part][phase]

        def body(flat, carry):
            place = []
            for size in reversed(lead):
                place.insert(0, lax.rem(flat, size))
                flat = flat // size
            place = tuple(place) + (slice(None), slice(None))
            target[place] = total_at(place).astype(target.dtype)
            return carry

        lax.fori_loop(0, math.prod(lead), body, 0)

    def gain_copy(phase, step):
        return pltpu.make_async_remote_copy(
            src_ref=gain_total.at[phase],
            dst_ref=gain_arrived.at[phase, step - 1],
            send_sem=gain_send.at[phase, step],
            recv_sem=gain_recv.at[phase, step],
            device_id=device_at(moved(me, sizes, phase, step)),
            device_id_type=MESH,
        )

    def start(phase, part):
        for step in range(1, sizes[scatter_order(pieces[part])[phase]]):
            copy(part, phase, step).start()

    def gain_start(phase):
        for step in range(1, sizes[phase]):
            gain_copy(phase, step).start()

    def gain_turn(phase):
        value = gain_total[phase]
        for step in range(1, sizes[phase]):
            gain_copy(phase, step).wait_recv()
        slots = [value] + [gain_arrived[phase, s - 1] for s in range(1, sizes[phase])]
        value = sum(slots[1:], slots[0])
        if phase < 3:
            gain_total[phase + 1] = value
            gain_start(phase + 1)
        else:
            outs[arrays][...] = value

    for part in range(parts):
        start(0, part)
    if with_gains:
        gain_total[0] = grads[arrays][...]
        gain_start(0)
    yield
    turns = [(phase, part) for phase in range(4) for part in range(parts + with_gains)]

    def rank(turn):
        phase, part = turn
        return (0, part, 0) if phase == 0 else (1, phase + part, -phase)

    for phase, part in sorted(turns, key=rank):
        if part == parts:
            gain_turn(phase)
            continue
        for step in range(1, sizes[scatter_order(pieces[part])[phase]]):
            copy(part, phase, step).wait_recv()
        add(part, phase)
        if phase < 3:
            start(phase + 1, part)
        yield
    for phase in range(4):
        for part in range(parts):
            for step in range(1, sizes[scatter_order(pieces[part])[phase]]):
                copy(part, phase, step).wait_send()
        if with_gains:
            for step in range(1, sizes[phase]):
                gain_copy(phase, step).wait_send()


def scatter_buffers(pieces, sizes):
    scratch = []
    for piece in pieces:
        left = [0, 1, 2, 3]
        for axis in scatter_order(piece):
            left.remove(axis)
            shape = (sizes[axis] - 1,) + tuple(sizes[a] for a in left) + (piece.rows, piece.columns)
            scratch.append(pltpu.VMEM(shape, jnp.bfloat16))
    for piece in pieces:
        left = [0, 1, 2, 3]
        for axis in scatter_order(piece)[:3]:
            left.remove(axis)
            shape = tuple(sizes[a] for a in left) + (piece.rows, piece.columns)
            scratch.append(pltpu.VMEM(shape, jnp.bfloat16))
    return scratch


def reduce_scatter(grads, gains, sizes, ident):
    arrays = len(grads)
    most = max(sizes)
    pieces = pieces_of(grads, [(ALONG_Y_LAST, ACROSS_LAST)] * arrays, [True] * arrays)
    scratch = scatter_buffers(pieces, sizes)
    outs = [jax.ShapeDtypeStruct(g.shape[4:], jnp.float32) for g in grads]
    args = list(grads)
    if gains is not None:
        args.append(gains)
        outs.append(jax.ShapeDtypeStruct(gains.shape, jnp.float32))
        scratch += [
            pltpu.VMEM((4, most - 1) + gains.shape, jnp.float32),
            pltpu.VMEM((4,) + gains.shape, jnp.float32),
            pltpu.SemaphoreType.DMA((4, most)),
            pltpu.SemaphoreType.DMA((4, most)),
        ]
    scratch += [pltpu.SemaphoreType.DMA((len(pieces), 4, most))] * 2
    return pl.pallas_call(
        functools.partial(scatter_kernel, sizes, pieces, arrays, int(gains is not None)),
        out_shape=outs,
        in_specs=[pl.BlockSpec(memory_space=pltpu.VMEM)] * len(args),
        out_specs=[pl.BlockSpec(memory_space=pltpu.VMEM)] * len(outs),
        scratch_shapes=scratch,
        compiler_params=pltpu.CompilerParams(
            collective_id=ident, has_side_effects=True, vmem_limit_bytes=VMEM_LIMIT
        ),
        cost_estimate=pl.CostEstimate(flops=0, bytes_accessed=60_000_000, transcendentals=0),
    )(*args)


def padded_rows(count):
    return -(-count // 2048) * 16


def whole_rows(size, width):
    return size % (16 * width) == 0


def pack(flat, lead, width=None):
    size = flat.shape[-1]
    if width and whole_rows(size, width):
        return flat.reshape(lead + (-1, width))
    rows = padded_rows(size)
    none = [(0, 0)] * len(lead)
    if size % 128 == 0:
        flat = flat.reshape(lead + (size // 128, 128))
        return jnp.pad(flat, none + [(0, rows - size // 128), (0, 0)])
    return jnp.pad(flat, none + [(0, rows * 128 - size)]).reshape(lead + (rows, 128))


def unpack(packed, lead, size, width=None):
    if width and whole_rows(size, width):
        return packed.reshape(lead + (size,))
    if size % 128 == 0:
        return packed[..., : size // 128, :].reshape(lead + (size,))
    return packed.reshape(lead + (-1,))[..., :size]


def dot_rows(left, right):
    return lax.dot_general(left, right, (((1,), (1,)), ((), ())), preferred_element_type=jnp.float32)


def dot_columns(left, right):
    return lax.dot_general(left, right, (((0,), (0,)), ((), ())), preferred_element_type=jnp.float32)


def head_columns(head):
    first = head * HEAD_SIZE
    second = first + KEY_VALUE_HEADS * HEAD_SIZE
    return slice(first, first + HEAD_SIZE), slice(second, second + HEAD_SIZE)


def head_columns(head):
    first = head * HEAD_SIZE
    second = first + KEY_VALUE_HEADS * HEAD_SIZE
    return slice(first, first + HEAD_SIZE), slice(second, second + HEAD_SIZE)


def blocks_of(offset, window, tile, tiles):
    return (tile if offset == window else 0), (tile + 1 if offset == 0 else tiles)


def neighbour(me, sizes, axis, step):
    return device_at(moved(me, sizes, axis, step))


class PairFlow:
    def __init__(self, me, sizes, mine, slots, chain_send, cross_send, recv):
        self.me, self.sizes, self.mine, self.slots = me, sizes, mine, slots
        self.chain_send, self.cross_send, self.recv = chain_send, cross_send, recv
        self.reach = sizes[0] // 2

    def chain(self, j):
        return pltpu.make_async_remote_copy(
            src_ref=self.mine if j == 0 else self.slots.at[2 * j],
            dst_ref=self.slots.at[2 * j + 2],
            send_sem=self.chain_send.at[j],
            recv_sem=self.recv.at[2 * j + 2],
            device_id=neighbour(self.me, self.sizes, 0, 1),
            device_id_type=MESH,
        )

    def cross(self, j, side):
        slot = 2 * j + 1 if side == 0 else 2 * j - 1
        return pltpu.make_async_remote_copy(
            src_ref=self.mine if j == 0 else self.slots.at[2 * j],
            dst_ref=self.slots.at[slot],
            send_sem=self.cross_send.at[j],
            recv_sem=self.recv.at[slot],
            device_id=neighbour(self.me, self.sizes, 1, 1),
            device_id_type=MESH,
        )

    def each(self, j, act):
        there = self.me[0] >= j
        if j < self.reach:

            @pl.when(there & (self.me[0] + 1 < self.sizes[0]))
            def _():
                act(self.chain(j))

            @pl.when(there & (self.me[1] == 0))
            def _():
                act(self.cross(j, 0))

        if j > 0:

            @pl.when(there & (self.me[1] == 1))
            def _():
                act(self.cross(j, 1))

    def forward(self, j):
        self.each(j, lambda copy: copy.start())

    def finish(self, j):
        self.each(j, lambda copy: copy.wait_send())

    def arrive(self, offset):
        block = self.slots.at[offset]
        pltpu.make_async_remote_copy(
            src_ref=block,
            dst_ref=block,
            send_sem=self.cross_send.at[0],
            recv_sem=self.recv.at[offset],
            device_id=neighbour(self.me, self.sizes, 1, 1),
            device_id_type=MESH,
        ).wait_recv()


def gather_attend_kernel(sizes, pieces, parts, tiles, *refs):
    shards, refs = refs[:parts], refs[parts:]
    (q_ref, mine_ref, index_ref, start_ref), refs = refs[:4], refs[4:]
    outs, refs = refs[:parts], refs[parts:]
    slots, o_ref, lse_ref, total_ref = refs[:4]
    semaphores, (chain_send, cross_send, recv, own_sem) = refs[4:9], refs[9:]
    me = coords()
    place = me[0] * 2 + me[1]
    window = sizes[0]
    greet(me, sizes)
    flow = PairFlow(me, sizes, mine_ref, slots, chain_send, cross_send, recv)
    flow.forward(0)
    own = pltpu.make_async_copy(mine_ref, slots.at[0], own_sem)
    own.start()
    weights = gather_steps(me, sizes, pieces, shards, outs, *semaphores)
    next(weights)
    token_rows = tiles * BLK

    def unit(offset, tile, head):
        key_part, value_part = head_columns(head)
        low, high = blocks_of(offset, window, tile, tiles)
        q = q_ref[head, tile]
        index, start = index_ref[tile], start_ref[tile]
        width = q.shape[0]
        held = mine_ref if offset == 0 else slots.at[offset]
        base = (place - offset) * token_rows

        def step(block, carry):
            highest, total, acc = carry
            first = pl.multiple_of(block * BLK, BLK)
            rows = pl.ds(first, BLK)
            s = dot_rows(held[rows, key_part], q)
            row = base + first + lax.broadcasted_iota(jnp.int32, s.shape, 0)
            s = jnp.where((row <= index) & (row >= start), s, MASKED)
            new = jnp.maximum(highest, jnp.max(s, axis=0, keepdims=True))
            p = jnp.exp(s - new)
            fade = jnp.exp(highest - new)
            total = total * fade + jnp.sum(p, axis=0, keepdims=True)
            acc = acc * fade + dot_columns(held[rows, value_part], p.astype(jnp.bfloat16))
            return new, total, acc

        if offset == 0:
            carry = (
                jnp.full((1, width), MASKED, jnp.float32),
                jnp.zeros((1, width), jnp.float32),
                jnp.zeros((HEAD_SIZE, width), jnp.float32),
            )
        else:
            carry = lse_ref[head, tile], total_ref[head, tile], o_ref[head, tile]
        highest, total, acc = lax.fori_loop(low, high, step, carry)
        lse_ref[head, tile], total_ref[head, tile], o_ref[head, tile] = highest, total, acc

    slot = 0

    def attend(offset, tile):
        nonlocal slot

        @pl.when(place >= offset)
        def _():
            for head in range(KEY_VALUE_HEADS):
                unit(offset, tile, head)

        for _ in range(GATHER_ROUNDS[slot] if slot < len(GATHER_ROUNDS) else 0):
            next(weights)
        slot += 1

    def receive(offset):
        @pl.when(place >= offset)
        def _():
            flow.arrive(offset)

        if offset % 2 == 0:
            flow.forward(offset // 2)

    for j in range(flow.reach + 1):
        for offset in (0,) if j == 0 else (2 * j, 2 * j - 1):
            if offset % 2:
                receive(offset)
            for tile in range(tiles):
                if tile == tiles - 1 and offset % 2 and j < flow.reach:
                    receive(2 * j + 2)
                attend(offset, tile)
        if j == 0:
            receive(2)
    for tile, head in [(t, h) for t in range(tiles) for h in range(KEY_VALUE_HEADS)]:
        total = total_ref[head, tile]
        o_ref[head, tile] = o_ref[head, tile] / total
        lse_ref[head, tile] = lse_ref[head, tile] + jnp.log(total)
    for _ in weights:
        pass
    for j in range(flow.reach + 1):
        flow.finish(j)
    own.wait()


def gather_attend(shards, query, pairs_mine, index_rows, start_rows, sizes, ident):
    parts = len(shards)
    pieces = pieces_of(shards, [(ALONG_Y_LAST,)] * parts, [False, False, True])
    kvh, tiles, width, _ = query.shape
    window = sizes[0]
    f32 = jnp.float32
    whole = pl.BlockSpec(memory_space=pltpu.VMEM)
    column = jax.ShapeDtypeStruct((kvh, tiles, HEAD_SIZE, width), f32)
    line = jax.ShapeDtypeStruct((kvh, tiles, 1, width), f32)
    out_shape = [jax.ShapeDtypeStruct(sizes + s.shape, s.dtype) for s in shards]
    out_shape += [
        jax.ShapeDtypeStruct((window + 1,) + pairs_mine.shape, pairs_mine.dtype),
        column,
        line,
    ]
    dma = pltpu.SemaphoreType.DMA
    results = pl.pallas_call(
        functools.partial(gather_attend_kernel, sizes, pieces, parts, tiles),
        out_shape=out_shape,
        in_specs=[whole] * (parts + 4),
        out_specs=[whole] * len(out_shape),
        scratch_shapes=[pltpu.VMEM(line.shape, f32)]
        + gather_semaphores(parts, len(pieces), max(sizes))
        + [dma((window // 2 + 1,)), dma((window // 2 + 1,)), dma((window + 1,)), dma],
        compiler_params=pltpu.CompilerParams(
            collective_id=ident, has_side_effects=True, vmem_limit_bytes=VMEM_LIMIT
        ),
        cost_estimate=pl.CostEstimate(
            flops=10_000_000_000, bytes_accessed=60_000_000, transcendentals=0
        ),
    )(*shards, query, pairs_mine, index_rows, start_rows)
    return results[:parts], *results[parts:]


class SumFlow:
    def __init__(self, me, sizes, partial, crossed, chained, chain_send, cross_send, chain_recv, cross_recv):
        self.me, self.sizes, self.partial = me, sizes, partial
        self.crossed, self.chained = crossed, chained
        self.chain_send, self.cross_send = chain_send, cross_send
        self.chain_recv, self.cross_recv = chain_recv, cross_recv
        self.reach = sizes[0] // 2

    def chain(self, j):
        return pltpu.make_async_remote_copy(
            src_ref=self.partial.at[2 * j],
            dst_ref=self.chained.at[j - 1],
            send_sem=self.chain_send.at[j],
            recv_sem=self.chain_recv.at[j - 1],
            device_id=neighbour(self.me, self.sizes, 0, -1),
            device_id_type=MESH,
        )

    def cross(self, offset, side):
        j = (offset + 1) // 2 if side == 0 else offset // 2
        return pltpu.make_async_remote_copy(
            src_ref=self.partial.at[offset],
            dst_ref=self.crossed.at[j],
            send_sem=self.cross_send.at[offset // 2],
            recv_sem=self.cross_recv.at[j],
            device_id=neighbour(self.me, self.sizes, 1, 1),
            device_id_type=MESH,
        )

    def each_cross(self, offset, act):
        for side in range(2):

            @pl.when((self.me[1] == side) & (self.me[0] * 2 + side >= offset))
            def _(side=side):
                act(self.cross(offset, side))

    def has_cross(self, j):
        side = self.me[1]
        if j == 0:
            return side == 0
        if j == self.reach:
            return (side == 1) & (self.me[0] >= j)
        return self.me[0] >= j

    def has_chain(self, j):
        return (self.me[0] >= j) & (self.me[0] + 1 < self.sizes[0])

    def cross_arrive(self, j):
        pltpu.make_async_remote_copy(
            src_ref=self.crossed.at[j],
            dst_ref=self.crossed.at[j],
            send_sem=self.cross_send.at[0],
            recv_sem=self.cross_recv.at[j],
            device_id=neighbour(self.me, self.sizes, 1, 1),
            device_id_type=MESH,
        ).wait_recv()

    def chain_arrive(self, j):
        pltpu.make_async_remote_copy(
            src_ref=self.chained.at[j],
            dst_ref=self.chained.at[j],
            send_sem=self.chain_send.at[0],
            recv_sem=self.chain_recv.at[j],
            device_id=neighbour(self.me, self.sizes, 0, -1),
            device_id_type=MESH,
        ).wait_recv()


def scatter_attend_kernel(sizes, pieces, parts, tiles, *refs):
    grads, refs = refs[:parts], refs[parts:]
    (q_ref, do_ref, slots, index_ref, start_ref, lse_ref, delta_ref), refs = refs[:7], refs[7:]
    outs, refs = refs[:parts], refs[parts:]
    (dq_ref, dkv_ref), refs = refs[:2], refs[2:]
    accs, refs = refs[: 2 * KEY_VALUE_HEADS], refs[2 * KEY_VALUE_HEADS :]
    flow_refs, scatter_refs = refs[:7], refs[7:]
    me = coords()
    place = me[0] * 2 + me[1]
    window = sizes[0]
    greet(me, sizes)
    flow = SumFlow(me, sizes, *flow_refs)
    partial, crossed, chained = flow_refs[:3]
    weights = scatter_steps(me, sizes, pieces, parts, 0, *grads, *outs, *scatter_refs)
    next(weights)
    token_rows = tiles * BLK
    dq_ref[...] = jnp.zeros_like(dq_ref)

    def unit(offset, tile, head):
        key_part, value_part = head_columns(head)
        low, high = blocks_of(offset, window, tile, tiles)
        q, do = q_ref[head, tile], do_ref[head, tile]
        index, start = index_ref[tile], start_ref[tile]
        lse, delta = lse_ref[head, tile], delta_ref[head, tile]
        dk_acc, dv_acc = accs[head], accs[KEY_VALUE_HEADS + head]
        base = (place - offset) * token_rows

        def step(block, dq):
            first = pl.multiple_of(block * BLK, BLK)
            rows = pl.ds(first, BLK)
            k = slots[offset, rows, key_part]
            s = dot_rows(k, q)
            dp = dot_rows(slots[offset, rows, value_part], do)
            row = base + first + lax.broadcasted_iota(jnp.int32, s.shape, 0)
            s = jnp.where((row <= index) & (row >= start), s - lse, MASKED)
            p = jnp.exp(s)
            ds = (p * (dp - delta)).astype(jnp.bfloat16)
            dv_acc[rows, :] += jnp.dot(p.astype(jnp.bfloat16), do, preferred_element_type=jnp.float32)
            dk_acc[rows, :] += jnp.dot(ds, q, preferred_element_type=jnp.float32)
            return dq + dot_columns(k, ds)

        dq_ref[head, tile] = lax.fori_loop(low, high, step, dq_ref[head, tile])

    slot = 0

    def collect(offset):
        nonlocal slot

        for tile in range(tiles):

            @pl.when(place >= offset)
            def _(tile=tile):
                if tile == 0:
                    for acc in accs:
                        acc[...] = jnp.zeros_like(acc)
                for head in range(KEY_VALUE_HEADS):
                    unit(offset, tile, head)

            if tile < tiles - 1:
                progress()

    def progress():
        nonlocal slot
        for _ in range(SCATTER_ROUNDS[slot] if slot < len(SCATTER_ROUNDS) else 0):
            next(weights)
        slot += 1

    def summed(rows):
        return jnp.concatenate([acc[rows, :] for acc in accs], axis=1)

    def over_rows(body):
        def run(block, carry):
            body(pl.ds(pl.multiple_of(block * BLK, BLK), BLK))
            return carry

        lax.fori_loop(0, tiles, run, 0)

    def keep(offset):
        def body(rows):
            partial[offset, rows, :] = summed(rows).astype(partial.dtype)

        over_rows(body)

    def fold(j, source):
        def body(rows):
            partial[2 * j, rows, :] = (
                partial[2 * j, rows, :].astype(jnp.float32) + source[j, rows, :].astype(jnp.float32)
            ).astype(partial.dtype)

        over_rows(body)

    def fold_own(source):
        def body(rows):
            dkv_ref[rows, :] += source[0, rows, :].astype(jnp.float32)

        over_rows(body)

    for j in reversed(range(1, flow.reach + 1)):
        odd = 2 * j - 1

        collect(odd)

        @pl.when(place >= odd)
        def _(odd=odd):
            keep(odd)

        flow.each_cross(odd, lambda copy: copy.start())
        progress()
        collect(2 * j)

        @pl.when(me[0] >= j)
        def _(j=j):
            keep(2 * j)

        @pl.when(flow.has_cross(j))
        def _(j=j):
            flow.cross_arrive(j)
            fold(j, crossed)

        if j < flow.reach:

            @pl.when(flow.has_chain(j))
            def _(j=j):
                flow.chain_arrive(j)
                fold(j, chained)

        @pl.when(me[0] >= j)
        def _(j=j):
            flow.chain(j).start()

        progress()
    collect(0)

    def first(rows):
        dkv_ref[rows, :] = summed(rows)

    over_rows(first)
    progress()

    @pl.when(flow.has_cross(0))
    def _():
        flow.cross_arrive(0)
        fold_own(crossed)

    @pl.when(flow.has_chain(0))
    def _():
        flow.chain_arrive(0)
        fold_own(chained)

    for _ in weights:
        pass
    for j in range(1, flow.reach + 1):
        flow.each_cross(2 * j - 1, lambda copy: copy.wait_send())

        @pl.when(me[0] >= j)
        def _(j=j):
            flow.chain(j).wait_send()


def scatter_attend(grads, arrays, sizes, ident):
    parts = len(grads)
    pieces = pieces_of(grads, [(ALONG_Y_LAST,)] * parts, [True, False, False])
    kvh, tiles, width, _ = arrays[0].shape
    window, reach = sizes[0], sizes[0] // 2
    pair_shape = arrays[2].shape[1:]
    f32 = jnp.float32
    whole = pl.BlockSpec(memory_space=pltpu.VMEM)
    out_shape = [jax.ShapeDtypeStruct(g.shape[4:], f32) for g in grads]
    out_shape += [
        jax.ShapeDtypeStruct((kvh, tiles, HEAD_SIZE, width), f32),
        jax.ShapeDtypeStruct(pair_shape, f32),
    ]
    dma = pltpu.SemaphoreType.DMA
    scratch = [pltpu.VMEM((pair_shape[0], HEAD_SIZE), f32)] * (2 * kvh)
    scratch += [
        pltpu.VMEM((window + 1,) + pair_shape, jnp.bfloat16),
        pltpu.VMEM((reach + 1,) + pair_shape, jnp.bfloat16),
        pltpu.VMEM((reach,) + pair_shape, jnp.bfloat16),
        dma((reach + 1,)),
        dma((reach + 1,)),
        dma((reach,)),
        dma((reach + 1,)),
    ]
    scratch += scatter_buffers(pieces, sizes) + [dma((len(pieces), 4, max(sizes)))] * 2
    results = pl.pallas_call(
        functools.partial(scatter_attend_kernel, sizes, pieces, parts, tiles),
        out_shape=out_shape,
        in_specs=[whole] * (parts + len(arrays)),
        out_specs=[whole] * len(out_shape),
        scratch_shapes=scratch,
        compiler_params=pltpu.CompilerParams(
            collective_id=ident, has_side_effects=True, vmem_limit_bytes=VMEM_LIMIT
        ),
        cost_estimate=pl.CostEstimate(
            flops=25_000_000_000, bytes_accessed=60_000_000, transcendentals=0
        ),
    )(*grads, *arrays)
    return results[:parts], *results[parts:]


def per_device(sizes, layer_input, w_qkv, w_out, w_gu, w_down, norm_gains, lengths, cotangent):
    token_rows = layer_input.shape[0]
    query_width = QUERY_HEADS * HEAD_SIZE
    key_width = KEY_VALUE_HEADS * HEAD_SIZE
    scale = 1.0 / math.sqrt(HEAD_SIZE)
    tiles = token_rows // BLK
    kvh = KEY_VALUE_HEADS

    (qkv_all,) = all_gather([pack(w_qkv, ())], sizes, 0)
    mixing_in = unpack(qkv_all, sizes, w_qkv.shape[0]).reshape(D, -1)

    query_index = lax.axis_index("seq") * token_rows + jnp.arange(token_rows, dtype=jnp.int32)
    start = layout(lengths[0], query_index)
    half = HEAD_SIZE // 2
    freq = jnp.exp(jnp.arange(half, dtype=jnp.float32) * (-2.0 * math.log(THETA) / HEAD_SIZE))
    angle = (query_index - start).astype(jnp.float32)[:, None] * freq[None, :]
    cosine, sine = jnp.cos(angle)[:, None, :], jnp.sin(angle)[:, None, :]

    def rotated(rows, sign):
        first, second = rows[..., :half], rows[..., half:]
        turn = sign * sine
        return jnp.concatenate(
            [first * cosine - second * turn, second * cosine + first * turn], axis=-1
        )

    inputs = layer_input.astype(jnp.float32)
    normed, norm_back = jax.vjp(rms_norm, inputs, norm_gains[0])
    normed_low = normed.astype(jnp.bfloat16)
    projected = jnp.dot(normed_low, mixing_in, preferred_element_type=jnp.float32)
    heads = projected[:, : query_width + key_width].reshape(token_rows, -1, HEAD_SIZE)
    turned = rotated(heads, 1.0).astype(jnp.bfloat16)
    pairs_mine = jnp.concatenate(
        [
            turned[:, QUERY_HEADS:].reshape(token_rows, key_width),
            projected[:, query_width + key_width :].astype(jnp.bfloat16),
        ],
        axis=1,
    )
    def stacked(rows):
        return (
            rows.reshape(tiles, BLK, kvh, HG, HEAD_SIZE)
            .transpose(2, 0, 3, 1, 4)
            .reshape(kvh, tiles, HG * BLK, HEAD_SIZE)
        )

    def unstacked(columns):
        return (
            columns.reshape(kvh, tiles, HEAD_SIZE, HG, BLK)
            .transpose(1, 4, 0, 3, 2)
            .reshape(token_rows, QUERY_HEADS, HEAD_SIZE)
        )

    def row_vector(values):
        return jnp.tile(values.reshape(tiles, 1, BLK), (1, 1, HG))

    query = stacked(turned[:, :QUERY_HEADS] * jnp.bfloat16(scale))
    index_rows, start_rows = row_vector(query_index), row_vector(start)

    width = HG * BLK
    f32 = jnp.float32
    gathered, pairs, attended_t, lse = gather_attend(
        [pack(w_out, ()), pack(w_down, (), D), pack(w_gu, ())],
        query,
        pairs_mine,
        index_rows,
        start_rows,
        sizes,
        1,
    )
    expand_matrix = unpack(gathered[2], sizes, w_gu.shape[0]).reshape(D, 2 * FF)
    if whole_rows(w_down.shape[0], D):
        shrink_matrix = gathered[1].reshape(FF, D)
    else:
        shrink_matrix = unpack(gathered[1], sizes, w_down.shape[0]).reshape(FF, D)
    mixing_out = unpack(gathered[0], sizes, w_out.shape[0]).reshape(query_width, D)
    attended_rows = unstacked(attended_t)
    attended_low = attended_rows.reshape(token_rows, query_width).astype(jnp.bfloat16)
    mid = inputs + jnp.dot(attended_low, mixing_out, preferred_element_type=f32)
    normed_two, norm_two_back = jax.vjp(rms_norm, mid, norm_gains[1])
    normed_two_low = normed_two.astype(jnp.bfloat16)
    gate_up = jnp.dot(normed_two_low, expand_matrix, preferred_element_type=f32)
    hidden, hidden_back = jax.vjp(silu_product, gate_up)
    hidden_low = hidden.astype(jnp.bfloat16)
    result = (mid + jnp.dot(hidden_low, shrink_matrix, preferred_element_type=f32)).astype(
        jnp.bfloat16
    )
    grad_down = jnp.einsum("tf,td->fd", hidden_low, cotangent, preferred_element_type=f32)
    d_hidden = jnp.einsum("td,fd->tf", cotangent, shrink_matrix, preferred_element_type=f32)
    d_gate_up = hidden_back(d_hidden)[0].astype(jnp.bfloat16)
    grad_expand = jnp.einsum("td,tf->df", normed_two_low, d_gate_up, preferred_element_type=f32)
    d_normed_two = jnp.einsum("tf,df->td", d_gate_up, expand_matrix, preferred_element_type=f32)
    d_mid_part, grad_gain_two = norm_two_back(d_normed_two)
    d_mid = cotangent.astype(f32) + d_mid_part
    d_branch = d_mid.astype(jnp.bfloat16)
    grad_mixing_out = jnp.einsum("tq,td->qd", attended_low, d_branch, preferred_element_type=f32)
    d_attended = jnp.einsum("td,qd->tq", d_branch, mixing_out, preferred_element_type=f32).astype(
        jnp.bfloat16
    )
    delta = jnp.sum(
        d_attended.reshape(token_rows, QUERY_HEADS, HEAD_SIZE).astype(f32) * attended_rows, axis=-1
    )
    delta_rows = (
        delta.reshape(tiles, BLK, kvh, HG).transpose(2, 0, 3, 1).reshape(kvh, tiles, 1, width)
    )
    def by_owner(grad):
        return grad.astype(jnp.bfloat16).reshape(sizes + (-1,))

    if whole_rows(w_down.shape[0], D):
        down_sent = grad_down.astype(jnp.bfloat16).reshape(sizes + (-1, D))
    else:
        down_sent = pack(by_owner(grad_down), sizes)
    (gu_mine, down_mine, out_mine), d_query_t, d_pairs_mine = scatter_attend(
        [pack(by_owner(grad_expand), sizes), down_sent, pack(by_owner(grad_mixing_out), sizes)],
        [query, stacked(d_attended), pairs, index_rows, start_rows, lse, delta_rows],
        sizes,
        2,
    )
    d_query = unstacked(d_query_t) * scale
    d_turned = jnp.concatenate(
        [d_query, d_pairs_mine[:, :key_width].reshape(token_rows, kvh, HEAD_SIZE)], axis=1
    )
    d_projected = jnp.concatenate(
        [rotated(d_turned, -1.0).reshape(token_rows, -1), d_pairs_mine[:, key_width:]], axis=1
    ).astype(jnp.bfloat16)
    grad_mixing_in = jnp.einsum("td,tq->dq", normed_low, d_projected, preferred_element_type=f32)
    d_normed = jnp.einsum("tq,dq->td", d_projected, mixing_in, preferred_element_type=f32)
    d_input_part, grad_gain_one = norm_back(d_normed)
    gains = jnp.stack([grad_gain_one, grad_gain_two])
    qkv_mine, gains_sum = reduce_scatter(
        [pack(by_owner(grad_mixing_in), sizes)], gains, sizes, 3
    )
    return (
        result,
        d_mid + d_input_part,
        unpack(qkv_mine, (), w_qkv.shape[0]),
        unpack(out_mine, (), w_out.shape[0]),
        unpack(gu_mine, (), w_gu.shape[0]),
        unpack(down_mine, (), w_down.shape[0], D),
        gains_sum,
    )


def solution(mesh):
    spread = P(("seq", "dp"))
    rows = P(("seq", "dp"), None)
    return jax.shard_map(
        functools.partial(per_device, grid_sizes(mesh.shape["seq"], mesh.shape["dp"])),
        mesh=mesh,
        in_specs=(rows, spread, spread, spread, spread, P(), P("dp", None), rows),
        out_specs=(rows, rows, spread, spread, spread, spread, P()),
        check_vma=False,
    )
```

```python
import functools
import math

import jax
import jax.numpy as jnp
from jax import lax
from jax.experimental import pallas as pl
from jax.experimental.pallas import tpu as pltpu
from jax.sharding import PartitionSpec as P

D = 576
QUERY_HEADS = 9
KEY_VALUE_HEADS = 3
HEAD_SIZE = 64
FF = 1536
HG = QUERY_HEADS // KEY_VALUE_HEADS

EPS = 1e-05
THETA = 100000.0
MASKED = -1e30
MESH = pl.DeviceIdType.MESH
BLK = 256
VMEM_LIMIT = 56 * 1024 * 1024
ACROSS_LAST, ALONG_Y_LAST = (0, 2, 1), (0, 1, 2)
GATHER_ROUNDS = (0, 2, 2, 2, 2, 1, 1, 0, 1)
SCATTER_ROUNDS = (2, 2, 0, 1, 1, 2, 2, 1, 2)


def rms_norm(value_rows, gain):
    return (
        value_rows
        * lax.rsqrt(jnp.mean(value_rows * value_rows, axis=-1, keepdims=True) + EPS)
        * gain
    )


def layout(lengths_row, index):
    count = lengths_row.shape[0]
    earlier = jnp.arange(count)[:, None] >= jnp.arange(count)[None, :]
    ends = jnp.sum(jnp.where(earlier, lengths_row[None, :], 0), axis=1, dtype=jnp.int32)
    done = ends[None, :] <= index[:, None]
    return jnp.sum(jnp.where(done, lengths_row[None, :], 0), axis=1, dtype=jnp.int32)


def silu_product(gate_up):
    width = gate_up.shape[1] // 2
    return jax.nn.silu(gate_up[:, :width]) * gate_up[:, width:]


def grid_sizes(seq_count, dp_count):
    return (seq_count // 2, 2, dp_count // 2, 2)


def coords():
    seq, dp = lax.axis_index("seq"), lax.axis_index("dp")
    return [seq // 2, seq % 2, dp // 2, dp % 2]


def device_at(coord):
    return (coord[0] * 2 + coord[1], coord[2] * 2 + coord[3])


def moved(me, sizes, axis, step):
    other = list(me)
    other[axis] = lax.rem(me[axis] + step + sizes[axis], sizes[axis])
    return other


def greet(me, sizes):
    barrier = pltpu.get_barrier_semaphore()
    count = 0
    for axis in range(4):
        for step in range(1, sizes[axis]):
            pl.semaphore_signal(
                barrier,
                inc=1,
                device_id=device_at(moved(me, sizes, axis, step)),
                device_id_type=MESH,
            )
            count += 1
    pl.semaphore_wait(barrier, count)


class Piece:
    def __init__(self, array, shape, order):
        self.array, self.order = array, order
        self.rows, self.columns = shape[0][1], shape[1][1]
        self.at = tuple(pl.ds(first, size) for first, size in shape)


def pieces_of(shards, orders, cuts):
    pieces = []
    for array, shard in enumerate(shards):
        rows, columns = shard.shape[-2:]
        cut = rows // 32 * 16 if cuts[array] and rows >= 64 else 0
        spans = [(0, cut), (cut, rows - cut)] if cut else [(0, rows)]
        for number, span in enumerate(spans):
            order = orders[array][number % len(orders[array])]
            pieces.append(Piece(array, (span, (0, columns)), order))
    return pieces


def gather_steps(me, sizes, pieces, shards, outs, send, recv, core_send, core_recv, local):
    parts = len(pieces)
    started = []
    for array in range(len(shards)):
        own = pltpu.make_async_copy(
            shards[array], outs[array].at[me[0], me[1], me[2], me[3]], local.at[array]
        )
        own.start()
        started.append(own)

    def region(part, held, where):
        piece = pieces[part]
        lead = tuple(slice(None) if a in held else where[a] for a in range(3)) + (where[3],)
        return outs[piece.array].at[lead + piece.at]

    def copy(part, phase, step, arriving=False):
        order = pieces[part].order
        where = moved(me, sizes, order[phase], -step) if arriving else me
        block = region(part, order[:phase], where)
        source = block
        if phase == 0 and not arriving:
            source = shards[pieces[part].array].at[pieces[part].at]
        return pltpu.make_async_remote_copy(
            src_ref=source,
            dst_ref=block,
            send_sem=send.at[part, phase, step],
            recv_sem=recv.at[part, phase, step],
            device_id=device_at(moved(me, sizes, order[phase], step)),
            device_id_type=MESH,
        )

    def to_core(part, slot, held, where, arriving=False):
        there = moved(where, sizes, 3, 1) if arriving else where
        block = region(part, held, there)
        return pltpu.make_async_remote_copy(
            src_ref=block,
            dst_ref=block,
            send_sem=core_send.at[part, slot],
            recv_sem=core_recv.at[part, slot],
            device_id=device_at(moved(me, sizes, 3, 1)),
            device_id_type=MESH,
        )

    for part in range(parts):
        for step in range(1, sizes[pieces[part].order[0]]):
            copy(part, 0, step).start()
    for own in started:
        own.wait()
    yield
    pending = []
    turns = [(phase, part) for phase in range(3) for part in range(parts)]
    for phase, part in sorted(turns, key=lambda turn: (2 * turn[0] + turn[1], turn[0])):
        order = pieces[part].order
        held = order[:phase]
        for step in range(1, sizes[order[phase]]):
            copy(part, phase, step, arriving=True).wait_recv()
            if phase == 2:
                origin = moved(me, sizes, order[phase], -step)
                to_core(part, step, held, origin).start()
                pending.append((part, step, held, origin))
        if phase < 2:
            for step in range(1, sizes[order[phase + 1]]):
                copy(part, phase + 1, step).start()
        if phase == 1:
            to_core(part, 0, order[:2], me).start()
            pending.append((part, 0, order[:2], me))
        yield
    for part in range(parts):
        for phase in range(3):
            for step in range(1, sizes[pieces[part].order[phase]]):
                copy(part, phase, step).wait_send()
    for part, slot, held, origin in pending:
        to_core(part, slot, held, origin).wait_send()
        to_core(part, slot, held, origin, arriving=True).wait_recv()


def gather_semaphores(arrays, parts, most):
    return [
        pltpu.SemaphoreType.DMA((parts, 3, most)),
        pltpu.SemaphoreType.DMA((parts, 3, most)),
        pltpu.SemaphoreType.DMA((parts, most)),
        pltpu.SemaphoreType.DMA((parts, most)),
        pltpu.SemaphoreType.DMA((arrays,)),
    ]


def gather_kernel(sizes, pieces, arrays, *refs):
    me = coords()
    greet(me, sizes)
    for _ in gather_steps(
        me, sizes, pieces, refs[:arrays], refs[arrays : 2 * arrays], *refs[2 * arrays :]
    ):
        pass


def all_gather(shards, sizes, ident):
    arrays = len(shards)
    pieces = pieces_of(shards, [(ALONG_Y_LAST, ACROSS_LAST)] * arrays, [True] * arrays)
    return pl.pallas_call(
        functools.partial(gather_kernel, sizes, pieces, arrays),
        out_shape=[jax.ShapeDtypeStruct(sizes + s.shape, s.dtype) for s in shards],
        in_specs=[pl.BlockSpec(memory_space=pltpu.VMEM)] * arrays,
        out_specs=[pl.BlockSpec(memory_space=pltpu.VMEM)] * arrays,
        scratch_shapes=gather_semaphores(arrays, len(pieces), max(sizes)),
        compiler_params=pltpu.CompilerParams(
            collective_id=ident, has_side_effects=True, vmem_limit_bytes=VMEM_LIMIT
        ),
        cost_estimate=pl.CostEstimate(flops=0, bytes_accessed=60_000_000, transcendentals=0),
    )(*shards)


def scatter_order(piece):
    return (3,) + tuple(reversed(piece.order))


def scatter_kernel(sizes, pieces, arrays, with_gains, *refs):
    me = coords()
    greet(me, sizes)
    for _ in scatter_steps(me, sizes, pieces, arrays, with_gains, *refs):
        pass


def scatter_steps(me, sizes, pieces, arrays, with_gains, *refs):
    parts = len(pieces)
    n_in = arrays + with_gains
    grads, outs = refs[:n_in], refs[n_in : 2 * n_in]
    rest = list(refs[2 * n_in :])
    arrived = [[rest.pop(0) for _ in range(4)] for _ in range(parts)]
    totals = [[rest.pop(0) for _ in range(3)] for _ in range(parts)]
    if with_gains:
        gain_arrived, gain_total = rest.pop(0), rest.pop(0)
        gain_send, gain_recv = rest.pop(0), rest.pop(0)
    send, recv = rest

    def held_at(part, phase, index):
        order = scatter_order(pieces[part])
        left = sorted(set(range(4)) - set(order[:phase]))
        lead = tuple(index if a == order[phase] else slice(None) for a in left)
        if phase == 0:
            return grads[pieces[part].array].at[lead + pieces[part].at]
        return totals[part][phase - 1].at[lead]

    def copy(part, phase, step):
        axis = scatter_order(pieces[part])[phase]
        target = moved(me, sizes, axis, step)
        return pltpu.make_async_remote_copy(
            src_ref=held_at(part, phase, target[axis]),
            dst_ref=arrived[part][phase].at[step - 1],
            send_sem=send.at[part, phase, step],
            recv_sem=recv.at[part, phase, step],
            device_id=device_at(target),
            device_id_type=MESH,
        )

    def add(part, phase):
        piece = pieces[part]
        axis = scatter_order(piece)[phase]
        mine = held_at(part, phase, me[axis])
        lead = mine.shape[:-2]
        others = arrived[part][phase]

        def total_at(place):
            if phase < 3 and sizes[axis] == 2:
                return mine[place] + others[(0,) + place]
            value = mine[place].astype(jnp.float32)
            for step in range(1, sizes[axis]):
                value = value + others[(step - 1,) + place].astype(jnp.float32)
            return value

        if phase == 3:
            outs[piece.array][piece.at] = total_at((slice(None), slice(None)))
            return
        target = totals[part][phase]

        def body(flat, carry):
            place = []
            for size in reversed(lead):
                place.insert(0, lax.rem(flat, size))
                flat = flat // size
            place = tuple(place) + (slice(None), slice(None))
            target[place] = total_at(place).astype(target.dtype)
            return carry

        lax.fori_loop(0, math.prod(lead), body, 0)

    def gain_copy(phase, step):
        return pltpu.make_async_remote_copy(
            src_ref=gain_total.at[phase],
            dst_ref=gain_arrived.at[phase, step - 1],
            send_sem=gain_send.at[phase, step],
            recv_sem=gain_recv.at[phase, step],
            device_id=device_at(moved(me, sizes, phase, step)),
            device_id_type=MESH,
        )

    def start(phase, part):
        for step in range(1, sizes[scatter_order(pieces[part])[phase]]):
            copy(part, phase, step).start()

    def gain_start(phase):
        for step in range(1, sizes[phase]):
            gain_copy(phase, step).start()

    def gain_turn(phase):
        value = gain_total[phase]
        for step in range(1, sizes[phase]):
            gain_copy(phase, step).wait_recv()
        slots = [value] + [gain_arrived[phase, s - 1] for s in range(1, sizes[phase])]
        value = sum(slots[1:], slots[0])
        if phase < 3:
            gain_total[phase + 1] = value
            gain_start(phase + 1)
        else:
            outs[arrays][...] = value

    for part in range(parts):
        start(0, part)
    if with_gains:
        gain_total[0] = grads[arrays][...]
        gain_start(0)
    yield
    turns = [(phase, part) for phase in range(4) for part in range(parts + with_gains)]

    def rank(turn):
        phase, part = turn
        return (0, part, 0) if phase == 0 else (1, phase + part, -phase)

    for phase, part in sorted(turns, key=rank):
        if part == parts:
            gain_turn(phase)
            continue
        for step in range(1, sizes[scatter_order(pieces[part])[phase]]):
            copy(part, phase, step).wait_recv()
        add(part, phase)
        if phase < 3:
            start(phase + 1, part)
        yield
    for phase in range(4):
        for part in range(parts):
            for step in range(1, sizes[scatter_order(pieces[part])[phase]]):
                copy(part, phase, step).wait_send()
        if with_gains:
            for step in range(1, sizes[phase]):
                gain_copy(phase, step).wait_send()


def scatter_buffers(pieces, sizes):
    scratch = []
    for piece in pieces:
        left = [0, 1, 2, 3]
        for axis in scatter_order(piece):
            left.remove(axis)
            shape = (sizes[axis] - 1,) + tuple(sizes[a] for a in left) + (piece.rows, piece.columns)
            scratch.append(pltpu.VMEM(shape, jnp.bfloat16))
    for piece in pieces:
        left = [0, 1, 2, 3]
        for axis in scatter_order(piece)[:3]:
            left.remove(axis)
            shape = tuple(sizes[a] for a in left) + (piece.rows, piece.columns)
            scratch.append(pltpu.VMEM(shape, jnp.bfloat16))
    return scratch


def reduce_scatter(grads, gains, sizes, ident):
    arrays = len(grads)
    most = max(sizes)
    pieces = pieces_of(grads, [(ALONG_Y_LAST, ACROSS_LAST)] * arrays, [True] * arrays)
    scratch = scatter_buffers(pieces, sizes)
    outs = [jax.ShapeDtypeStruct(g.shape[4:], jnp.float32) for g in grads]
    args = list(grads)
    if gains is not None:
        args.append(gains)
        outs.append(jax.ShapeDtypeStruct(gains.shape, jnp.float32))
        scratch += [
            pltpu.VMEM((4, most - 1) + gains.shape, jnp.float32),
            pltpu.VMEM((4,) + gains.shape, jnp.float32),
            pltpu.SemaphoreType.DMA((4, most)),
            pltpu.SemaphoreType.DMA((4, most)),
        ]
    scratch += [pltpu.SemaphoreType.DMA((len(pieces), 4, most))] * 2
    return pl.pallas_call(
        functools.partial(scatter_kernel, sizes, pieces, arrays, int(gains is not None)),
        out_shape=outs,
        in_specs=[pl.BlockSpec(memory_space=pltpu.VMEM)] * len(args),
        out_specs=[pl.BlockSpec(memory_space=pltpu.VMEM)] * len(outs),
        scratch_shapes=scratch,
        compiler_params=pltpu.CompilerParams(
            collective_id=ident, has_side_effects=True, vmem_limit_bytes=VMEM_LIMIT
        ),
        cost_estimate=pl.CostEstimate(flops=0, bytes_accessed=60_000_000, transcendentals=0),
    )(*args)


def padded_rows(count):
    return -(-count // 2048) * 16


def whole_rows(size, width):
    return size % (16 * width) == 0


def pack(flat, lead, width=None):
    size = flat.shape[-1]
    if width and whole_rows(size, width):
        return flat.reshape(lead + (-1, width))
    rows = padded_rows(size)
    none = [(0, 0)] * len(lead)
    if size % 128 == 0:
        flat = flat.reshape(lead + (size // 128, 128))
        return jnp.pad(flat, none + [(0, rows - size // 128), (0, 0)])
    return jnp.pad(flat, none + [(0, rows * 128 - size)]).reshape(lead + (rows, 128))


def unpack(packed, lead, size, width=None):
    if width and whole_rows(size, width):
        return packed.reshape(lead + (size,))
    if size % 128 == 0:
        return packed[..., : size // 128, :].reshape(lead + (size,))
    return packed.reshape(lead + (-1,))[..., :size]


def dot_rows(left, right):
    return lax.dot_general(left, right, (((1,), (1,)), ((), ())), preferred_element_type=jnp.float32)


def dot_columns(left, right):
    return lax.dot_general(left, right, (((0,), (0,)), ((), ())), preferred_element_type=jnp.float32)


def head_columns(head):
    first = head * HEAD_SIZE
    second = first + KEY_VALUE_HEADS * HEAD_SIZE
    return slice(first, first + HEAD_SIZE), slice(second, second + HEAD_SIZE)


def head_columns(head):
    first = head * HEAD_SIZE
    second = first + KEY_VALUE_HEADS * HEAD_SIZE
    return slice(first, first + HEAD_SIZE), slice(second, second + HEAD_SIZE)


def blocks_of(offset, window, tile, tiles):
    return (tile if offset == window else 0), (tile + 1 if offset == 0 else tiles)


def query_part(head, within):
    first = (head * HG + within) * HEAD_SIZE
    return slice(first, first + HEAD_SIZE)


def stack_heads(rows_ref, stacked_ref, tile):
    for head in range(KEY_VALUE_HEADS):
        for within in range(HG):
            stacked_ref[head, tile, pl.ds(within * BLK, BLK), :] = rows_ref[
                pl.ds(tile * BLK, BLK), query_part(head, within)
            ]


def lay_heads(columns):
    return jnp.concatenate(
        [
            columns[head][:, within * BLK : (within + 1) * BLK].T
            for head in range(KEY_VALUE_HEADS)
            for within in range(HG)
        ],
        axis=1,
    )


def places(place, tile, tiles, start_ref):
    lane = lax.broadcasted_iota(jnp.int32, (1, HG * BLK), 1)
    index = (place * tiles + tile) * BLK + lax.rem(lane, BLK)
    return index, jnp.concatenate([start_ref[tile]] * HG, axis=1)


def neighbour(me, sizes, axis, step):
    return device_at(moved(me, sizes, axis, step))


class PairFlow:
    def __init__(self, me, sizes, mine, slots, chain_send, cross_send, recv):
        self.me, self.sizes, self.mine, self.slots = me, sizes, mine, slots
        self.chain_send, self.cross_send, self.recv = chain_send, cross_send, recv
        self.reach = sizes[0] // 2

    def chain(self, j):
        return pltpu.make_async_remote_copy(
            src_ref=self.mine if j == 0 else self.slots.at[2 * j],
            dst_ref=self.slots.at[2 * j + 2],
            send_sem=self.chain_send.at[j],
            recv_sem=self.recv.at[2 * j + 2],
            device_id=neighbour(self.me, self.sizes, 0, 1),
            device_id_type=MESH,
        )

    def cross(self, j, side):
        slot = 2 * j + 1 if side == 0 else 2 * j - 1
        return pltpu.make_async_remote_copy(
            src_ref=self.mine if j == 0 else self.slots.at[2 * j],
            dst_ref=self.slots.at[slot],
            send_sem=self.cross_send.at[j],
            recv_sem=self.recv.at[slot],
            device_id=neighbour(self.me, self.sizes, 1, 1),
            device_id_type=MESH,
        )

    def each(self, j, act):
        there = self.me[0] >= j
        if j < self.reach:

            @pl.when(there & (self.me[0] + 1 < self.sizes[0]))
            def _():
                act(self.chain(j))

            @pl.when(there & (self.me[1] == 0))
            def _():
                act(self.cross(j, 0))

        if j > 0:

            @pl.when(there & (self.me[1] == 1))
            def _():
                act(self.cross(j, 1))

    def forward(self, j):
        self.each(j, lambda copy: copy.start())

    def finish(self, j):
        self.each(j, lambda copy: copy.wait_send())

    def arrive(self, offset):
        block = self.slots.at[offset]
        pltpu.make_async_remote_copy(
            src_ref=block,
            dst_ref=block,
            send_sem=self.cross_send.at[0],
            recv_sem=self.recv.at[offset],
            device_id=neighbour(self.me, self.sizes, 1, 1),
            device_id_type=MESH,
        ).wait_recv()


def gather_attend_kernel(sizes, pieces, parts, tiles, *refs):
    shards, refs = refs[:parts], refs[parts:]
    (rows_ref, mine_ref, start_ref), refs = refs[:3], refs[3:]
    outs, refs = refs[:parts], refs[parts:]
    slots, o_ref, out_ref, lse_ref, total_ref, q_ref = refs[:6]
    semaphores, (chain_send, cross_send, recv, own_sem) = refs[6:11], refs[11:]
    me = coords()
    place = me[0] * 2 + me[1]
    window = sizes[0]
    greet(me, sizes)
    flow = PairFlow(me, sizes, mine_ref, slots, chain_send, cross_send, recv)
    flow.forward(0)
    own = pltpu.make_async_copy(mine_ref, slots.at[0], own_sem)
    own.start()
    weights = gather_steps(me, sizes, pieces, shards, outs, *semaphores)
    next(weights)
    token_rows = tiles * BLK
    for tile in range(tiles):
        stack_heads(rows_ref, q_ref, tile)

    def unit(offset, tile, head):
        key_part, value_part = head_columns(head)
        low, high = blocks_of(offset, window, tile, tiles)
        q = q_ref[head, tile]
        index, start = places(place, tile, tiles, start_ref)
        width = q.shape[0]
        held = mine_ref if offset == 0 else slots.at[offset]
        base = (place - offset) * token_rows

        def step(block, carry):
            highest, total, acc = carry
            first = pl.multiple_of(block * BLK, BLK)
            rows = pl.ds(first, BLK)
            s = dot_rows(held[rows, key_part], q)
            row = base + first + lax.broadcasted_iota(jnp.int32, s.shape, 0)
            s = jnp.where((row <= index) & (row >= start), s, MASKED)
            new = jnp.maximum(highest, jnp.max(s, axis=0, keepdims=True))
            p = jnp.exp(s - new)
            fade = jnp.exp(highest - new)
            total = total * fade + jnp.sum(p, axis=0, keepdims=True)
            acc = acc * fade + dot_columns(held[rows, value_part], p.astype(jnp.bfloat16))
            return new, total, acc

        if offset == 0:
            carry = (
                jnp.full((1, width), MASKED, jnp.float32),
                jnp.zeros((1, width), jnp.float32),
                jnp.zeros((HEAD_SIZE, width), jnp.float32),
            )
        else:
            carry = lse_ref[head, tile], total_ref[head, tile], o_ref[head, tile]
        highest, total, acc = lax.fori_loop(low, high, step, carry)
        lse_ref[head, tile], total_ref[head, tile], o_ref[head, tile] = highest, total, acc

    slot = 0

    def attend(offset, tile):
        nonlocal slot

        @pl.when(place >= offset)
        def _():
            for head in range(KEY_VALUE_HEADS):
                unit(offset, tile, head)

        for _ in range(GATHER_ROUNDS[slot] if slot < len(GATHER_ROUNDS) else 0):
            next(weights)
        slot += 1

    def receive(offset):
        @pl.when(place >= offset)
        def _():
            flow.arrive(offset)

        if offset % 2 == 0:
            flow.forward(offset // 2)

    for j in range(flow.reach + 1):
        for offset in (0,) if j == 0 else (2 * j, 2 * j - 1):
            if offset % 2:
                receive(offset)
            for tile in range(tiles):
                if tile == tiles - 1 and offset % 2 and j < flow.reach:
                    receive(2 * j + 2)
                attend(offset, tile)
        if j == 0:
            receive(2)
    for tile, head in [(t, h) for t in range(tiles) for h in range(KEY_VALUE_HEADS)]:
        total = total_ref[head, tile]
        o_ref[head, tile] = o_ref[head, tile] / total
        lse_ref[head, tile] = lse_ref[head, tile] + jnp.log(total)
    for tile in range(tiles):
        laid = lay_heads([o_ref[head, tile] for head in range(KEY_VALUE_HEADS)])
        out_ref[pl.ds(tile * BLK, BLK), :] = laid.astype(out_ref.dtype)
    for _ in weights:
        pass
    for j in range(flow.reach + 1):
        flow.finish(j)
    own.wait()


def gather_attend(shards, query, pairs_mine, start_rows, sizes, ident):
    parts = len(shards)
    pieces = pieces_of(shards, [(ALONG_Y_LAST,)] * parts, [False, False, True])
    kvh, tiles, width = KEY_VALUE_HEADS, query.shape[0] // BLK, HG * BLK
    window = sizes[0]
    f32 = jnp.float32
    whole = pl.BlockSpec(memory_space=pltpu.VMEM)
    column = jax.ShapeDtypeStruct((kvh, tiles, HEAD_SIZE, width), f32)
    line = jax.ShapeDtypeStruct((kvh, tiles, 1, width), f32)
    out_shape = [jax.ShapeDtypeStruct(sizes + s.shape, s.dtype) for s in shards]
    out_shape += [
        jax.ShapeDtypeStruct((window + 1,) + pairs_mine.shape, pairs_mine.dtype),
        column,
        jax.ShapeDtypeStruct(query.shape, query.dtype),
        line,
    ]
    dma = pltpu.SemaphoreType.DMA
    results = pl.pallas_call(
        functools.partial(gather_attend_kernel, sizes, pieces, parts, tiles),
        out_shape=out_shape,
        in_specs=[whole] * (parts + 3),
        out_specs=[whole] * len(out_shape),
        scratch_shapes=[
            pltpu.VMEM(line.shape, f32),
            pltpu.VMEM((kvh, tiles, width, HEAD_SIZE), query.dtype),
        ]
        + gather_semaphores(parts, len(pieces), max(sizes))
        + [dma((window // 2 + 1,)), dma((window // 2 + 1,)), dma((window + 1,)), dma],
        compiler_params=pltpu.CompilerParams(
            collective_id=ident, has_side_effects=True, vmem_limit_bytes=VMEM_LIMIT
        ),
        cost_estimate=pl.CostEstimate(
            flops=10_000_000_000, bytes_accessed=60_000_000, transcendentals=0
        ),
    )(*shards, query, pairs_mine, start_rows)
    return results[:parts], *results[parts:]


class SumFlow:
    def __init__(self, me, sizes, partial, crossed, chained, chain_send, cross_send, chain_recv, cross_recv):
        self.me, self.sizes, self.partial = me, sizes, partial
        self.crossed, self.chained = crossed, chained
        self.chain_send, self.cross_send = chain_send, cross_send
        self.chain_recv, self.cross_recv = chain_recv, cross_recv
        self.reach = sizes[0] // 2

    def chain(self, j):
        return pltpu.make_async_remote_copy(
            src_ref=self.partial.at[2 * j],
            dst_ref=self.chained.at[j - 1],
            send_sem=self.chain_send.at[j],
            recv_sem=self.chain_recv.at[j - 1],
            device_id=neighbour(self.me, self.sizes, 0, -1),
            device_id_type=MESH,
        )

    def cross(self, offset, side):
        j = (offset + 1) // 2 if side == 0 else offset // 2
        return pltpu.make_async_remote_copy(
            src_ref=self.partial.at[offset],
            dst_ref=self.crossed.at[j],
            send_sem=self.cross_send.at[offset // 2],
            recv_sem=self.cross_recv.at[j],
            device_id=neighbour(self.me, self.sizes, 1, 1),
            device_id_type=MESH,
        )

    def each_cross(self, offset, act):
        for side in range(2):

            @pl.when((self.me[1] == side) & (self.me[0] * 2 + side >= offset))
            def _(side=side):
                act(self.cross(offset, side))

    def has_cross(self, j):
        side = self.me[1]
        if j == 0:
            return side == 0
        if j == self.reach:
            return (side == 1) & (self.me[0] >= j)
        return self.me[0] >= j

    def has_chain(self, j):
        return (self.me[0] >= j) & (self.me[0] + 1 < self.sizes[0])

    def cross_arrive(self, j):
        pltpu.make_async_remote_copy(
            src_ref=self.crossed.at[j],
            dst_ref=self.crossed.at[j],
            send_sem=self.cross_send.at[0],
            recv_sem=self.cross_recv.at[j],
            device_id=neighbour(self.me, self.sizes, 1, 1),
            device_id_type=MESH,
        ).wait_recv()

    def chain_arrive(self, j):
        pltpu.make_async_remote_copy(
            src_ref=self.chained.at[j],
            dst_ref=self.chained.at[j],
            send_sem=self.chain_send.at[0],
            recv_sem=self.chain_recv.at[j],
            device_id=neighbour(self.me, self.sizes, 0, -1),
            device_id_type=MESH,
        ).wait_recv()


def scatter_attend_kernel(sizes, pieces, parts, tiles, *refs):
    grads, refs = refs[:parts], refs[parts:]
    (rows_ref, do_rows_ref, slots, start_ref, lse_ref, o_ref), refs = refs[:6], refs[6:]
    outs, refs = refs[:parts], refs[parts:]
    (dq_rows_ref, dkv_ref), refs = refs[:2], refs[2:]
    (dq_ref, q_ref, do_ref, delta_ref), refs = refs[:4], refs[4:]
    accs, refs = refs[: 2 * KEY_VALUE_HEADS], refs[2 * KEY_VALUE_HEADS :]
    flow_refs, scatter_refs = refs[:7], refs[7:]
    me = coords()
    place = me[0] * 2 + me[1]
    window = sizes[0]
    greet(me, sizes)
    flow = SumFlow(me, sizes, *flow_refs)
    partial, crossed, chained = flow_refs[:3]
    weights = scatter_steps(me, sizes, pieces, parts, 0, *grads, *outs, *scatter_refs)
    next(weights)
    token_rows = tiles * BLK
    dq_ref[...] = jnp.zeros_like(dq_ref)
    for tile in range(tiles):
        stack_heads(rows_ref, q_ref, tile)
        stack_heads(do_rows_ref, do_ref, tile)
        for head in range(KEY_VALUE_HEADS):
            columns = do_ref[head, tile].astype(jnp.float32).T
            delta_ref[head, tile] = jnp.sum(columns * o_ref[head, tile], axis=0, keepdims=True)

    def unit(offset, tile, head):
        key_part, value_part = head_columns(head)
        low, high = blocks_of(offset, window, tile, tiles)
        q, do = q_ref[head, tile], do_ref[head, tile]
        index, start = places(place, tile, tiles, start_ref)
        lse, delta = lse_ref[head, tile], delta_ref[head, tile]
        dk_acc, dv_acc = accs[head], accs[KEY_VALUE_HEADS + head]
        base = (place - offset) * token_rows

        def step(block, dq):
            first = pl.multiple_of(block * BLK, BLK)
            rows = pl.ds(first, BLK)
            k = slots[offset, rows, key_part]
            s = dot_rows(k, q)
            dp = dot_rows(slots[offset, rows, value_part], do)
            row = base + first + lax.broadcasted_iota(jnp.int32, s.shape, 0)
            s = jnp.where((row <= index) & (row >= start), s - lse, MASKED)
            p = jnp.exp(s)
            ds = (p * (dp - delta)).astype(jnp.bfloat16)
            dv_acc[rows, :] += jnp.dot(p.astype(jnp.bfloat16), do, preferred_element_type=jnp.float32)
            dk_acc[rows, :] += jnp.dot(ds, q, preferred_element_type=jnp.float32)
            return dq + dot_columns(k, ds)

        dq_ref[head, tile] = lax.fori_loop(low, high, step, dq_ref[head, tile])

    slot = 0

    def collect(offset):
        nonlocal slot

        for tile in range(tiles):

            @pl.when(place >= offset)
            def _(tile=tile):
                if tile == 0:
                    for acc in accs:
                        acc[...] = jnp.zeros_like(acc)
                for head in range(KEY_VALUE_HEADS):
                    unit(offset, tile, head)

            if tile < tiles - 1:
                progress()

    def progress():
        nonlocal slot
        for _ in range(SCATTER_ROUNDS[slot] if slot < len(SCATTER_ROUNDS) else 0):
            next(weights)
        slot += 1

    def summed(rows):
        return jnp.concatenate([acc[rows, :] for acc in accs], axis=1)

    def over_rows(body):
        def run(block, carry):
            body(pl.ds(pl.multiple_of(block * BLK, BLK), BLK))
            return carry

        lax.fori_loop(0, tiles, run, 0)

    def keep(offset):
        def body(rows):
            partial[offset, rows, :] = summed(rows).astype(partial.dtype)

        over_rows(body)

    def fold(j, source):
        def body(rows):
            partial[2 * j, rows, :] = (
                partial[2 * j, rows, :].astype(jnp.float32) + source[j, rows, :].astype(jnp.float32)
            ).astype(partial.dtype)

        over_rows(body)

    def fold_own(source):
        def body(rows):
            dkv_ref[rows, :] += source[0, rows, :].astype(jnp.float32)

        over_rows(body)

    for j in reversed(range(1, flow.reach + 1)):
        odd = 2 * j - 1

        collect(odd)

        @pl.when(place >= odd)
        def _(odd=odd):
            keep(odd)

        flow.each_cross(odd, lambda copy: copy.start())
        progress()
        collect(2 * j)

        @pl.when(me[0] >= j)
        def _(j=j):
            keep(2 * j)

        @pl.when(flow.has_cross(j))
        def _(j=j):
            flow.cross_arrive(j)
            fold(j, crossed)

        if j < flow.reach:

            @pl.when(flow.has_chain(j))
            def _(j=j):
                flow.chain_arrive(j)
                fold(j, chained)

        @pl.when(me[0] >= j)
        def _(j=j):
            flow.chain(j).start()

        progress()
    collect(0)

    def first(rows):
        dkv_ref[rows, :] = summed(rows)

    over_rows(first)
    progress()

    for tile in range(tiles):
        laid = lay_heads([dq_ref[head, tile] for head in range(KEY_VALUE_HEADS)])
        dq_rows_ref[pl.ds(tile * BLK, BLK), :] = laid * (1.0 / math.sqrt(HEAD_SIZE))

    @pl.when(flow.has_cross(0))
    def _():
        flow.cross_arrive(0)
        fold_own(crossed)

    @pl.when(flow.has_chain(0))
    def _():
        flow.chain_arrive(0)
        fold_own(chained)

    for _ in weights:
        pass
    for j in range(1, flow.reach + 1):
        flow.each_cross(2 * j - 1, lambda copy: copy.wait_send())

        @pl.when(me[0] >= j)
        def _(j=j):
            flow.chain(j).wait_send()


def scatter_attend(grads, arrays, sizes, ident):
    parts = len(grads)
    pieces = pieces_of(grads, [(ALONG_Y_LAST,)] * parts, [True, False, False])
    token_rows = arrays[0].shape[0]
    kvh, tiles, width = KEY_VALUE_HEADS, token_rows // BLK, HG * BLK
    window, reach = sizes[0], sizes[0] // 2
    pair_shape = arrays[2].shape[1:]
    f32 = jnp.float32
    whole = pl.BlockSpec(memory_space=pltpu.VMEM)
    out_shape = [jax.ShapeDtypeStruct(g.shape[4:], f32) for g in grads]
    out_shape += [
        jax.ShapeDtypeStruct(arrays[0].shape, f32),
        jax.ShapeDtypeStruct(pair_shape, f32),
    ]
    dma = pltpu.SemaphoreType.DMA
    scratch = [
        pltpu.VMEM((kvh, tiles, HEAD_SIZE, width), f32),
        pltpu.VMEM((kvh, tiles, width, HEAD_SIZE), jnp.bfloat16),
        pltpu.VMEM((kvh, tiles, width, HEAD_SIZE), jnp.bfloat16),
        pltpu.VMEM((kvh, tiles, 1, width), f32),
    ]
    scratch += [pltpu.VMEM((pair_shape[0], HEAD_SIZE), f32)] * (2 * kvh)
    scratch += [
        pltpu.VMEM((window + 1,) + pair_shape, jnp.bfloat16),
        pltpu.VMEM((reach + 1,) + pair_shape, jnp.bfloat16),
        pltpu.VMEM((reach,) + pair_shape, jnp.bfloat16),
        dma((reach + 1,)),
        dma((reach + 1,)),
        dma((reach,)),
        dma((reach + 1,)),
    ]
    scratch += scatter_buffers(pieces, sizes) + [dma((len(pieces), 4, max(sizes)))] * 2
    results = pl.pallas_call(
        functools.partial(scatter_attend_kernel, sizes, pieces, parts, tiles),
        out_shape=out_shape,
        in_specs=[whole] * (parts + len(arrays)),
        out_specs=[whole] * len(out_shape),
        scratch_shapes=scratch,
        compiler_params=pltpu.CompilerParams(
            collective_id=ident, has_side_effects=True, vmem_limit_bytes=VMEM_LIMIT
        ),
        cost_estimate=pl.CostEstimate(
            flops=25_000_000_000, bytes_accessed=60_000_000, transcendentals=0
        ),
    )(*grads, *arrays)
    return results[:parts], *results[parts:]


def per_device(sizes, layer_input, w_qkv, w_out, w_gu, w_down, norm_gains, lengths, cotangent):
    token_rows = layer_input.shape[0]
    query_width = QUERY_HEADS * HEAD_SIZE
    key_width = KEY_VALUE_HEADS * HEAD_SIZE
    scale = 1.0 / math.sqrt(HEAD_SIZE)
    tiles = token_rows // BLK

    (qkv_all,) = all_gather([pack(w_qkv, ())], sizes, 0)
    mixing_in = unpack(qkv_all, sizes, w_qkv.shape[0]).reshape(D, -1)

    query_index = lax.axis_index("seq") * token_rows + jnp.arange(token_rows, dtype=jnp.int32)
    start = layout(lengths[0], query_index)
    half = HEAD_SIZE // 2
    freq = jnp.exp(jnp.arange(half, dtype=jnp.float32) * (-2.0 * math.log(THETA) / HEAD_SIZE))
    angle = (query_index - start).astype(jnp.float32)[:, None] * freq[None, :]
    cosine, sine = jnp.cos(angle)[:, None, :], jnp.sin(angle)[:, None, :]

    def rotated(rows, sign):
        first, second = rows[..., :half], rows[..., half:]
        turn = sign * sine
        return jnp.concatenate(
            [first * cosine - second * turn, second * cosine + first * turn], axis=-1
        )

    inputs = layer_input.astype(jnp.float32)
    normed, norm_back = jax.vjp(rms_norm, inputs, norm_gains[0])
    normed_low = normed.astype(jnp.bfloat16)
    projected = jnp.dot(normed_low, mixing_in, preferred_element_type=jnp.float32)
    heads = projected[:, : query_width + key_width].reshape(token_rows, -1, HEAD_SIZE)
    turned = rotated(heads, 1.0).astype(jnp.bfloat16)
    pairs_mine = jnp.concatenate(
        [
            turned[:, QUERY_HEADS:].reshape(token_rows, key_width),
            projected[:, query_width + key_width :].astype(jnp.bfloat16),
        ],
        axis=1,
    )
    query = (turned[:, :QUERY_HEADS] * jnp.bfloat16(scale)).reshape(token_rows, query_width)
    start_rows = start.reshape(tiles, 1, BLK)

    f32 = jnp.float32
    gathered, pairs, attended_t, attended_low, lse = gather_attend(
        [pack(w_out, ()), pack(w_down, (), D), pack(w_gu, ())],
        query,
        pairs_mine,
        start_rows,
        sizes,
        1,
    )
    expand_matrix = unpack(gathered[2], sizes, w_gu.shape[0]).reshape(D, 2 * FF)
    if whole_rows(w_down.shape[0], D):
        shrink_matrix = gathered[1].reshape(FF, D)
    else:
        shrink_matrix = unpack(gathered[1], sizes, w_down.shape[0]).reshape(FF, D)
    mixing_out = unpack(gathered[0], sizes, w_out.shape[0]).reshape(query_width, D)
    mid = inputs + jnp.dot(attended_low, mixing_out, preferred_element_type=f32)
    normed_two, norm_two_back = jax.vjp(rms_norm, mid, norm_gains[1])
    normed_two_low = normed_two.astype(jnp.bfloat16)
    gate_up = jnp.dot(normed_two_low, expand_matrix, preferred_element_type=f32)
    hidden, hidden_back = jax.vjp(silu_product, gate_up)
    hidden_low = hidden.astype(jnp.bfloat16)
    result = (mid + jnp.dot(hidden_low, shrink_matrix, preferred_element_type=f32)).astype(
        jnp.bfloat16
    )
    grad_down = jnp.einsum("tf,td->fd", hidden_low, cotangent, preferred_element_type=f32)
    d_hidden = jnp.einsum("td,fd->tf", cotangent, shrink_matrix, preferred_element_type=f32)
    d_gate_up = hidden_back(d_hidden)[0].astype(jnp.bfloat16)
    grad_expand = jnp.einsum("td,tf->df", normed_two_low, d_gate_up, preferred_element_type=f32)
    d_normed_two = jnp.einsum("tf,df->td", d_gate_up, expand_matrix, preferred_element_type=f32)
    d_mid_part, grad_gain_two = norm_two_back(d_normed_two)
    d_mid = cotangent.astype(f32) + d_mid_part
    d_branch = d_mid.astype(jnp.bfloat16)
    grad_mixing_out = jnp.einsum("tq,td->qd", attended_low, d_branch, preferred_element_type=f32)
    d_attended = jnp.einsum("td,qd->tq", d_branch, mixing_out, preferred_element_type=f32).astype(
        jnp.bfloat16
    )
    def by_owner(grad):
        return grad.astype(jnp.bfloat16).reshape(sizes + (-1,))

    if whole_rows(w_down.shape[0], D):
        down_sent = grad_down.astype(jnp.bfloat16).reshape(sizes + (-1, D))
    else:
        down_sent = pack(by_owner(grad_down), sizes)
    (gu_mine, down_mine, out_mine), d_query, d_pairs_mine = scatter_attend(
        [pack(by_owner(grad_expand), sizes), down_sent, pack(by_owner(grad_mixing_out), sizes)],
        [query, d_attended, pairs, start_rows, lse, attended_t],
        sizes,
        2,
    )
    d_turned = jnp.concatenate(
        [d_query, d_pairs_mine[:, :key_width]], axis=1
    ).reshape(token_rows, -1, HEAD_SIZE)
    d_projected = jnp.concatenate(
        [rotated(d_turned, -1.0).reshape(token_rows, -1), d_pairs_mine[:, key_width:]], axis=1
    ).astype(jnp.bfloat16)
    grad_mixing_in = jnp.einsum("td,tq->dq", normed_low, d_projected, preferred_element_type=f32)
    d_normed = jnp.einsum("tq,dq->td", d_projected, mixing_in, preferred_element_type=f32)
    d_input_part, grad_gain_one = norm_back(d_normed)
    gains = jnp.stack([grad_gain_one, grad_gain_two])
    qkv_mine, gains_sum = reduce_scatter(
        [pack(by_owner(grad_mixing_in), sizes)], gains, sizes, 3
    )
    return (
        result,
        d_mid + d_input_part,
        unpack(qkv_mine, (), w_qkv.shape[0]),
        unpack(out_mine, (), w_out.shape[0]),
        unpack(gu_mine, (), w_gu.shape[0]),
        unpack(down_mine, (), w_down.shape[0], D),
        gains_sum,
    )


def solution(mesh):
    spread = P(("seq", "dp"))
    rows = P(("seq", "dp"), None)
    return jax.shard_map(
        functools.partial(per_device, grid_sizes(mesh.shape["seq"], mesh.shape["dp"])),
        mesh=mesh,
        in_specs=(rows, spread, spread, spread, spread, P(), P("dp", None), rows),
        out_specs=(rows, rows, spread, spread, spread, spread, P()),
        check_vma=False,
    )
```

```python
import functools
import math

import jax
import jax.numpy as jnp
from jax import lax
from jax.experimental import pallas as pl
from jax.experimental.pallas import tpu as pltpu
from jax.sharding import PartitionSpec as P

D = 576
QUERY_HEADS = 9
KEY_VALUE_HEADS = 3
HEAD_SIZE = 64
FF = 1536
HG = QUERY_HEADS // KEY_VALUE_HEADS

EPS = 1e-05
THETA = 100000.0
MASKED = -1e30
MESH = pl.DeviceIdType.MESH
BLK = 256
VMEM_LIMIT = 56 * 1024 * 1024
ACROSS_LAST, ALONG_Y_LAST = (0, 2, 1), (0, 1, 2)
GATHER_ROUNDS = (0, 1, 2, 3, 3, 2, 2, 1, 2)
SCATTER_ROUNDS = (2, 2, 0, 1, 1, 2, 2, 1, 2)


def rms_norm(value_rows, gain):
    return (
        value_rows
        * lax.rsqrt(jnp.mean(value_rows * value_rows, axis=-1, keepdims=True) + EPS)
        * gain
    )


def layout(lengths_row, index):
    count = lengths_row.shape[0]
    earlier = jnp.arange(count)[:, None] >= jnp.arange(count)[None, :]
    ends = jnp.sum(jnp.where(earlier, lengths_row[None, :], 0), axis=1, dtype=jnp.int32)
    done = ends[None, :] <= index[:, None]
    return jnp.sum(jnp.where(done, lengths_row[None, :], 0), axis=1, dtype=jnp.int32)


def silu_product(gate_up):
    width = gate_up.shape[1] // 2
    return jax.nn.silu(gate_up[:, :width]) * gate_up[:, width:]


def grid_sizes(seq_count, dp_count):
    return (seq_count // 2, 2, dp_count // 2, 2)


def coords():
    seq, dp = lax.axis_index("seq"), lax.axis_index("dp")
    return [seq // 2, seq % 2, dp // 2, dp % 2]


def device_at(coord):
    return (coord[0] * 2 + coord[1], coord[2] * 2 + coord[3])


def moved(me, sizes, axis, step):
    other = list(me)
    other[axis] = lax.rem(me[axis] + step + sizes[axis], sizes[axis])
    return other


def greet(me, sizes):
    barrier = pltpu.get_barrier_semaphore()
    count = 0
    for axis in range(4):
        for step in range(1, sizes[axis]):
            pl.semaphore_signal(
                barrier,
                inc=1,
                device_id=device_at(moved(me, sizes, axis, step)),
                device_id_type=MESH,
            )
            count += 1
    pl.semaphore_wait(barrier, count)


class Piece:
    def __init__(self, array, shape, order):
        self.array, self.order = array, order
        self.rows, self.columns = shape[0][1], shape[1][1]
        self.at = tuple(pl.ds(first, size) for first, size in shape)


def pieces_of(shards, orders, cuts):
    pieces = []
    for array, shard in enumerate(shards):
        rows, columns = shard.shape[-2:]
        cut = rows // 32 * 16 if cuts[array] and rows >= 32 else 0
        spans = [(0, cut), (cut, rows - cut)] if cut else [(0, rows)]
        for number, span in enumerate(spans):
            order = orders[array][number % len(orders[array])]
            pieces.append(Piece(array, (span, (0, columns)), order))
    return pieces


def gather_steps(me, sizes, pieces, shards, outs, send, recv, core_send, core_recv, local):
    parts = len(pieces)
    started = []
    for array in range(len(shards)):
        own = pltpu.make_async_copy(
            shards[array], outs[array].at[me[0], me[1], me[2], me[3]], local.at[array]
        )
        own.start()
        started.append(own)

    def region(part, held, where):
        piece = pieces[part]
        lead = tuple(slice(None) if a in held else where[a] for a in range(3)) + (where[3],)
        return outs[piece.array].at[lead + piece.at]

    def copy(part, phase, step, arriving=False):
        order = pieces[part].order
        where = moved(me, sizes, order[phase], -step) if arriving else me
        block = region(part, order[:phase], where)
        source = block
        if phase == 0 and not arriving:
            source = shards[pieces[part].array].at[pieces[part].at]
        return pltpu.make_async_remote_copy(
            src_ref=source,
            dst_ref=block,
            send_sem=send.at[part, phase, step],
            recv_sem=recv.at[part, phase, step],
            device_id=device_at(moved(me, sizes, order[phase], step)),
            device_id_type=MESH,
        )

    def to_core(part, slot, held, where, arriving=False):
        there = moved(where, sizes, 3, 1) if arriving else where
        block = region(part, held, there)
        return pltpu.make_async_remote_copy(
            src_ref=block,
            dst_ref=block,
            send_sem=core_send.at[part, slot],
            recv_sem=core_recv.at[part, slot],
            device_id=device_at(moved(me, sizes, 3, 1)),
            device_id_type=MESH,
        )

    for part in range(parts):
        for step in range(1, sizes[pieces[part].order[0]]):
            copy(part, 0, step).start()
    for own in started:
        own.wait()
    yield
    pending = []
    turns = [(phase, part) for phase in range(3) for part in range(parts)]
    for phase, part in sorted(turns, key=lambda turn: (3 * turn[0] + turn[1], turn[0])):
        order = pieces[part].order
        held = order[:phase]
        for step in range(1, sizes[order[phase]]):
            copy(part, phase, step, arriving=True).wait_recv()
            if phase == 2:
                origin = moved(me, sizes, order[phase], -step)
                to_core(part, step, held, origin).start()
                pending.append((part, step, held, origin))
        if phase < 2:
            for step in range(1, sizes[order[phase + 1]]):
                copy(part, phase + 1, step).start()
        if phase == 1:
            to_core(part, 0, order[:2], me).start()
            pending.append((part, 0, order[:2], me))
        yield
    for part in range(parts):
        for phase in range(3):
            for step in range(1, sizes[pieces[part].order[phase]]):
                copy(part, phase, step).wait_send()
    for part, slot, held, origin in pending:
        to_core(part, slot, held, origin).wait_send()
        to_core(part, slot, held, origin, arriving=True).wait_recv()


def gather_semaphores(arrays, parts, most):
    return [
        pltpu.SemaphoreType.DMA((parts, 3, most)),
        pltpu.SemaphoreType.DMA((parts, 3, most)),
        pltpu.SemaphoreType.DMA((parts, most)),
        pltpu.SemaphoreType.DMA((parts, most)),
        pltpu.SemaphoreType.DMA((arrays,)),
    ]


def gather_kernel(sizes, pieces, arrays, *refs):
    me = coords()
    greet(me, sizes)
    for _ in gather_steps(
        me, sizes, pieces, refs[:arrays], refs[arrays : 2 * arrays], *refs[2 * arrays :]
    ):
        pass


def all_gather(shards, sizes, ident):
    arrays = len(shards)
    pieces = pieces_of(shards, [(ALONG_Y_LAST, ACROSS_LAST)] * arrays, [True] * arrays)
    return pl.pallas_call(
        functools.partial(gather_kernel, sizes, pieces, arrays),
        out_shape=[jax.ShapeDtypeStruct(sizes + s.shape, s.dtype) for s in shards],
        in_specs=[pl.BlockSpec(memory_space=pltpu.VMEM)] * arrays,
        out_specs=[pl.BlockSpec(memory_space=pltpu.VMEM)] * arrays,
        scratch_shapes=gather_semaphores(arrays, len(pieces), max(sizes)),
        compiler_params=pltpu.CompilerParams(
            collective_id=ident, has_side_effects=True, vmem_limit_bytes=VMEM_LIMIT
        ),
        cost_estimate=pl.CostEstimate(flops=0, bytes_accessed=60_000_000, transcendentals=0),
    )(*shards)


def scatter_order(piece):
    return (3,) + tuple(reversed(piece.order))


def scatter_kernel(sizes, pieces, arrays, with_gains, *refs):
    me = coords()
    greet(me, sizes)
    for _ in scatter_steps(me, sizes, pieces, arrays, with_gains, *refs):
        pass


def scatter_steps(me, sizes, pieces, arrays, with_gains, *refs):
    parts = len(pieces)
    n_in = arrays + with_gains
    grads, outs = refs[:n_in], refs[n_in : 2 * n_in]
    rest = list(refs[2 * n_in :])
    arrived = [[rest.pop(0) for _ in range(4)] for _ in range(parts)]
    totals = [[rest.pop(0) for _ in range(3)] for _ in range(parts)]
    if with_gains:
        gain_arrived, gain_total = rest.pop(0), rest.pop(0)
        gain_send, gain_recv = rest.pop(0), rest.pop(0)
    send, recv = rest

    def held_at(part, phase, index):
        order = scatter_order(pieces[part])
        left = sorted(set(range(4)) - set(order[:phase]))
        lead = tuple(index if a == order[phase] else slice(None) for a in left)
        if phase == 0:
            return grads[pieces[part].array].at[lead + pieces[part].at]
        return totals[part][phase - 1].at[lead]

    def copy(part, phase, step):
        axis = scatter_order(pieces[part])[phase]
        target = moved(me, sizes, axis, step)
        return pltpu.make_async_remote_copy(
            src_ref=held_at(part, phase, target[axis]),
            dst_ref=arrived[part][phase].at[step - 1],
            send_sem=send.at[part, phase, step],
            recv_sem=recv.at[part, phase, step],
            device_id=device_at(target),
            device_id_type=MESH,
        )

    def add(part, phase):
        piece = pieces[part]
        axis = scatter_order(piece)[phase]
        mine = held_at(part, phase, me[axis])
        lead = mine.shape[:-2]
        others = arrived[part][phase]

        def total_at(place):
            if phase < 3 and sizes[axis] == 2:
                return mine[place] + others[(0,) + place]
            value = mine[place].astype(jnp.float32)
            for step in range(1, sizes[axis]):
                value = value + others[(step - 1,) + place].astype(jnp.float32)
            return value

        if phase == 3:
            outs[piece.array][piece.at] = total_at((slice(None), slice(None)))
            return
        target = totals[part][phase]

        def body(flat, carry):
            place = []
            for size in reversed(lead):
                place.insert(0, lax.rem(flat, size))
                flat = flat // size
            place = tuple(place) + (slice(None), slice(None))
            target[place] = total_at(place).astype(target.dtype)
            return carry

        lax.fori_loop(0, math.prod(lead), body, 0)

    def gain_copy(phase, step):
        return pltpu.make_async_remote_copy(
            src_ref=gain_total.at[phase],
            dst_ref=gain_arrived.at[phase, step - 1],
            send_sem=gain_send.at[phase, step],
            recv_sem=gain_recv.at[phase, step],
            device_id=device_at(moved(me, sizes, phase, step)),
            device_id_type=MESH,
        )

    def start(phase, part):
        for step in range(1, sizes[scatter_order(pieces[part])[phase]]):
            copy(part, phase, step).start()

    def gain_start(phase):
        for step in range(1, sizes[phase]):
            gain_copy(phase, step).start()

    def gain_turn(phase):
        value = gain_total[phase]
        for step in range(1, sizes[phase]):
            gain_copy(phase, step).wait_recv()
        slots = [value] + [gain_arrived[phase, s - 1] for s in range(1, sizes[phase])]
        value = sum(slots[1:], slots[0])
        if phase < 3:
            gain_total[phase + 1] = value
            gain_start(phase + 1)
        else:
            outs[arrays][...] = value

    for part in range(parts):
        start(0, part)
    if with_gains:
        gain_total[0] = grads[arrays][...]
        gain_start(0)
    yield
    turns = [(phase, part) for phase in range(4) for part in range(parts + with_gains)]

    def rank(turn):
        phase, part = turn
        return (0, part, 0) if phase == 0 else (1, phase + part, -phase)

    for phase, part in sorted(turns, key=rank):
        if part == parts:
            gain_turn(phase)
            continue
        for step in range(1, sizes[scatter_order(pieces[part])[phase]]):
            copy(part, phase, step).wait_recv()
        add(part, phase)
        if phase < 3:
            start(phase + 1, part)
        yield
    for phase in range(4):
        for part in range(parts):
            for step in range(1, sizes[scatter_order(pieces[part])[phase]]):
                copy(part, phase, step).wait_send()
        if with_gains:
            for step in range(1, sizes[phase]):
                gain_copy(phase, step).wait_send()


def scatter_buffers(pieces, sizes):
    scratch = []
    for piece in pieces:
        left = [0, 1, 2, 3]
        for axis in scatter_order(piece):
            left.remove(axis)
            shape = (sizes[axis] - 1,) + tuple(sizes[a] for a in left) + (piece.rows, piece.columns)
            scratch.append(pltpu.VMEM(shape, jnp.bfloat16))
    for piece in pieces:
        left = [0, 1, 2, 3]
        for axis in scatter_order(piece)[:3]:
            left.remove(axis)
            shape = tuple(sizes[a] for a in left) + (piece.rows, piece.columns)
            scratch.append(pltpu.VMEM(shape, jnp.bfloat16))
    return scratch


def reduce_scatter(grads, gains, sizes, ident):
    arrays = len(grads)
    most = max(sizes)
    pieces = pieces_of(grads, [(ALONG_Y_LAST, ACROSS_LAST)] * arrays, [True] * arrays)
    scratch = scatter_buffers(pieces, sizes)
    outs = [jax.ShapeDtypeStruct(g.shape[4:], jnp.float32) for g in grads]
    args = list(grads)
    if gains is not None:
        args.append(gains)
        outs.append(jax.ShapeDtypeStruct(gains.shape, jnp.float32))
        scratch += [
            pltpu.VMEM((4, most - 1) + gains.shape, jnp.float32),
            pltpu.VMEM((4,) + gains.shape, jnp.float32),
            pltpu.SemaphoreType.DMA((4, most)),
            pltpu.SemaphoreType.DMA((4, most)),
        ]
    scratch += [pltpu.SemaphoreType.DMA((len(pieces), 4, most))] * 2
    return pl.pallas_call(
        functools.partial(scatter_kernel, sizes, pieces, arrays, int(gains is not None)),
        out_shape=outs,
        in_specs=[pl.BlockSpec(memory_space=pltpu.VMEM)] * len(args),
        out_specs=[pl.BlockSpec(memory_space=pltpu.VMEM)] * len(outs),
        scratch_shapes=scratch,
        compiler_params=pltpu.CompilerParams(
            collective_id=ident, has_side_effects=True, vmem_limit_bytes=VMEM_LIMIT
        ),
        cost_estimate=pl.CostEstimate(flops=0, bytes_accessed=60_000_000, transcendentals=0),
    )(*args)


def padded_rows(count):
    return -(-count // 2048) * 16


def whole_rows(size, width):
    return size % (16 * width) == 0


def pack(flat, lead, width=None):
    size = flat.shape[-1]
    if width and whole_rows(size, width):
        return flat.reshape(lead + (-1, width))
    rows = padded_rows(size)
    none = [(0, 0)] * len(lead)
    if size % 128 == 0:
        flat = flat.reshape(lead + (size // 128, 128))
        return jnp.pad(flat, none + [(0, rows - size // 128), (0, 0)])
    return jnp.pad(flat, none + [(0, rows * 128 - size)]).reshape(lead + (rows, 128))


def unpack(packed, lead, size, width=None):
    if width and whole_rows(size, width):
        return packed.reshape(lead + (size,))
    if size % 128 == 0:
        return packed[..., : size // 128, :].reshape(lead + (size,))
    return packed.reshape(lead + (-1,))[..., :size]


def dot_rows(left, right):
    return lax.dot_general(left, right, (((1,), (1,)), ((), ())), preferred_element_type=jnp.float32)


def dot_columns(left, right):
    return lax.dot_general(left, right, (((0,), (0,)), ((), ())), preferred_element_type=jnp.float32)


def head_columns(head):
    first = head * HEAD_SIZE
    second = first + KEY_VALUE_HEADS * HEAD_SIZE
    return slice(first, first + HEAD_SIZE), slice(second, second + HEAD_SIZE)


def head_columns(head):
    first = head * HEAD_SIZE
    second = first + KEY_VALUE_HEADS * HEAD_SIZE
    return slice(first, first + HEAD_SIZE), slice(second, second + HEAD_SIZE)


def blocks_of(offset, window, tile, tiles):
    return (tile if offset == window else 0), (tile + 1 if offset == 0 else tiles)


def query_part(head, within):
    first = (head * HG + within) * HEAD_SIZE
    return slice(first, first + HEAD_SIZE)


def stack_heads(rows_ref, stacked_ref, tile):
    for head in range(KEY_VALUE_HEADS):
        for within in range(HG):
            stacked_ref[head, tile, pl.ds(within * BLK, BLK), :] = rows_ref[
                pl.ds(tile * BLK, BLK), query_part(head, within)
            ]


def lay_heads(columns):
    return jnp.concatenate(
        [
            columns[head][:, within * BLK : (within + 1) * BLK].T
            for head in range(KEY_VALUE_HEADS)
            for within in range(HG)
        ],
        axis=1,
    )


def places(place, tile, tiles, start_ref):
    lane = lax.broadcasted_iota(jnp.int32, (1, HG * BLK), 1)
    index = (place * tiles + tile) * BLK + lax.rem(lane, BLK)
    return index, jnp.concatenate([start_ref[tile]] * HG, axis=1)


def neighbour(me, sizes, axis, step):
    return device_at(moved(me, sizes, axis, step))


class PairFlow:
    def __init__(self, me, sizes, mine, slots, chain_send, cross_send, recv):
        self.me, self.sizes, self.mine, self.slots = me, sizes, mine, slots
        self.chain_send, self.cross_send, self.recv = chain_send, cross_send, recv
        self.reach = sizes[0] // 2

    def chain(self, j):
        return pltpu.make_async_remote_copy(
            src_ref=self.mine if j == 0 else self.slots.at[2 * j],
            dst_ref=self.slots.at[2 * j + 2],
            send_sem=self.chain_send.at[j],
            recv_sem=self.recv.at[2 * j + 2],
            device_id=neighbour(self.me, self.sizes, 0, 1),
            device_id_type=MESH,
        )

    def cross(self, j, side):
        slot = 2 * j + 1 if side == 0 else 2 * j - 1
        return pltpu.make_async_remote_copy(
            src_ref=self.mine if j == 0 else self.slots.at[2 * j],
            dst_ref=self.slots.at[slot],
            send_sem=self.cross_send.at[j],
            recv_sem=self.recv.at[slot],
            device_id=neighbour(self.me, self.sizes, 1, 1),
            device_id_type=MESH,
        )

    def each(self, j, act):
        there = self.me[0] >= j
        if j < self.reach:

            @pl.when(there & (self.me[0] + 1 < self.sizes[0]))
            def _():
                act(self.chain(j))

            @pl.when(there & (self.me[1] == 0))
            def _():
                act(self.cross(j, 0))

        if j > 0:

            @pl.when(there & (self.me[1] == 1))
            def _():
                act(self.cross(j, 1))

    def forward(self, j):
        self.each(j, lambda copy: copy.start())

    def finish(self, j):
        self.each(j, lambda copy: copy.wait_send())

    def arrive(self, offset):
        block = self.slots.at[offset]
        pltpu.make_async_remote_copy(
            src_ref=block,
            dst_ref=block,
            send_sem=self.cross_send.at[0],
            recv_sem=self.recv.at[offset],
            device_id=neighbour(self.me, self.sizes, 1, 1),
            device_id_type=MESH,
        ).wait_recv()


def gather_attend_kernel(sizes, pieces, parts, tiles, *refs):
    shards, refs = refs[:parts], refs[parts:]
    (rows_ref, mine_ref, start_ref), refs = refs[:3], refs[3:]
    outs, refs = refs[:parts], refs[parts:]
    slots, o_ref, out_ref, lse_ref, total_ref, q_ref = refs[:6]
    semaphores, (chain_send, cross_send, recv, own_sem) = refs[6:11], refs[11:]
    me = coords()
    place = me[0] * 2 + me[1]
    window = sizes[0]
    greet(me, sizes)
    flow = PairFlow(me, sizes, mine_ref, slots, chain_send, cross_send, recv)
    flow.forward(0)
    own = pltpu.make_async_copy(mine_ref, slots.at[0], own_sem)
    own.start()
    weights = gather_steps(me, sizes, pieces, shards, outs, *semaphores)
    token_rows = tiles * BLK
    for tile in range(tiles):
        stack_heads(rows_ref, q_ref, tile)

    def unit(offset, tile, head):
        key_part, value_part = head_columns(head)
        low, high = blocks_of(offset, window, tile, tiles)
        q = q_ref[head, tile]
        index, start = places(place, tile, tiles, start_ref)
        width = q.shape[0]
        held = mine_ref if offset == 0 else slots.at[offset]
        base = (place - offset) * token_rows

        def step(block, carry):
            highest, total, acc = carry
            first = pl.multiple_of(block * BLK, BLK)
            rows = pl.ds(first, BLK)
            s = dot_rows(held[rows, key_part], q)
            row = base + first + lax.broadcasted_iota(jnp.int32, s.shape, 0)
            s = jnp.where((row <= index) & (row >= start), s, MASKED)
            new = jnp.maximum(highest, jnp.max(s, axis=0, keepdims=True))
            p = jnp.exp(s - new)
            fade = jnp.exp(highest - new)
            total = total * fade + jnp.sum(p, axis=0, keepdims=True)
            acc = acc * fade + dot_columns(held[rows, value_part], p.astype(jnp.bfloat16))
            return new, total, acc

        if offset == 0:
            carry = (
                jnp.full((1, width), MASKED, jnp.float32),
                jnp.zeros((1, width), jnp.float32),
                jnp.zeros((HEAD_SIZE, width), jnp.float32),
            )
        else:
            carry = lse_ref[head, tile], total_ref[head, tile], o_ref[head, tile]
        highest, total, acc = lax.fori_loop(low, high, step, carry)
        lse_ref[head, tile], total_ref[head, tile], o_ref[head, tile] = highest, total, acc

    slot = 0

    def attend(offset, tile):
        nonlocal slot

        @pl.when(place >= offset)
        def _():
            for head in range(KEY_VALUE_HEADS):
                unit(offset, tile, head)

        for _ in range(GATHER_ROUNDS[slot] if slot < len(GATHER_ROUNDS) else 0):
            next(weights)
        slot += 1

    def receive(offset):
        @pl.when(place >= offset)
        def _():
            flow.arrive(offset)

        if offset % 2 == 0:
            flow.forward(offset // 2)

    for j in range(flow.reach + 1):
        for offset in (0,) if j == 0 else (2 * j, 2 * j - 1):
            if offset % 2:
                receive(offset)
            for tile in range(tiles):
                if tile == tiles - 1 and offset % 2 and j < flow.reach:
                    receive(2 * j + 2)
                attend(offset, tile)
        if j == 0:
            receive(2)
    for tile, head in [(t, h) for t in range(tiles) for h in range(KEY_VALUE_HEADS)]:
        total = total_ref[head, tile]
        o_ref[head, tile] = o_ref[head, tile] / total
        lse_ref[head, tile] = lse_ref[head, tile] + jnp.log(total)
    for tile in range(tiles):
        laid = lay_heads([o_ref[head, tile] for head in range(KEY_VALUE_HEADS)])
        out_ref[pl.ds(tile * BLK, BLK), :] = laid.astype(out_ref.dtype)
    for _ in weights:
        pass
    for j in range(flow.reach + 1):
        flow.finish(j)
    own.wait()


def gather_attend(shards, query, pairs_mine, start_rows, sizes, ident):
    parts = len(shards)
    pieces = pieces_of(shards, [(ALONG_Y_LAST,), (ALONG_Y_LAST, ACROSS_LAST), (ALONG_Y_LAST, ACROSS_LAST)], [False, True, True])
    kvh, tiles, width = KEY_VALUE_HEADS, query.shape[0] // BLK, HG * BLK
    window = sizes[0]
    f32 = jnp.float32
    whole = pl.BlockSpec(memory_space=pltpu.VMEM)
    column = jax.ShapeDtypeStruct((kvh, tiles, HEAD_SIZE, width), f32)
    line = jax.ShapeDtypeStruct((kvh, tiles, 1, width), f32)
    out_shape = [jax.ShapeDtypeStruct(sizes + s.shape, s.dtype) for s in shards]
    out_shape += [
        jax.ShapeDtypeStruct((window + 1,) + pairs_mine.shape, pairs_mine.dtype),
        column,
        jax.ShapeDtypeStruct(query.shape, query.dtype),
        line,
    ]
    dma = pltpu.SemaphoreType.DMA
    results = pl.pallas_call(
        functools.partial(gather_attend_kernel, sizes, pieces, parts, tiles),
        out_shape=out_shape,
        in_specs=[whole] * (parts + 3),
        out_specs=[whole] * len(out_shape),
        scratch_shapes=[
            pltpu.VMEM(line.shape, f32),
            pltpu.VMEM((kvh, tiles, width, HEAD_SIZE), query.dtype),
        ]
        + gather_semaphores(parts, len(pieces), max(sizes))
        + [dma((window // 2 + 1,)), dma((window // 2 + 1,)), dma((window + 1,)), dma],
        compiler_params=pltpu.CompilerParams(
            collective_id=ident, has_side_effects=True, vmem_limit_bytes=VMEM_LIMIT
        ),
        cost_estimate=pl.CostEstimate(
            flops=10_000_000_000, bytes_accessed=60_000_000, transcendentals=0
        ),
    )(*shards, query, pairs_mine, start_rows)
    return results[:parts], *results[parts:]


class SumFlow:
    def __init__(self, me, sizes, partial, crossed, chained, chain_send, cross_send, chain_recv, cross_recv):
        self.me, self.sizes, self.partial = me, sizes, partial
        self.crossed, self.chained = crossed, chained
        self.chain_send, self.cross_send = chain_send, cross_send
        self.chain_recv, self.cross_recv = chain_recv, cross_recv
        self.reach = sizes[0] // 2

    def chain(self, j):
        return pltpu.make_async_remote_copy(
            src_ref=self.partial.at[2 * j],
            dst_ref=self.chained.at[j - 1],
            send_sem=self.chain_send.at[j],
            recv_sem=self.chain_recv.at[j - 1],
            device_id=neighbour(self.me, self.sizes, 0, -1),
            device_id_type=MESH,
        )

    def cross(self, offset, side):
        j = (offset + 1) // 2 if side == 0 else offset // 2
        return pltpu.make_async_remote_copy(
            src_ref=self.partial.at[offset],
            dst_ref=self.crossed.at[j],
            send_sem=self.cross_send.at[offset // 2],
            recv_sem=self.cross_recv.at[j],
            device_id=neighbour(self.me, self.sizes, 1, 1),
            device_id_type=MESH,
        )

    def each_cross(self, offset, act):
        for side in range(2):

            @pl.when((self.me[1] == side) & (self.me[0] * 2 + side >= offset))
            def _(side=side):
                act(self.cross(offset, side))

    def has_cross(self, j):
        side = self.me[1]
        if j == 0:
            return side == 0
        if j == self.reach:
            return (side == 1) & (self.me[0] >= j)
        return self.me[0] >= j

    def has_chain(self, j):
        return (self.me[0] >= j) & (self.me[0] + 1 < self.sizes[0])

    def cross_arrive(self, j):
        pltpu.make_async_remote_copy(
            src_ref=self.crossed.at[j],
            dst_ref=self.crossed.at[j],
            send_sem=self.cross_send.at[0],
            recv_sem=self.cross_recv.at[j],
            device_id=neighbour(self.me, self.sizes, 1, 1),
            device_id_type=MESH,
        ).wait_recv()

    def chain_arrive(self, j):
        pltpu.make_async_remote_copy(
            src_ref=self.chained.at[j],
            dst_ref=self.chained.at[j],
            send_sem=self.chain_send.at[0],
            recv_sem=self.chain_recv.at[j],
            device_id=neighbour(self.me, self.sizes, 0, -1),
            device_id_type=MESH,
        ).wait_recv()


def scatter_attend_kernel(sizes, pieces, parts, tiles, *refs):
    grads, refs = refs[:parts], refs[parts:]
    (rows_ref, do_rows_ref, slots, start_ref, lse_ref, o_ref), refs = refs[:6], refs[6:]
    outs, refs = refs[:parts], refs[parts:]
    (dq_rows_ref, dkv_ref), refs = refs[:2], refs[2:]
    (dq_ref, q_ref, do_ref, delta_ref), refs = refs[:4], refs[4:]
    accs, refs = refs[: 2 * KEY_VALUE_HEADS], refs[2 * KEY_VALUE_HEADS :]
    flow_refs, scatter_refs = refs[:7], refs[7:]
    me = coords()
    place = me[0] * 2 + me[1]
    window = sizes[0]
    greet(me, sizes)
    flow = SumFlow(me, sizes, *flow_refs)
    partial, crossed, chained = flow_refs[:3]
    weights = scatter_steps(me, sizes, pieces, parts, 0, *grads, *outs, *scatter_refs)
    next(weights)
    token_rows = tiles * BLK
    dq_ref[...] = jnp.zeros_like(dq_ref)
    for tile in range(tiles):
        stack_heads(rows_ref, q_ref, tile)
        stack_heads(do_rows_ref, do_ref, tile)
        for head in range(KEY_VALUE_HEADS):
            columns = do_ref[head, tile].astype(jnp.float32).T
            delta_ref[head, tile] = jnp.sum(columns * o_ref[head, tile], axis=0, keepdims=True)

    def unit(offset, tile, head):
        key_part, value_part = head_columns(head)
        low, high = blocks_of(offset, window, tile, tiles)
        q, do = q_ref[head, tile], do_ref[head, tile]
        index, start = places(place, tile, tiles, start_ref)
        lse, delta = lse_ref[head, tile], delta_ref[head, tile]
        dk_acc, dv_acc = accs[head], accs[KEY_VALUE_HEADS + head]
        base = (place - offset) * token_rows

        def step(block, dq):
            first = pl.multiple_of(block * BLK, BLK)
            rows = pl.ds(first, BLK)
            k = slots[offset, rows, key_part]
            s = dot_rows(k, q)
            dp = dot_rows(slots[offset, rows, value_part], do)
            row = base + first + lax.broadcasted_iota(jnp.int32, s.shape, 0)
            s = jnp.where((row <= index) & (row >= start), s - lse, MASKED)
            p = jnp.exp(s)
            ds = (p * (dp - delta)).astype(jnp.bfloat16)
            dv_acc[rows, :] += jnp.dot(p.astype(jnp.bfloat16), do, preferred_element_type=jnp.float32)
            dk_acc[rows, :] += jnp.dot(ds, q, preferred_element_type=jnp.float32)
            return dq + dot_columns(k, ds)

        dq_ref[head, tile] = lax.fori_loop(low, high, step, dq_ref[head, tile])

    slot = 0

    def collect(offset):
        nonlocal slot

        for tile in range(tiles):

            @pl.when(place >= offset)
            def _(tile=tile):
                if tile == 0:
                    for acc in accs:
                        acc[...] = jnp.zeros_like(acc)
                for head in range(KEY_VALUE_HEADS):
                    unit(offset, tile, head)

            if tile < tiles - 1:
                progress()

    def progress():
        nonlocal slot
        for _ in range(SCATTER_ROUNDS[slot] if slot < len(SCATTER_ROUNDS) else 0):
            next(weights)
        slot += 1

    def summed(rows):
        return jnp.concatenate([acc[rows, :] for acc in accs], axis=1)

    def over_rows(body):
        def run(block, carry):
            body(pl.ds(pl.multiple_of(block * BLK, BLK), BLK))
            return carry

        lax.fori_loop(0, tiles, run, 0)

    def keep(offset):
        def body(rows):
            partial[offset, rows, :] = summed(rows).astype(partial.dtype)

        over_rows(body)

    def fold(j, source):
        def body(rows):
            partial[2 * j, rows, :] = (
                partial[2 * j, rows, :].astype(jnp.float32) + source[j, rows, :].astype(jnp.float32)
            ).astype(partial.dtype)

        over_rows(body)

    def fold_own(source):
        def body(rows):
            dkv_ref[rows, :] += source[0, rows, :].astype(jnp.float32)

        over_rows(body)

    for j in reversed(range(1, flow.reach + 1)):
        odd = 2 * j - 1

        collect(odd)

        @pl.when(place >= odd)
        def _(odd=odd):
            keep(odd)

        flow.each_cross(odd, lambda copy: copy.start())
        progress()
        collect(2 * j)

        @pl.when(me[0] >= j)
        def _(j=j):
            keep(2 * j)

        @pl.when(flow.has_cross(j))
        def _(j=j):
            flow.cross_arrive(j)
            fold(j, crossed)

        if j < flow.reach:

            @pl.when(flow.has_chain(j))
            def _(j=j):
                flow.chain_arrive(j)
                fold(j, chained)

        @pl.when(me[0] >= j)
        def _(j=j):
            flow.chain(j).start()

        progress()
    collect(0)

    def first(rows):
        dkv_ref[rows, :] = summed(rows)

    over_rows(first)
    progress()

    for tile in range(tiles):
        laid = lay_heads([dq_ref[head, tile] for head in range(KEY_VALUE_HEADS)])
        dq_rows_ref[pl.ds(tile * BLK, BLK), :] = laid * (1.0 / math.sqrt(HEAD_SIZE))

    @pl.when(flow.has_cross(0))
    def _():
        flow.cross_arrive(0)
        fold_own(crossed)

    @pl.when(flow.has_chain(0))
    def _():
        flow.chain_arrive(0)
        fold_own(chained)

    for _ in weights:
        pass
    for j in range(1, flow.reach + 1):
        flow.each_cross(2 * j - 1, lambda copy: copy.wait_send())

        @pl.when(me[0] >= j)
        def _(j=j):
            flow.chain(j).wait_send()


def scatter_attend(grads, arrays, sizes, ident):
    parts = len(grads)
    pieces = pieces_of(grads, [(ALONG_Y_LAST, ACROSS_LAST), (ALONG_Y_LAST,), (ALONG_Y_LAST,)], [True, False, False])
    token_rows = arrays[0].shape[0]
    kvh, tiles, width = KEY_VALUE_HEADS, token_rows // BLK, HG * BLK
    window, reach = sizes[0], sizes[0] // 2
    pair_shape = arrays[2].shape[1:]
    f32 = jnp.float32
    whole = pl.BlockSpec(memory_space=pltpu.VMEM)
    out_shape = [jax.ShapeDtypeStruct(g.shape[4:], f32) for g in grads]
    out_shape += [
        jax.ShapeDtypeStruct(arrays[0].shape, f32),
        jax.ShapeDtypeStruct(pair_shape, f32),
    ]
    dma = pltpu.SemaphoreType.DMA
    scratch = [
        pltpu.VMEM((kvh, tiles, HEAD_SIZE, width), f32),
        pltpu.VMEM((kvh, tiles, width, HEAD_SIZE), jnp.bfloat16),
        pltpu.VMEM((kvh, tiles, width, HEAD_SIZE), jnp.bfloat16),
        pltpu.VMEM((kvh, tiles, 1, width), f32),
    ]
    scratch += [pltpu.VMEM((pair_shape[0], HEAD_SIZE), f32)] * (2 * kvh)
    scratch += [
        pltpu.VMEM((window + 1,) + pair_shape, jnp.bfloat16),
        pltpu.VMEM((reach + 1,) + pair_shape, jnp.bfloat16),
        pltpu.VMEM((reach,) + pair_shape, jnp.bfloat16),
        dma((reach + 1,)),
        dma((reach + 1,)),
        dma((reach,)),
        dma((reach + 1,)),
    ]
    scratch += scatter_buffers(pieces, sizes) + [dma((len(pieces), 4, max(sizes)))] * 2
    results = pl.pallas_call(
        functools.partial(scatter_attend_kernel, sizes, pieces, parts, tiles),
        out_shape=out_shape,
        in_specs=[whole] * (parts + len(arrays)),
        out_specs=[whole] * len(out_shape),
        scratch_shapes=scratch,
        compiler_params=pltpu.CompilerParams(
            collective_id=ident, has_side_effects=True, vmem_limit_bytes=VMEM_LIMIT
        ),
        cost_estimate=pl.CostEstimate(
            flops=25_000_000_000, bytes_accessed=60_000_000, transcendentals=0
        ),
    )(*grads, *arrays)
    return results[:parts], *results[parts:]


def per_device(sizes, layer_input, w_qkv, w_out, w_gu, w_down, norm_gains, lengths, cotangent):
    token_rows = layer_input.shape[0]
    query_width = QUERY_HEADS * HEAD_SIZE
    key_width = KEY_VALUE_HEADS * HEAD_SIZE
    scale = 1.0 / math.sqrt(HEAD_SIZE)
    tiles = token_rows // BLK

    (qkv_all,) = all_gather([pack(w_qkv, ())], sizes, 0)
    mixing_in = unpack(qkv_all, sizes, w_qkv.shape[0]).reshape(D, -1)

    query_index = lax.axis_index("seq") * token_rows + jnp.arange(token_rows, dtype=jnp.int32)
    start = layout(lengths[0], query_index)
    half = HEAD_SIZE // 2
    freq = jnp.exp(jnp.arange(half, dtype=jnp.float32) * (-2.0 * math.log(THETA) / HEAD_SIZE))
    angle = (query_index - start).astype(jnp.float32)[:, None] * freq[None, :]
    cosine, sine = jnp.cos(angle)[:, None, :], jnp.sin(angle)[:, None, :]

    def rotated(rows, sign):
        first, second = rows[..., :half], rows[..., half:]
        turn = sign * sine
        return jnp.concatenate(
            [first * cosine - second * turn, second * cosine + first * turn], axis=-1
        )

    inputs = layer_input.astype(jnp.float32)
    normed, norm_back = jax.vjp(rms_norm, inputs, norm_gains[0])
    normed_low = normed.astype(jnp.bfloat16)
    projected = jnp.dot(normed_low, mixing_in, preferred_element_type=jnp.float32)
    heads = projected[:, : query_width + key_width].reshape(token_rows, -1, HEAD_SIZE)
    turned = rotated(heads, 1.0).astype(jnp.bfloat16)
    pairs_mine = jnp.concatenate(
        [
            turned[:, QUERY_HEADS:].reshape(token_rows, key_width),
            projected[:, query_width + key_width :].astype(jnp.bfloat16),
        ],
        axis=1,
    )
    query = (turned[:, :QUERY_HEADS] * jnp.bfloat16(scale)).reshape(token_rows, query_width)
    start_rows = start.reshape(tiles, 1, BLK)

    f32 = jnp.float32
    gathered, pairs, attended_t, attended_low, lse = gather_attend(
        [pack(w_out, ()), pack(w_down, (), D), pack(w_gu, ())],
        query,
        pairs_mine,
        start_rows,
        sizes,
        1,
    )
    expand_matrix = unpack(gathered[2], sizes, w_gu.shape[0]).reshape(D, 2 * FF)
    if whole_rows(w_down.shape[0], D):
        shrink_matrix = gathered[1].reshape(FF, D)
    else:
        shrink_matrix = unpack(gathered[1], sizes, w_down.shape[0]).reshape(FF, D)
    mixing_out = unpack(gathered[0], sizes, w_out.shape[0]).reshape(query_width, D)
    mid = inputs + jnp.dot(attended_low, mixing_out, preferred_element_type=f32)
    normed_two, norm_two_back = jax.vjp(rms_norm, mid, norm_gains[1])
    normed_two_low = normed_two.astype(jnp.bfloat16)
    gate_up = jnp.dot(normed_two_low, expand_matrix, preferred_element_type=f32)
    hidden, hidden_back = jax.vjp(silu_product, gate_up)
    hidden_low = hidden.astype(jnp.bfloat16)
    result = (mid + jnp.dot(hidden_low, shrink_matrix, preferred_element_type=f32)).astype(
        jnp.bfloat16
    )
    grad_down = jnp.einsum("tf,td->fd", hidden_low, cotangent, preferred_element_type=f32)
    d_hidden = jnp.einsum("td,fd->tf", cotangent, shrink_matrix, preferred_element_type=f32)
    d_gate_up = hidden_back(d_hidden)[0].astype(jnp.bfloat16)
    grad_expand = jnp.einsum("td,tf->df", normed_two_low, d_gate_up, preferred_element_type=f32)
    d_normed_two = jnp.einsum("tf,df->td", d_gate_up, expand_matrix, preferred_element_type=f32)
    d_mid_part, grad_gain_two = norm_two_back(d_normed_two)
    d_mid = cotangent.astype(f32) + d_mid_part
    d_branch = d_mid.astype(jnp.bfloat16)
    grad_mixing_out = jnp.einsum("tq,td->qd", attended_low, d_branch, preferred_element_type=f32)
    d_attended = jnp.einsum("td,qd->tq", d_branch, mixing_out, preferred_element_type=f32).astype(
        jnp.bfloat16
    )
    def by_owner(grad):
        return grad.astype(jnp.bfloat16).reshape(sizes + (-1,))

    if whole_rows(w_down.shape[0], D):
        down_sent = grad_down.astype(jnp.bfloat16).reshape(sizes + (-1, D))
    else:
        down_sent = pack(by_owner(grad_down), sizes)
    (gu_mine, down_mine, out_mine), d_query, d_pairs_mine = scatter_attend(
        [pack(by_owner(grad_expand), sizes), down_sent, pack(by_owner(grad_mixing_out), sizes)],
        [query, d_attended, pairs, start_rows, lse, attended_t],
        sizes,
        2,
    )
    d_turned = jnp.concatenate(
        [d_query, d_pairs_mine[:, :key_width]], axis=1
    ).reshape(token_rows, -1, HEAD_SIZE)
    d_projected = jnp.concatenate(
        [rotated(d_turned, -1.0).reshape(token_rows, -1), d_pairs_mine[:, key_width:]], axis=1
    ).astype(jnp.bfloat16)
    grad_mixing_in = jnp.einsum("td,tq->dq", normed_low, d_projected, preferred_element_type=f32)
    d_normed = jnp.einsum("tq,dq->td", d_projected, mixing_in, preferred_element_type=f32)
    d_input_part, grad_gain_one = norm_back(d_normed)
    gains = jnp.stack([grad_gain_one, grad_gain_two])
    qkv_mine, gains_sum = reduce_scatter(
        [pack(by_owner(grad_mixing_in), sizes)], gains, sizes, 3
    )
    return (
        result,
        d_mid + d_input_part,
        unpack(qkv_mine, (), w_qkv.shape[0]),
        unpack(out_mine, (), w_out.shape[0]),
        unpack(gu_mine, (), w_gu.shape[0]),
        unpack(down_mine, (), w_down.shape[0], D),
        gains_sum,
    )


def solution(mesh):
    spread = P(("seq", "dp"))
    rows = P(("seq", "dp"), None)
    return jax.shard_map(
        functools.partial(per_device, grid_sizes(mesh.shape["seq"], mesh.shape["dp"])),
        mesh=mesh,
        in_specs=(rows, spread, spread, spread, spread, P(), P("dp", None), rows),
        out_specs=(rows, rows, spread, spread, spread, spread, P()),
        check_vma=False,
    )
```

```python
import functools
import math

import jax
import jax.numpy as jnp
from jax import lax
from jax.experimental import pallas as pl
from jax.experimental.pallas import tpu as pltpu
from jax.sharding import PartitionSpec as P

D = 576
QUERY_HEADS = 9
KEY_VALUE_HEADS = 3
HEAD_SIZE = 64
FF = 1536
HG = QUERY_HEADS // KEY_VALUE_HEADS

EPS = 1e-05
THETA = 100000.0
MASKED = -1e30
MESH = pl.DeviceIdType.MESH
BLK = 256
VMEM_LIMIT = 48 * 1024 * 1024
ACROSS_LAST, ALONG_Y_LAST = (0, 2, 1), (0, 1, 2)
GATHER_ROUNDS = (0, 1, 2, 3, 3, 2, 2, 1, 2)
SCATTER_ROUNDS = (2, 2, 0, 1, 1, 2, 2, 1, 2)


def rms_norm(value_rows, gain):
    return (
        value_rows
        * lax.rsqrt(jnp.mean(value_rows * value_rows, axis=-1, keepdims=True) + EPS)
        * gain
    )


def layout(lengths_row, index):
    count = lengths_row.shape[0]
    earlier = jnp.arange(count)[:, None] >= jnp.arange(count)[None, :]
    ends = jnp.sum(jnp.where(earlier, lengths_row[None, :], 0), axis=1, dtype=jnp.int32)
    done = ends[None, :] <= index[:, None]
    return jnp.sum(jnp.where(done, lengths_row[None, :], 0), axis=1, dtype=jnp.int32)


def silu_product(gate_up):
    width = gate_up.shape[1] // 2
    return jax.nn.silu(gate_up[:, :width]) * gate_up[:, width:]


def grid_sizes(seq_count, dp_count):
    return (seq_count // 2, 2, dp_count // 2, 2)


def coords():
    seq, dp = lax.axis_index("seq"), lax.axis_index("dp")
    return [seq // 2, seq % 2, dp // 2, dp % 2]


def device_at(coord):
    return (coord[0] * 2 + coord[1], coord[2] * 2 + coord[3])


def moved(me, sizes, axis, step):
    other = list(me)
    other[axis] = lax.rem(me[axis] + step + sizes[axis], sizes[axis])
    return other


def greet(me, sizes):
    barrier = pltpu.get_barrier_semaphore()
    count = 0
    for axis in range(4):
        for step in range(1, sizes[axis]):
            pl.semaphore_signal(
                barrier,
                inc=1,
                device_id=device_at(moved(me, sizes, axis, step)),
                device_id_type=MESH,
            )
            count += 1
    pl.semaphore_wait(barrier, count)


class Piece:
    def __init__(self, array, shape, order):
        self.array, self.order = array, order
        self.rows, self.columns = shape[0][1], shape[1][1]
        self.at = tuple(pl.ds(first, size) for first, size in shape)


def pieces_of(shards, orders, cuts):
    pieces = []
    for array, shard in enumerate(shards):
        rows, columns = shard.shape[-2:]
        cut = rows // 32 * 16 if cuts[array] and rows >= 32 else 0
        spans = [(0, cut), (cut, rows - cut)] if cut else [(0, rows)]
        for number, span in enumerate(spans):
            order = orders[array][number % len(orders[array])]
            pieces.append(Piece(array, (span, (0, columns)), order))
    return pieces


def gather_steps(me, sizes, pieces, shards, outs, send, recv, core_send, core_recv, local):
    parts = len(pieces)
    started = []
    for array in range(len(shards)):
        own = pltpu.make_async_copy(
            shards[array], outs[array].at[me[0], me[1], me[2], me[3]], local.at[array]
        )
        own.start()
        started.append(own)

    def region(part, held, where):
        piece = pieces[part]
        lead = tuple(slice(None) if a in held else where[a] for a in range(3)) + (where[3],)
        return outs[piece.array].at[lead + piece.at]

    def copy(part, phase, step, arriving=False):
        order = pieces[part].order
        where = moved(me, sizes, order[phase], -step) if arriving else me
        block = region(part, order[:phase], where)
        source = block
        if phase == 0 and not arriving:
            source = shards[pieces[part].array].at[pieces[part].at]
        return pltpu.make_async_remote_copy(
            src_ref=source,
            dst_ref=block,
            send_sem=send.at[part, phase, step],
            recv_sem=recv.at[part, phase, step],
            device_id=device_at(moved(me, sizes, order[phase], step)),
            device_id_type=MESH,
        )

    def to_core(part, slot, held, where, arriving=False):
        there = moved(where, sizes, 3, 1) if arriving else where
        block = region(part, held, there)
        return pltpu.make_async_remote_copy(
            src_ref=block,
            dst_ref=block,
            send_sem=core_send.at[part, slot],
            recv_sem=core_recv.at[part, slot],
            device_id=device_at(moved(me, sizes, 3, 1)),
            device_id_type=MESH,
        )

    for part in range(parts):
        for step in range(1, sizes[pieces[part].order[0]]):
            copy(part, 0, step).start()
    for own in started:
        own.wait()
    yield
    pending = []
    turns = [(phase, part) for phase in range(3) for part in range(parts)]
    for phase, part in sorted(turns, key=lambda turn: (3 * turn[0] + turn[1], turn[0])):
        order = pieces[part].order
        held = order[:phase]
        for step in range(1, sizes[order[phase]]):
            copy(part, phase, step, arriving=True).wait_recv()
            if phase == 2:
                origin = moved(me, sizes, order[phase], -step)
                to_core(part, step, held, origin).start()
                pending.append((part, step, held, origin))
        if phase < 2:
            for step in range(1, sizes[order[phase + 1]]):
                copy(part, phase + 1, step).start()
        if phase == 1:
            to_core(part, 0, order[:2], me).start()
            pending.append((part, 0, order[:2], me))
        yield
    for part in range(parts):
        for phase in range(3):
            for step in range(1, sizes[pieces[part].order[phase]]):
                copy(part, phase, step).wait_send()
    for part, slot, held, origin in pending:
        to_core(part, slot, held, origin).wait_send()
        to_core(part, slot, held, origin, arriving=True).wait_recv()


def gather_semaphores(arrays, parts, most):
    return [
        pltpu.SemaphoreType.DMA((parts, 3, most)),
        pltpu.SemaphoreType.DMA((parts, 3, most)),
        pltpu.SemaphoreType.DMA((parts, most)),
        pltpu.SemaphoreType.DMA((parts, most)),
        pltpu.SemaphoreType.DMA((arrays,)),
    ]


def gather_kernel(sizes, pieces, arrays, *refs):
    me = coords()
    greet(me, sizes)
    for _ in gather_steps(
        me, sizes, pieces, refs[:arrays], refs[arrays : 2 * arrays], *refs[2 * arrays :]
    ):
        pass


def all_gather(shards, sizes, ident):
    arrays = len(shards)
    pieces = pieces_of(shards, [(ALONG_Y_LAST, ACROSS_LAST)] * arrays, [True] * arrays)
    return pl.pallas_call(
        functools.partial(gather_kernel, sizes, pieces, arrays),
        out_shape=[jax.ShapeDtypeStruct(sizes + s.shape, s.dtype) for s in shards],
        in_specs=[pl.BlockSpec(memory_space=pltpu.VMEM)] * arrays,
        out_specs=[pl.BlockSpec(memory_space=pltpu.VMEM)] * arrays,
        scratch_shapes=gather_semaphores(arrays, len(pieces), max(sizes)),
        compiler_params=pltpu.CompilerParams(
            collective_id=ident, has_side_effects=True, vmem_limit_bytes=VMEM_LIMIT
        ),
        cost_estimate=pl.CostEstimate(flops=0, bytes_accessed=60_000_000, transcendentals=0),
    )(*shards)


def scatter_order(piece):
    return (3,) + tuple(reversed(piece.order))


def scatter_kernel(sizes, pieces, arrays, with_gains, *refs):
    me = coords()
    greet(me, sizes)
    for _ in scatter_steps(me, sizes, pieces, arrays, with_gains, *refs):
        pass


def scatter_steps(me, sizes, pieces, arrays, with_gains, *refs):
    parts = len(pieces)
    n_in = arrays + with_gains
    grads, outs = refs[:n_in], refs[n_in : 2 * n_in]
    rest = list(refs[2 * n_in :])
    arrived = [[rest.pop(0) for _ in range(4)] for _ in range(parts)]
    totals = [[rest.pop(0) for _ in range(3)] for _ in range(parts)]
    if with_gains:
        gain_arrived, gain_total = rest.pop(0), rest.pop(0)
        gain_send, gain_recv = rest.pop(0), rest.pop(0)
    send, recv = rest

    def held_at(part, phase, index):
        order = scatter_order(pieces[part])
        left = sorted(set(range(4)) - set(order[:phase]))
        lead = tuple(index if a == order[phase] else slice(None) for a in left)
        if phase == 0:
            return grads[pieces[part].array].at[lead + pieces[part].at]
        return totals[part][phase - 1].at[lead]

    def copy(part, phase, step):
        axis = scatter_order(pieces[part])[phase]
        target = moved(me, sizes, axis, step)
        return pltpu.make_async_remote_copy(
            src_ref=held_at(part, phase, target[axis]),
            dst_ref=arrived[part][phase].at[step - 1],
            send_sem=send.at[part, phase, step],
            recv_sem=recv.at[part, phase, step],
            device_id=device_at(target),
            device_id_type=MESH,
        )

    def add(part, phase):
        piece = pieces[part]
        axis = scatter_order(piece)[phase]
        mine = held_at(part, phase, me[axis])
        lead = mine.shape[:-2]
        others = arrived[part][phase]

        def total_at(place):
            if phase < 3 and sizes[axis] == 2:
                return mine[place] + others[(0,) + place]
            value = mine[place].astype(jnp.float32)
            for step in range(1, sizes[axis]):
                value = value + others[(step - 1,) + place].astype(jnp.float32)
            return value

        if phase == 3:
            outs[piece.array][piece.at] = total_at((slice(None), slice(None)))
            return
        target = totals[part][phase]

        def body(flat, carry):
            place = []
            for size in reversed(lead):
                place.insert(0, lax.rem(flat, size))
                flat = flat // size
            place = tuple(place) + (slice(None), slice(None))
            target[place] = total_at(place).astype(target.dtype)
            return carry

        lax.fori_loop(0, math.prod(lead), body, 0)

    def gain_copy(phase, step):
        return pltpu.make_async_remote_copy(
            src_ref=gain_total.at[phase],
            dst_ref=gain_arrived.at[phase, step - 1],
            send_sem=gain_send.at[phase, step],
            recv_sem=gain_recv.at[phase, step],
            device_id=device_at(moved(me, sizes, phase, step)),
            device_id_type=MESH,
        )

    def start(phase, part):
        for step in range(1, sizes[scatter_order(pieces[part])[phase]]):
            copy(part, phase, step).start()

    def gain_start(phase):
        for step in range(1, sizes[phase]):
            gain_copy(phase, step).start()

    def gain_turn(phase):
        value = gain_total[phase]
        for step in range(1, sizes[phase]):
            gain_copy(phase, step).wait_recv()
        slots = [value] + [gain_arrived[phase, s - 1] for s in range(1, sizes[phase])]
        value = sum(slots[1:], slots[0])
        if phase < 3:
            gain_total[phase + 1] = value
            gain_start(phase + 1)
        else:
            outs[arrays][...] = value

    for part in range(parts):
        start(0, part)
    if with_gains:
        gain_total[0] = grads[arrays][...]
        gain_start(0)
    yield
    turns = [(phase, part) for phase in range(4) for part in range(parts + with_gains)]

    def rank(turn):
        phase, part = turn
        return (0, part, 0) if phase == 0 else (1, phase + part, -phase)

    for phase, part in sorted(turns, key=rank):
        if part == parts:
            gain_turn(phase)
            continue
        for step in range(1, sizes[scatter_order(pieces[part])[phase]]):
            copy(part, phase, step).wait_recv()
        add(part, phase)
        if phase < 3:
            start(phase + 1, part)
        yield
    for phase in range(4):
        for part in range(parts):
            for step in range(1, sizes[scatter_order(pieces[part])[phase]]):
                copy(part, phase, step).wait_send()
        if with_gains:
            for step in range(1, sizes[phase]):
                gain_copy(phase, step).wait_send()


def scatter_buffers(pieces, sizes):
    scratch = []
    for piece in pieces:
        left = [0, 1, 2, 3]
        for axis in scatter_order(piece):
            left.remove(axis)
            shape = (sizes[axis] - 1,) + tuple(sizes[a] for a in left) + (piece.rows, piece.columns)
            scratch.append(pltpu.VMEM(shape, jnp.bfloat16))
    for piece in pieces:
        left = [0, 1, 2, 3]
        for axis in scatter_order(piece)[:3]:
            left.remove(axis)
            shape = tuple(sizes[a] for a in left) + (piece.rows, piece.columns)
            scratch.append(pltpu.VMEM(shape, jnp.bfloat16))
    return scratch


def reduce_scatter(grads, gains, sizes, ident):
    arrays = len(grads)
    most = max(sizes)
    pieces = pieces_of(grads, [(ALONG_Y_LAST, ACROSS_LAST)] * arrays, [True] * arrays)
    scratch = scatter_buffers(pieces, sizes)
    outs = [jax.ShapeDtypeStruct(g.shape[4:], jnp.float32) for g in grads]
    args = list(grads)
    if gains is not None:
        args.append(gains)
        outs.append(jax.ShapeDtypeStruct(gains.shape, jnp.float32))
        scratch += [
            pltpu.VMEM((4, most - 1) + gains.shape, jnp.float32),
            pltpu.VMEM((4,) + gains.shape, jnp.float32),
            pltpu.SemaphoreType.DMA((4, most)),
            pltpu.SemaphoreType.DMA((4, most)),
        ]
    scratch += [pltpu.SemaphoreType.DMA((len(pieces), 4, most))] * 2
    return pl.pallas_call(
        functools.partial(scatter_kernel, sizes, pieces, arrays, int(gains is not None)),
        out_shape=outs,
        in_specs=[pl.BlockSpec(memory_space=pltpu.VMEM)] * len(args),
        out_specs=[pl.BlockSpec(memory_space=pltpu.VMEM)] * len(outs),
        scratch_shapes=scratch,
        compiler_params=pltpu.CompilerParams(
            collective_id=ident, has_side_effects=True, vmem_limit_bytes=VMEM_LIMIT
        ),
        cost_estimate=pl.CostEstimate(flops=0, bytes_accessed=60_000_000, transcendentals=0),
    )(*args)


def padded_rows(count):
    return -(-count // 2048) * 16


def whole_rows(size, width):
    return size % (16 * width) == 0


def pack(flat, lead, width=None):
    size = flat.shape[-1]
    if width and whole_rows(size, width):
        return flat.reshape(lead + (-1, width))
    rows = padded_rows(size)
    none = [(0, 0)] * len(lead)
    if lead and size % 128 == 0:
        flat = flat.reshape(lead + (size // 128, 128))
        return jnp.pad(flat, none + [(0, rows - size // 128), (0, 0)])
    return jnp.pad(flat, none + [(0, rows * 128 - size)]).reshape(lead + (rows, 128))


def unpack(packed, lead, size, width=None):
    if width and whole_rows(size, width):
        return packed.reshape(lead + (size,))
    if size % 128 == 0:
        return packed[..., : size // 128, :].reshape(lead + (size,))
    return packed.reshape(lead + (-1,))[..., :size]


def dot_rows(left, right):
    return lax.dot_general(left, right, (((1,), (1,)), ((), ())), preferred_element_type=jnp.float32)


def dot_columns(left, right):
    return lax.dot_general(left, right, (((0,), (0,)), ((), ())), preferred_element_type=jnp.float32)


def head_columns(head):
    first = head * HEAD_SIZE
    second = first + KEY_VALUE_HEADS * HEAD_SIZE
    return slice(first, first + HEAD_SIZE), slice(second, second + HEAD_SIZE)


def head_columns(head):
    first = head * HEAD_SIZE
    second = first + KEY_VALUE_HEADS * HEAD_SIZE
    return slice(first, first + HEAD_SIZE), slice(second, second + HEAD_SIZE)


def blocks_of(offset, window, tile, tiles):
    return (tile if offset == window else 0), (tile + 1 if offset == 0 else tiles)


def query_part(head, within):
    first = (head * HG + within) * HEAD_SIZE
    return slice(first, first + HEAD_SIZE)


def stack_heads(rows_ref, stacked_ref, tile):
    for head in range(KEY_VALUE_HEADS):
        for within in range(HG):
            stacked_ref[head, tile, pl.ds(within * BLK, BLK), :] = rows_ref[
                pl.ds(tile * BLK, BLK), query_part(head, within)
            ]


def lay_heads(columns):
    return jnp.concatenate(
        [
            columns[head][:, within * BLK : (within + 1) * BLK].T
            for head in range(KEY_VALUE_HEADS)
            for within in range(HG)
        ],
        axis=1,
    )


def turn_back(columns, cosine, sine):
    first, second = columns[: HEAD_SIZE // 2], columns[HEAD_SIZE // 2 :]
    return jnp.concatenate([first * cosine + second * sine, second * cosine - first * sine], axis=0)


def places(place, tile, tiles, start_ref):
    lane = lax.broadcasted_iota(jnp.int32, (1, HG * BLK), 1)
    index = (place * tiles + tile) * BLK + lax.rem(lane, BLK)
    return index, jnp.concatenate([start_ref[tile]] * HG, axis=1)


def neighbour(me, sizes, axis, step):
    return device_at(moved(me, sizes, axis, step))


class PairFlow:
    def __init__(self, me, sizes, mine, slots, chain_send, cross_send, recv):
        self.me, self.sizes, self.mine, self.slots = me, sizes, mine, slots
        self.chain_send, self.cross_send, self.recv = chain_send, cross_send, recv
        self.reach = sizes[0] // 2

    def chain(self, j):
        return pltpu.make_async_remote_copy(
            src_ref=self.mine if j == 0 else self.slots.at[2 * j],
            dst_ref=self.slots.at[2 * j + 2],
            send_sem=self.chain_send.at[j],
            recv_sem=self.recv.at[2 * j + 2],
            device_id=neighbour(self.me, self.sizes, 0, 1),
            device_id_type=MESH,
        )

    def cross(self, j, side):
        slot = 2 * j + 1 if side == 0 else 2 * j - 1
        return pltpu.make_async_remote_copy(
            src_ref=self.mine if j == 0 else self.slots.at[2 * j],
            dst_ref=self.slots.at[slot],
            send_sem=self.cross_send.at[j],
            recv_sem=self.recv.at[slot],
            device_id=neighbour(self.me, self.sizes, 1, 1),
            device_id_type=MESH,
        )

    def each(self, j, act):
        there = self.me[0] >= j
        if j < self.reach:

            @pl.when(there & (self.me[0] + 1 < self.sizes[0]))
            def _():
                act(self.chain(j))

            @pl.when(there & (self.me[1] == 0))
            def _():
                act(self.cross(j, 0))

        if j > 0:

            @pl.when(there & (self.me[1] == 1))
            def _():
                act(self.cross(j, 1))

    def forward(self, j):
        self.each(j, lambda copy: copy.start())

    def finish(self, j):
        self.each(j, lambda copy: copy.wait_send())

    def arrive(self, offset):
        block = self.slots.at[offset]
        pltpu.make_async_remote_copy(
            src_ref=block,
            dst_ref=block,
            send_sem=self.cross_send.at[0],
            recv_sem=self.recv.at[offset],
            device_id=neighbour(self.me, self.sizes, 1, 1),
            device_id_type=MESH,
        ).wait_recv()


def gather_attend_kernel(sizes, pieces, parts, tiles, *refs):
    shards, refs = refs[:parts], refs[parts:]
    (rows_ref, mine_ref, start_ref), refs = refs[:3], refs[3:]
    outs, refs = refs[:parts], refs[parts:]
    slots, o_ref, out_ref, lse_ref, total_ref, q_ref = refs[:6]
    semaphores, (chain_send, cross_send, recv, own_sem) = refs[6:11], refs[11:]
    me = coords()
    place = me[0] * 2 + me[1]
    window = sizes[0]
    greet(me, sizes)
    flow = PairFlow(me, sizes, mine_ref, slots, chain_send, cross_send, recv)
    flow.forward(0)
    own = pltpu.make_async_copy(mine_ref, slots.at[0], own_sem)
    own.start()
    weights = gather_steps(me, sizes, pieces, shards, outs, *semaphores)
    token_rows = tiles * BLK
    for tile in range(tiles):
        stack_heads(rows_ref, q_ref, tile)

    def unit(offset, tile, head):
        key_part, value_part = head_columns(head)
        low, high = blocks_of(offset, window, tile, tiles)
        q = q_ref[head, tile]
        index, start = places(place, tile, tiles, start_ref)
        width = q.shape[0]
        held = mine_ref if offset == 0 else slots.at[offset]
        base = (place - offset) * token_rows

        def step(block, carry):
            highest, total, acc = carry
            first = pl.multiple_of(block * BLK, BLK)
            rows = pl.ds(first, BLK)
            s = dot_rows(held[rows, key_part], q)
            row = base + first + lax.broadcasted_iota(jnp.int32, s.shape, 0)
            s = jnp.where((row <= index) & (row >= start), s, MASKED)
            new = jnp.maximum(highest, jnp.max(s, axis=0, keepdims=True))
            p = jnp.exp(s - new)
            fade = jnp.exp(highest - new)
            total = total * fade + jnp.sum(p, axis=0, keepdims=True)
            acc = acc * fade + dot_columns(held[rows, value_part], p.astype(jnp.bfloat16))
            return new, total, acc

        if offset == 0:
            carry = (
                jnp.full((1, width), MASKED, jnp.float32),
                jnp.zeros((1, width), jnp.float32),
                jnp.zeros((HEAD_SIZE, width), jnp.float32),
            )
        else:
            carry = lse_ref[head, tile], total_ref[head, tile], o_ref[head, tile]
        highest, total, acc = lax.fori_loop(low, high, step, carry)
        lse_ref[head, tile], total_ref[head, tile], o_ref[head, tile] = highest, total, acc

    slot = 0

    def attend(offset, tile):
        nonlocal slot

        @pl.when(place >= offset)
        def _():
            for head in range(KEY_VALUE_HEADS):
                unit(offset, tile, head)

        for _ in range(GATHER_ROUNDS[slot] if slot < len(GATHER_ROUNDS) else 0):
            next(weights)
        slot += 1

    def receive(offset):
        @pl.when(place >= offset)
        def _():
            flow.arrive(offset)

        if offset % 2 == 0:
            flow.forward(offset // 2)

    for j in range(flow.reach + 1):
        for offset in (0,) if j == 0 else (2 * j, 2 * j - 1):
            if offset % 2:
                receive(offset)
            for tile in range(tiles):
                if tile == tiles - 1 and offset % 2 and j < flow.reach:
                    receive(2 * j + 2)
                attend(offset, tile)
        if j == 0:
            receive(2)
    for tile, head in [(t, h) for t in range(tiles) for h in range(KEY_VALUE_HEADS)]:
        total = total_ref[head, tile]
        o_ref[head, tile] = o_ref[head, tile] / total
        lse_ref[head, tile] = lse_ref[head, tile] + jnp.log(total)
    for tile in range(tiles):
        laid = lay_heads([o_ref[head, tile] for head in range(KEY_VALUE_HEADS)])
        out_ref[pl.ds(tile * BLK, BLK), :] = laid.astype(out_ref.dtype)
    for _ in weights:
        pass
    for j in range(flow.reach + 1):
        flow.finish(j)
    own.wait()


def gather_attend(shards, query, pairs_mine, start_rows, sizes, ident):
    parts = len(shards)
    pieces = pieces_of(shards, [(ALONG_Y_LAST,), (ALONG_Y_LAST, ACROSS_LAST), (ALONG_Y_LAST, ACROSS_LAST)], [False, True, True])
    kvh, tiles, width = KEY_VALUE_HEADS, query.shape[0] // BLK, HG * BLK
    window = sizes[0]
    f32 = jnp.float32
    whole = pl.BlockSpec(memory_space=pltpu.VMEM)
    column = jax.ShapeDtypeStruct((kvh, tiles, HEAD_SIZE, width), f32)
    line = jax.ShapeDtypeStruct((kvh, tiles, 1, width), f32)
    out_shape = [jax.ShapeDtypeStruct(sizes + s.shape, s.dtype) for s in shards]
    out_shape += [
        jax.ShapeDtypeStruct((window + 1,) + pairs_mine.shape, pairs_mine.dtype),
        column,
        jax.ShapeDtypeStruct(query.shape, query.dtype),
        line,
    ]
    dma = pltpu.SemaphoreType.DMA
    results = pl.pallas_call(
        functools.partial(gather_attend_kernel, sizes, pieces, parts, tiles),
        out_shape=out_shape,
        in_specs=[whole] * (parts + 3),
        out_specs=[whole] * len(out_shape),
        scratch_shapes=[
            pltpu.VMEM(line.shape, f32),
            pltpu.VMEM((kvh, tiles, width, HEAD_SIZE), query.dtype),
        ]
        + gather_semaphores(parts, len(pieces), max(sizes))
        + [dma((window // 2 + 1,)), dma((window // 2 + 1,)), dma((window + 1,)), dma],
        compiler_params=pltpu.CompilerParams(
            collective_id=ident, has_side_effects=True, vmem_limit_bytes=VMEM_LIMIT
        ),
        cost_estimate=pl.CostEstimate(
            flops=10_000_000_000, bytes_accessed=60_000_000, transcendentals=0
        ),
    )(*shards, query, pairs_mine, start_rows)
    return results[:parts], *results[parts:]


class SumFlow:
    def __init__(self, me, sizes, partial, crossed, chained, chain_send, cross_send, chain_recv, cross_recv):
        self.me, self.sizes, self.partial = me, sizes, partial
        self.crossed, self.chained = crossed, chained
        self.chain_send, self.cross_send = chain_send, cross_send
        self.chain_recv, self.cross_recv = chain_recv, cross_recv
        self.reach = sizes[0] // 2

    def chain(self, j):
        return pltpu.make_async_remote_copy(
            src_ref=self.partial.at[2 * j],
            dst_ref=self.chained.at[j - 1],
            send_sem=self.chain_send.at[j],
            recv_sem=self.chain_recv.at[j - 1],
            device_id=neighbour(self.me, self.sizes, 0, -1),
            device_id_type=MESH,
        )

    def cross(self, offset, side):
        j = (offset + 1) // 2 if side == 0 else offset // 2
        return pltpu.make_async_remote_copy(
            src_ref=self.partial.at[offset],
            dst_ref=self.crossed.at[j],
            send_sem=self.cross_send.at[offset // 2],
            recv_sem=self.cross_recv.at[j],
            device_id=neighbour(self.me, self.sizes, 1, 1),
            device_id_type=MESH,
        )

    def each_cross(self, offset, act):
        for side in range(2):

            @pl.when((self.me[1] == side) & (self.me[0] * 2 + side >= offset))
            def _(side=side):
                act(self.cross(offset, side))

    def has_cross(self, j):
        side = self.me[1]
        if j == 0:
            return side == 0
        if j == self.reach:
            return (side == 1) & (self.me[0] >= j)
        return self.me[0] >= j

    def has_chain(self, j):
        return (self.me[0] >= j) & (self.me[0] + 1 < self.sizes[0])

    def cross_arrive(self, j):
        pltpu.make_async_remote_copy(
            src_ref=self.crossed.at[j],
            dst_ref=self.crossed.at[j],
            send_sem=self.cross_send.at[0],
            recv_sem=self.cross_recv.at[j],
            device_id=neighbour(self.me, self.sizes, 1, 1),
            device_id_type=MESH,
        ).wait_recv()

    def chain_arrive(self, j):
        pltpu.make_async_remote_copy(
            src_ref=self.chained.at[j],
            dst_ref=self.chained.at[j],
            send_sem=self.chain_send.at[0],
            recv_sem=self.chain_recv.at[j],
            device_id=neighbour(self.me, self.sizes, 0, -1),
            device_id_type=MESH,
        ).wait_recv()


def scatter_attend_kernel(sizes, pieces, parts, tiles, *refs):
    grads, refs = refs[:parts], refs[parts:]
    (rows_ref, do_rows_ref, slots, start_ref, lse_ref, o_ref), refs = refs[:6], refs[6:]
    (cos_ref, sin_ref), refs = refs[:2], refs[2:]
    outs, refs = refs[:parts], refs[parts:]
    d_projected_ref, refs = refs[0], refs[1:]
    (dq_rows_ref, dkv_ref), refs = refs[:2], refs[2:]
    (dq_ref, q_ref, do_ref, delta_ref), refs = refs[:4], refs[4:]
    accs, refs = refs[: 2 * KEY_VALUE_HEADS], refs[2 * KEY_VALUE_HEADS :]
    flow_refs, scatter_refs = refs[:7], refs[7:]
    me = coords()
    place = me[0] * 2 + me[1]
    window = sizes[0]
    greet(me, sizes)
    flow = SumFlow(me, sizes, *flow_refs)
    partial, crossed, chained = flow_refs[:3]
    weights = scatter_steps(me, sizes, pieces, parts, 0, *grads, *outs, *scatter_refs)
    next(weights)
    token_rows = tiles * BLK
    dq_ref[...] = jnp.zeros_like(dq_ref)
    for tile in range(tiles):
        stack_heads(rows_ref, q_ref, tile)
        stack_heads(do_rows_ref, do_ref, tile)
        for head in range(KEY_VALUE_HEADS):
            columns = do_ref[head, tile].astype(jnp.float32).T
            delta_ref[head, tile] = jnp.sum(columns * o_ref[head, tile], axis=0, keepdims=True)

    def unit(offset, tile, head):
        key_part, value_part = head_columns(head)
        low, high = blocks_of(offset, window, tile, tiles)
        q, do = q_ref[head, tile], do_ref[head, tile]
        index, start = places(place, tile, tiles, start_ref)
        lse, delta = lse_ref[head, tile], delta_ref[head, tile]
        dk_acc, dv_acc = accs[head], accs[KEY_VALUE_HEADS + head]
        base = (place - offset) * token_rows

        def step(block, dq):
            first = pl.multiple_of(block * BLK, BLK)
            rows = pl.ds(first, BLK)
            k = slots[offset, rows, key_part]
            s = dot_rows(k, q)
            dp = dot_rows(slots[offset, rows, value_part], do)
            row = base + first + lax.broadcasted_iota(jnp.int32, s.shape, 0)
            s = jnp.where((row <= index) & (row >= start), s - lse, MASKED)
            p = jnp.exp(s)
            ds = (p * (dp - delta)).astype(jnp.bfloat16)
            dv_acc[rows, :] += jnp.dot(p.astype(jnp.bfloat16), do, preferred_element_type=jnp.float32)
            dk_acc[rows, :] += jnp.dot(ds, q, preferred_element_type=jnp.float32)
            return dq + dot_columns(k, ds)

        dq_ref[head, tile] = lax.fori_loop(low, high, step, dq_ref[head, tile])

    slot = 0

    def collect(offset):
        nonlocal slot

        for tile in range(tiles):

            @pl.when(place >= offset)
            def _(tile=tile):
                if tile == 0:
                    for acc in accs:
                        acc[...] = jnp.zeros_like(acc)
                for head in range(KEY_VALUE_HEADS):
                    unit(offset, tile, head)

            if tile < tiles - 1:
                progress()

    def progress():
        nonlocal slot
        for _ in range(SCATTER_ROUNDS[slot] if slot < len(SCATTER_ROUNDS) else 0):
            next(weights)
        slot += 1

    def summed(rows):
        return jnp.concatenate([acc[rows, :] for acc in accs], axis=1)

    def over_rows(body):
        def run(block, carry):
            body(pl.ds(pl.multiple_of(block * BLK, BLK), BLK))
            return carry

        lax.fori_loop(0, tiles, run, 0)

    def keep(offset):
        def body(rows):
            partial[offset, rows, :] = summed(rows).astype(partial.dtype)

        over_rows(body)

    def fold(j, source):
        def body(rows):
            partial[2 * j, rows, :] = (
                partial[2 * j, rows, :].astype(jnp.float32) + source[j, rows, :].astype(jnp.float32)
            ).astype(partial.dtype)

        over_rows(body)

    def fold_own(source):
        def body(rows):
            dkv_ref[rows, :] += source[0, rows, :].astype(jnp.float32)

        over_rows(body)

    for j in reversed(range(1, flow.reach + 1)):
        odd = 2 * j - 1

        collect(odd)

        @pl.when(place >= odd)
        def _(odd=odd):
            keep(odd)

        flow.each_cross(odd, lambda copy: copy.start())
        progress()
        collect(2 * j)

        @pl.when(me[0] >= j)
        def _(j=j):
            keep(2 * j)

        @pl.when(flow.has_cross(j))
        def _(j=j):
            flow.cross_arrive(j)
            fold(j, crossed)

        if j < flow.reach:

            @pl.when(flow.has_chain(j))
            def _(j=j):
                flow.chain_arrive(j)
                fold(j, chained)

        @pl.when(me[0] >= j)
        def _(j=j):
            flow.chain(j).start()

        progress()
    collect(0)

    def first(rows):
        dkv_ref[rows, :] = summed(rows)

    over_rows(first)
    progress()

    for tile in range(tiles):
        cosine, sine = (jnp.concatenate([r[tile]] * HG, axis=1) for r in (cos_ref, sin_ref))
        scale = 1.0 / math.sqrt(HEAD_SIZE)
        laid = lay_heads(
            [turn_back(dq_ref[h, tile] * scale, cosine, sine) for h in range(KEY_VALUE_HEADS)]
        )
        dq_rows_ref[pl.ds(tile * BLK, BLK), :] = laid.astype(dq_rows_ref.dtype)

    @pl.when(flow.has_cross(0))
    def _():
        flow.cross_arrive(0)
        fold_own(crossed)

    @pl.when(flow.has_chain(0))
    def _():
        flow.chain_arrive(0)
        fold_own(chained)

    for tile in range(tiles):
        rows = pl.ds(tile * BLK, BLK)
        keys = [
            turn_back(dkv_ref[rows, head_columns(h)[0]].T, cos_ref[tile], sin_ref[tile]).T
            for h in range(KEY_VALUE_HEADS)
        ]
        pairs = jnp.concatenate(keys + [dkv_ref[rows, KEY_VALUE_HEADS * HEAD_SIZE :]], axis=1)
        d_projected_ref[rows, :] = jnp.concatenate(
            [dq_rows_ref[rows, :], pairs.astype(jnp.bfloat16)], axis=1
        )

    for _ in weights:
        pass
    for j in range(1, flow.reach + 1):
        flow.each_cross(2 * j - 1, lambda copy: copy.wait_send())

        @pl.when(me[0] >= j)
        def _(j=j):
            flow.chain(j).wait_send()


def scatter_attend(grads, arrays, sizes, ident):
    parts = len(grads)
    pieces = pieces_of(grads, [(ALONG_Y_LAST, ACROSS_LAST), (ALONG_Y_LAST,), (ALONG_Y_LAST,)], [True, False, False])
    token_rows = arrays[0].shape[0]
    kvh, tiles, width = KEY_VALUE_HEADS, token_rows // BLK, HG * BLK
    window, reach = sizes[0], sizes[0] // 2
    pair_shape = arrays[2].shape[1:]
    f32 = jnp.float32
    whole = pl.BlockSpec(memory_space=pltpu.VMEM)
    out_shape = [jax.ShapeDtypeStruct(g.shape[4:], f32) for g in grads]
    out_shape += [
        jax.ShapeDtypeStruct((token_rows, arrays[0].shape[1] + pair_shape[1]), jnp.bfloat16)
    ]
    dma = pltpu.SemaphoreType.DMA
    scratch = [
        pltpu.VMEM(arrays[0].shape, jnp.bfloat16),
        pltpu.VMEM(pair_shape, f32),
        pltpu.VMEM((kvh, tiles, HEAD_SIZE, width), f32),
        pltpu.VMEM((kvh, tiles, width, HEAD_SIZE), jnp.bfloat16),
        pltpu.VMEM((kvh, tiles, width, HEAD_SIZE), jnp.bfloat16),
        pltpu.VMEM((kvh, tiles, 1, width), f32),
    ]
    scratch += [pltpu.VMEM((pair_shape[0], HEAD_SIZE), f32)] * (2 * kvh)
    scratch += [
        pltpu.VMEM((window + 1,) + pair_shape, jnp.bfloat16),
        pltpu.VMEM((reach + 1,) + pair_shape, jnp.bfloat16),
        pltpu.VMEM((reach,) + pair_shape, jnp.bfloat16),
        dma((reach + 1,)),
        dma((reach + 1,)),
        dma((reach,)),
        dma((reach + 1,)),
    ]
    scratch += scatter_buffers(pieces, sizes) + [dma((len(pieces), 4, max(sizes)))] * 2
    results = pl.pallas_call(
        functools.partial(scatter_attend_kernel, sizes, pieces, parts, tiles),
        out_shape=out_shape,
        in_specs=[whole] * (parts + len(arrays)),
        out_specs=[whole] * len(out_shape),
        scratch_shapes=scratch,
        compiler_params=pltpu.CompilerParams(
            collective_id=ident, has_side_effects=True, vmem_limit_bytes=VMEM_LIMIT
        ),
        cost_estimate=pl.CostEstimate(
            flops=25_000_000_000, bytes_accessed=60_000_000, transcendentals=0
        ),
    )(*grads, *arrays)
    return results[:parts], results[parts]


def per_device(sizes, layer_input, w_qkv, w_out, w_gu, w_down, norm_gains, lengths, cotangent):
    token_rows = layer_input.shape[0]
    query_width = QUERY_HEADS * HEAD_SIZE
    key_width = KEY_VALUE_HEADS * HEAD_SIZE
    scale = 1.0 / math.sqrt(HEAD_SIZE)
    tiles = token_rows // BLK

    (qkv_all,) = all_gather([pack(w_qkv, ())], sizes, 0)
    mixing_in = unpack(qkv_all, sizes, w_qkv.shape[0]).reshape(D, -1)

    query_index = lax.axis_index("seq") * token_rows + jnp.arange(token_rows, dtype=jnp.int32)
    start = layout(lengths[0], query_index)
    half = HEAD_SIZE // 2
    freq = jnp.exp(jnp.arange(half, dtype=jnp.float32) * (-2.0 * math.log(THETA) / HEAD_SIZE))
    angle = (query_index - start).astype(jnp.float32)[:, None] * freq[None, :]
    turns = (query_index - start).astype(jnp.float32).reshape(tiles, 1, BLK) * freq[:, None]
    cosine, sine = jnp.cos(angle)[:, None, :], jnp.sin(angle)[:, None, :]

    def rotated(rows):
        first, second = rows[..., :half], rows[..., half:]
        return jnp.concatenate(
            [first * cosine - second * sine, second * cosine + first * sine], axis=-1
        )

    inputs = layer_input.astype(jnp.float32)
    normed, norm_back = jax.vjp(rms_norm, inputs, norm_gains[0])
    normed_low = normed.astype(jnp.bfloat16)
    projected = jnp.dot(normed_low, mixing_in, preferred_element_type=jnp.float32)
    heads = projected[:, : query_width + key_width].reshape(token_rows, -1, HEAD_SIZE)
    turned = rotated(heads).astype(jnp.bfloat16)
    pairs_mine = jnp.concatenate(
        [
            turned[:, QUERY_HEADS:].reshape(token_rows, key_width),
            projected[:, query_width + key_width :].astype(jnp.bfloat16),
        ],
        axis=1,
    )
    query = (turned[:, :QUERY_HEADS] * jnp.bfloat16(scale)).reshape(token_rows, query_width)
    start_rows = start.reshape(tiles, 1, BLK)

    f32 = jnp.float32
    gathered, pairs, attended_t, attended_low, lse = gather_attend(
        [pack(w_out, ()), pack(w_down, (), D), pack(w_gu, ())],
        query,
        pairs_mine,
        start_rows,
        sizes,
        1,
    )
    expand_matrix = unpack(gathered[2], sizes, w_gu.shape[0]).reshape(D, 2 * FF)
    if whole_rows(w_down.shape[0], D):
        shrink_matrix = gathered[1].reshape(FF, D)
    else:
        shrink_matrix = unpack(gathered[1], sizes, w_down.shape[0]).reshape(FF, D)
    mixing_out = unpack(gathered[0], sizes, w_out.shape[0]).reshape(query_width, D)
    mid = inputs + jnp.dot(attended_low, mixing_out, preferred_element_type=f32)
    normed_two, norm_two_back = jax.vjp(rms_norm, mid, norm_gains[1])
    normed_two_low = normed_two.astype(jnp.bfloat16)
    gate_up = jnp.dot(normed_two_low, expand_matrix, preferred_element_type=f32)
    hidden, hidden_back = jax.vjp(silu_product, gate_up)
    hidden_low = hidden.astype(jnp.bfloat16)
    result = (mid + jnp.dot(hidden_low, shrink_matrix, preferred_element_type=f32)).astype(
        jnp.bfloat16
    )
    grad_down = jnp.einsum("tf,td->fd", hidden_low, cotangent, preferred_element_type=f32)
    d_hidden = jnp.einsum("td,fd->tf", cotangent, shrink_matrix, preferred_element_type=f32)
    d_gate_up = hidden_back(d_hidden)[0].astype(jnp.bfloat16)
    grad_expand = jnp.einsum("td,tf->df", normed_two_low, d_gate_up, preferred_element_type=f32)
    d_normed_two = jnp.einsum("tf,df->td", d_gate_up, expand_matrix, preferred_element_type=f32)
    d_mid_part, grad_gain_two = norm_two_back(d_normed_two)
    d_mid = cotangent.astype(f32) + d_mid_part
    d_branch = d_mid.astype(jnp.bfloat16)
    grad_mixing_out = jnp.einsum("tq,td->qd", attended_low, d_branch, preferred_element_type=f32)
    d_attended = jnp.einsum("td,qd->tq", d_branch, mixing_out, preferred_element_type=f32).astype(
        jnp.bfloat16
    )
    def by_owner(grad):
        return grad.astype(jnp.bfloat16).reshape(sizes + (-1,))

    if whole_rows(w_down.shape[0], D):
        down_sent = grad_down.astype(jnp.bfloat16).reshape(sizes + (-1, D))
    else:
        down_sent = pack(by_owner(grad_down), sizes)
    (gu_mine, down_mine, out_mine), d_projected = scatter_attend(
        [pack(by_owner(grad_expand), sizes), down_sent, pack(by_owner(grad_mixing_out), sizes)],
        [query, d_attended, pairs, start_rows, lse, attended_t, jnp.cos(turns), jnp.sin(turns)],
        sizes,
        2,
    )
    grad_mixing_in = jnp.einsum("td,tq->dq", normed_low, d_projected, preferred_element_type=f32)
    d_normed = jnp.einsum("tq,dq->td", d_projected, mixing_in, preferred_element_type=f32)
    d_input_part, grad_gain_one = norm_back(d_normed)
    gains = jnp.stack([grad_gain_one, grad_gain_two])
    qkv_mine, gains_sum = reduce_scatter(
        [pack(by_owner(grad_mixing_in), sizes)], gains, sizes, 3
    )
    return (
        result,
        d_mid + d_input_part,
        unpack(qkv_mine, (), w_qkv.shape[0]),
        unpack(out_mine, (), w_out.shape[0]),
        unpack(gu_mine, (), w_gu.shape[0]),
        unpack(down_mine, (), w_down.shape[0], D),
        gains_sum,
    )


def solution(mesh):
    spread = P(("seq", "dp"))
    rows = P(("seq", "dp"), None)
    return jax.shard_map(
        functools.partial(per_device, grid_sizes(mesh.shape["seq"], mesh.shape["dp"])),
        mesh=mesh,
        in_specs=(rows, spread, spread, spread, spread, P(), P("dp", None), rows),
        out_specs=(rows, rows, spread, spread, spread, spread, P()),
        check_vma=False,
    )
```
